128 devices in a mesh: bulk: 8 (over x, core), group: 16 (over z, y).
Axes of the slice: x: 4, y: 4, z: 4, core: 2. Of those that a mesh axis runs over, the one named last changes fastest.
Arguments:
- points: float32 [8, 786432], P(None, ('bulk', 'group')), may hold values from -6 to 6
- weights: float32 [64, 786432], P(None, ('bulk', 'group')), may hold values from -0.75 to 0.75
- leaf_order: int32 [786432], P(('bulk', 'group')), may hold values from 0 to 786431, as said below
- basis: float32 [3072, 256, 128], P(('bulk', 'group')), may hold values from -0.375 to 0.375
- transfer: float32 [3072, 128, 128], P(('bulk', 'group')), may hold values from -0.1875 to 0.1875
- skel_leaf: bfloat16 [3072, 8, 128], P(('bulk', 'group')), may hold values from -6 to 6
- skel_upper: bfloat16 [384, 8, 128], P(('bulk', 'group')), may hold values from -6 to 6
- near_list: int32 [3072, 12], P(('bulk', 'group')), may hold values from 0 to 3071, as said below
- leaf_interaction_list: int32 [3072, 32], P(('bulk', 'group')), may hold values from 0 to 3071, as said below
- far_upper: int32 [384, 32], P(('bulk', 'group')), may hold values from 0 to 383
Outputs:
- potential: float32 [64, 786432], P(None, ('bulk', 'group'))
The draws below stay inside these ranges and needn't reach their ends.
Inputs may be any that keep to these rules, and one draw needn't show every extreme that they name: `leaf_order`: A permutation of the point indices. The 6144 positions of each device take exactly 384 points from the input shard of every device of the same group. `near_list`: entry 0 of each row is the leaf itself; every entry is within 24 leaves of the row's leaf. `leaf_interaction_list`: every entry lies in the same aligned block of 384 leaves as the row's leaf.
All inputs are finite; a program needn't handle non-finite values.
Results may differ from the reference program's by a relative error of at most 0.0041.
Values may be sent and summed in bfloat16 or wider, within the bound.
No kernel may reach another device: no remote copies, remote signals or barrier semaphores. Data moves between devices by JAX's collectives and lax.ppermute only.
A program may use at most 128 MiB of HBM per device.

```python
import math
import jax
import jax.numpy as jnp
import numpy as np
from jax import lax

D = 8
COLS = 64
LEAF = 256
RANK = 128
NEAR = 12
FAR0 = 32
FAR1 = 32
KIDS = 8
LEAF_DEV = 24
ROWS_DEV = 6144
PAIR = 384
NPTS = 786432
NLEAF = 3072
SUB_LEAVES = 384
NC1 = 384


def shuffled(key_row, length):
    return jax.random.permutation(key_row, length).astype(jnp.int32)


def draw_leaf_order(key, part):
    key = jax.random.fold_in(key, 11)
    devices = NPTS // ROWS_DEV
    groups = ROWS_DEV // PAIR
    bulks = devices // groups
    first_keys = jax.random.split(jax.random.fold_in(key, 1), devices)
    second_keys = jax.random.split(jax.random.fold_in(key, 2), devices)
    row_perm = jax.vmap(partial_rows)(first_keys)
    offset = jnp.arange(devices, dtype=jnp.int32)[:, None] * ROWS_DEV
    sources = (row_perm + offset).reshape(bulks, groups, groups, PAIR)
    by_target = jnp.transpose(sources, (0, 2, 1, 3)).reshape(devices, ROWS_DEV)
    mixing = jax.vmap(partial_rows)(second_keys)
    mixed = jnp.take_along_axis(by_target, mixing, axis=1)
    return mixed.reshape(NPTS)


def partial_rows(key_row):
    return shuffled(key_row, ROWS_DEV)


def draw_near_list(key, part):
    key = jax.random.fold_in(key, 23)
    own_leaf = jnp.arange(NLEAF, dtype=jnp.int32)[:, None]
    shifts = jax.random.randint(key, (NLEAF, NEAR - 1), -LEAF_DEV, LEAF_DEV + 1, dtype=jnp.int32)
    others = jnp.clip(own_leaf + shifts, 0, NLEAF - 1)
    return jnp.concatenate([own_leaf, others], axis=1)


def draw_leaf_interaction_list(key, part):
    key = jax.random.fold_in(key, 37)
    own_leaf = jnp.arange(NLEAF, dtype=jnp.int32)[:, None]
    subtree = own_leaf // SUB_LEAVES * SUB_LEAVES
    return subtree + jax.random.randint(key, (NLEAF, FAR0), 0, SUB_LEAVES, dtype=jnp.int32)


def touch_ends(values, key, low, largest):
    longest = values.shape.index(max(values.shape))
    spots = []
    for shift in (0, 1):
        where = [jax.random.randint(jax.random.fold_in(key, axis), (), 0, length) for axis, length in enumerate(values.shape)]
        where[longest] = (where[longest] + shift) % values.shape[longest]
        spots.append(tuple(where))
    return values.at[spots[0]].set(low).at[spots[1]].set(largest)


def steps_of(stream_key, extent, pieces, smallest, high):
    level, own = 1.0, jax.random.fold_in(stream_key, 6)
    for position, blocks in pieces:
        heights = jnp.exp(jax.random.uniform(jax.random.fold_in(own, position), (blocks,), jnp.float32, smallest / len(pieces), high / len(pieces)))
        level = level * jnp.repeat(heights, extent[position] // blocks).reshape([-1 if axis == position else 1 for axis in range(len(extent))])
    return level


def cumulative_ranks(number_of, slope):
    portions = [(1 << 20) // math.isqrt(standing ** slope) + 1 for standing in range(1, number_of + 1)]
    spread = 1 + sum(portions) // (1 << 30)
    return np.cumsum(np.array([max(1, weight // spread) for weight in portions]))


def ranked(key, dims, count, slope):
    listing = cumulative_ranks(count, slope)
    lot = jax.random.randint(jax.random.fold_in(key, 1), dims, 0, int(listing[count - 1]))
    grade = jnp.searchsorted(jnp.asarray(listing, jnp.int32), lot, side="right")
    return jax.random.permutation(jax.random.fold_in(key, 2), count)[grade].astype(jnp.int32)


def normal_values(rng, extent, width, reach, cuts=(), held_as=jnp.bfloat16):
    array = width * jax.random.normal(rng, extent, jnp.float32)
    if cuts:
        array = array * steps_of(rng, extent, cuts, -0.22, 0.18)
    return jnp.clip(array, -reach, reach).astype(held_as)


def setup_inputs(seed: int = 0) -> dict:
    key_of = jax.random.split(jax.random.key(seed), 11)
    points = normal_values(key_of[0], (D, NPTS), 1.0, 6.0, ((1, 128),), jnp.float32)
    weights = normal_values(key_of[1], (COLS, NPTS), 0.125, 0.75, ((1, 128),), jnp.float32)
    leaf_order = draw_leaf_order(jax.random.fold_in(key_of[10], 71), 0)
    basis = normal_values(key_of[3], (NLEAF, LEAF, RANK), LEAF ** -0.5, 0.375, ((0, 128),), jnp.float32)
    transfer = normal_values(key_of[4], (NLEAF, RANK, RANK), (RANK * KIDS) ** -0.5, 0.1875, ((0, 128),), jnp.float32)
    skel_leaf = normal_values(key_of[5], (NLEAF, D, RANK), 1.0, 6.0, ((0, 128),))
    skel_upper = normal_values(key_of[6], (NC1, D, RANK), 1.0, 6.0, ((0, 128),))
    near_list = draw_near_list(jax.random.fold_in(key_of[10], 71), 0)
    leaf_interaction_list = draw_leaf_interaction_list(jax.random.fold_in(key_of[10], 71), 0)
    far_upper = touch_ends(ranked(key_of[9], (NC1, FAR1), NC1, 2), jax.random.fold_in(key_of[9], 3), 0, NC1 - 1).astype(jnp.int32)
    return dict(points=points, weights=weights, leaf_order=leaf_order, basis=basis, transfer=transfer, skel_leaf=skel_leaf, skel_upper=skel_upper, near_list=near_list, leaf_interaction_list=leaf_interaction_list, far_upper=far_upper)


matern_scale = 1.118033988749895
highest_precision = lax.Precision.HIGHEST

def matern(targets, sources):
    target_sq = lax.optimization_barrier(jnp.sum(targets * targets, axis=-2))[..., :, None]
    source_sq = lax.optimization_barrier(jnp.sum(sources * sources, axis=-2))[..., None, :]
    inner = jnp.einsum('...dm,...dn->...mn', targets, sources, precision=highest_precision)
    radius = jnp.sqrt(jnp.maximum(target_sq + source_sq - 2.0 * inner, 0.0)) * matern_scale
    return ((1.0 + radius + radius * radius / 3.0) * jnp.exp(-radius)).astype(jnp.bfloat16)

def couple(target_pts, source_pts, source_vals):
    tiled_pts = jnp.broadcast_to(target_pts[:, None], source_pts.shape[:2] + target_pts.shape[1:])
    kernel = matern(tiled_pts, source_pts)
    return jnp.einsum('nfck,nfmk->ncm', source_vals.astype(jnp.float32), kernel.astype(jnp.float32))

def reference(points, weights, leaf_order, basis, transfer, skel_leaf, skel_upper, near_list, leaf_interaction_list, far_upper):
    ordered_pts = jnp.take(points, leaf_order, axis=1)
    ordered_wts = jnp.take(weights, leaf_order, axis=1)
    leaf_pts = ordered_pts.reshape(D, NLEAF, LEAF).transpose(1, 0, 2)
    leaf_weight_values = ordered_wts.reshape(COLS, NLEAF, LEAF).transpose(1, 0, 2)
    skeleton_weight = jnp.einsum('njx,nxq->njq', leaf_weight_values, basis, precision=highest_precision)
    skel_wb = skeleton_weight.astype(jnp.bfloat16)
    upper_w = jnp.einsum('pkcr,pkrs->pcs', skeleton_weight.reshape(NC1, KIDS, COLS, RANK), transfer.reshape(NC1, KIDS, RANK, RANK), precision=highest_precision)
    upper_wb = upper_w.astype(jnp.bfloat16)
    upper_pts = skel_upper.astype(jnp.float32)
    leaf_skel = skel_leaf.astype(jnp.float32)
    leaf_wb = leaf_weight_values.astype(jnp.bfloat16)

    def upper_block(cluster_ids):
        source_ids = far_upper[cluster_ids]
        return couple(upper_pts[cluster_ids], upper_pts[source_ids], upper_wb[source_ids])
    upper_size = 8 if NC1 % 8 == 0 else 1
    upper_transposed = lax.map(upper_block, jnp.arange(NC1, dtype=jnp.int32).reshape(-1, upper_size)).reshape(NC1, COLS, RANK)

    def leaf_block(leaf_index_list):
        distant_index_list = leaf_interaction_list[leaf_index_list]
        near_ids = near_list[leaf_index_list]
        far_part = couple(leaf_skel[leaf_index_list], leaf_skel[distant_index_list], skel_wb[distant_index_list])
        downward = jnp.einsum('ncs,nrs->ncr', upper_transposed[leaf_index_list // KIDS], transfer[leaf_index_list], precision=highest_precision)
        result = jnp.einsum('ncr,nar->nca', far_part + downward, basis[leaf_index_list], precision=highest_precision)
        near_part = couple(leaf_pts[leaf_index_list], leaf_pts[near_ids], leaf_wb[near_ids])
        return result + near_part
    block_size = 8 if NLEAF % 8 == 0 else 1
    potential = lax.map(leaf_block, jnp.arange(NLEAF, dtype=jnp.int32).reshape(-1, block_size))
    return potential.reshape(NLEAF, COLS, LEAF).transpose(1, 0, 2).reshape(COLS, NPTS)
```

```python
import functools
import math

import jax
import jax.numpy as jnp
from jax import lax
from jax.experimental import pallas as pl
from jax.experimental.pallas import tpu as pltpu
from jax.sharding import PartitionSpec as P

KIDS = 8

POINT_SCALE = math.sqrt(5.0) / 2.0 / math.log(2.0)
POLY_A = 3.0 / math.log(2.0)
POLY_B = 3.0 / math.log(2.0) ** 2
POLY_LOG = math.log2(math.log(2.0) ** 2 / 3.0)
AUG = 48
VMEM_LIMIT = 56 * 1024 * 1024

f32 = jnp.float32
bf16 = jnp.bfloat16
NN = (((1,), (0,)), ((), ()))
NT = (((1,), (1,)), ((), ()))


def mm(a, b, dims=NN):
    return lax.dot_general(a, b, dims, preferred_element_type=f32)


def halves(x):
    high = x.astype(bf16)
    return high, (x - high.astype(f32)).astype(bf16)


def mm3(a, b):
    a_high, a_low = halves(a)
    b_high, b_low = halves(b)
    return mm(a_high, b_high) + (mm(a_high, b_low) + mm(a_low, b_high))


def squares(high, low):
    x = high + low
    norm = jnp.sum(x * x, axis=0, keepdims=True)
    first = norm.astype(bf16).astype(f32)
    second = (norm - first).astype(bf16).astype(f32)
    third = norm - first - second
    row = lax.broadcasted_iota(jnp.int32, high.shape, 0)
    parts = jnp.where(row % 3 == 0, first, jnp.where(row % 3 == 1, second, third))
    return row, parts


def source_rows(high, low):
    row, parts = squares(high, low)
    last = jnp.where(row < 3, 1.0, jnp.where(row < 6, parts, 0.0))
    high, low = -2.0 * high, -2.0 * low
    return jnp.concatenate([high, low, high, low, last, jnp.zeros_like(last)], axis=0).astype(bf16)


def target_rows(high, low):
    row, parts = squares(high, low)
    last = jnp.where(row < 3, parts, jnp.where(row < 6, 1.0, 0.0))
    rows = jnp.concatenate([high, high, low, low, last, jnp.zeros_like(last)], axis=0)
    return jnp.transpose(rows).astype(bf16)


def f32_halves(points):
    high, low = halves(points)
    return high.astype(f32), low.astype(f32)


def scaled_halves(points):
    return f32_halves(points.astype(f32) * POINT_SCALE)


def matern(square):
    square = jnp.maximum(square, 1e-30)
    t = square * lax.rsqrt(square)
    return (((t + POLY_A) * t + POLY_B) * jnp.exp2(POLY_LOG - t)).astype(bf16)


def index_body(src_ref, row_ref, want_ref, rank_ref):
    group_count, pair = want_ref.shape
    lines = src_ref.shape[0]
    src = src_ref[...]
    row = row_ref[...]
    before = (
        lax.broadcasted_iota(jnp.int32, (128, 128), 0)
        < lax.broadcasted_iota(jnp.int32, (128, 128), 1)
    ).astype(f32).astype(bf16)
    above = (
        lax.broadcasted_iota(jnp.int32, (lines, lines), 1)
        < lax.broadcasted_iota(jnp.int32, (lines, lines), 0)
    ).astype(f32).astype(bf16)
    all_ones = jnp.ones((128, 128), bf16)
    rank = jnp.zeros(src.shape, f32)
    for g in range(group_count):
        here = src == g
        mask = here.astype(f32).astype(bf16)
        total = mm(mask, all_ones).astype(bf16)
        rank = jnp.where(here, mm(mask, before) + mm(above, total), rank)
    rank = rank.astype(jnp.int32)
    rank_ref[...] = rank
    place = lax.broadcasted_iota(jnp.int32, (pair, 256), 0)
    owner = lax.broadcasted_iota(jnp.int32, (group_count, 256), 0)
    total = jnp.zeros((2 * group_count, pair), f32)
    for k in range(0, lines, 2):
        line = lambda x: jnp.concatenate([x[k : k + 1], x[k + 1 : k + 2]], axis=1)
        rank_line, src_line, row_line = line(rank), line(src), line(row)
        spots = (place == rank_line).astype(f32).astype(bf16)
        mine = owner == src_line
        high = jnp.where(mine, (row_line >> 7).astype(f32), 0.0)
        low = jnp.where(mine, (row_line & 127).astype(f32), 0.0)
        total += mm(jnp.concatenate([high, low], axis=0).astype(bf16), spots, NT)
    want_ref[...] = (total[:group_count] * 128.0 + total[group_count:]).astype(jnp.int32)


def index_lists(src, row, group_count, pair):
    lines = src.shape[0]
    return pl.pallas_call(
        index_body,
        out_shape=(
            jax.ShapeDtypeStruct((group_count, pair), jnp.int32),
            jax.ShapeDtypeStruct((lines, 128), jnp.int32),
        ),
        compiler_params=pltpu.CompilerParams(vmem_limit_bytes=VMEM_LIMIT),
        cost_estimate=pl.CostEstimate(flops=2 * 10**9, bytes_accessed=10**5, transcendentals=0),
        name="index_lists",
    )(src, row)


def pick_body(want_ref, points_ref, weights_ref, out_ref, table):
    row_count = points_ref.shape[1]
    high_count = row_count // 256
    group_count, height, pair = out_ref.shape
    for h in range(high_count):
        at = slice(h * 256, (h + 1) * 256)
        high, low = scaled_halves(points_ref[:, at])
        table[h * height : (h + 1) * height, :] = jnp.concatenate(
            [weights_ref[:, at], high, low], axis=0
        ).astype(bf16)
    batch = 4

    def device(d, carry):
        want = want_ref[d]
        low = want & 255
        high = want >> 8
        spots = (lax.broadcasted_iota(jnp.int32, (256, pair), 0) == low).astype(f32).astype(bf16)
        picked = jnp.zeros((height, pair), f32)
        for h in range(0, high_count, batch):
            found = mm(table[h * height : (h + batch) * height, :], spots)
            for k in range(batch):
                picked = jnp.where(high == h + k, found[k * height : (k + 1) * height], picked)
        out_ref[d] = picked.astype(bf16)
        return carry

    lax.fori_loop(0, group_count, device, 0)


def pick(want, points, weights):
    group_count, pair = want.shape
    row_count = points.shape[1]
    height = weights.shape[0] + 2 * points.shape[0]
    whole = pl.BlockSpec(memory_space=pltpu.VMEM)
    return pl.pallas_call(
        pick_body,
        in_specs=[whole, whole, whole],
        out_specs=whole,
        out_shape=jax.ShapeDtypeStruct((group_count, height, pair), bf16),
        scratch_shapes=[pltpu.VMEM((row_count // 256 * height, 256), bf16)],
        compiler_params=pltpu.CompilerParams(vmem_limit_bytes=VMEM_LIMIT),
        cost_estimate=pl.CostEstimate(flops=6 * 10**9, bytes_accessed=3 * 10**6, transcendentals=0),
        name="pick",
    )(want.reshape(group_count, 1, pair), points, weights)


def place_body(src_ref, rank_ref, arrived_ref, basis_ref, transfer_ref, leaf_ref, skel_ref, upper_ref):
    leaf_count, height, leaf_size = leaf_ref.shape
    pair = arrived_ref.shape[1]
    group_count = arrived_ref.shape[0] // height
    cols = skel_ref.shape[1]
    batch = 4

    def cluster(c, carry):
        total = jnp.zeros(upper_ref.shape[1:], f32)
        for n in range(KIDS):
            i = c * KIDS + n
            src = src_ref[i]
            spots = (
                lax.broadcasted_iota(jnp.int32, (pair, leaf_size), 0) == rank_ref[i]
            ).astype(f32).astype(bf16)
            placed = jnp.zeros((height, leaf_size), f32)
            for g in range(0, group_count, batch):
                found = mm(arrived_ref[g * height : (g + batch) * height, :], spots)
                for k in range(batch):
                    placed = jnp.where(src == g + k, found[k * height : (k + 1) * height], placed)
            placed = placed.astype(bf16)
            leaf_ref[i] = placed
            basis_high, basis_low = halves(basis_ref[i])
            skel = mm(placed[:cols], basis_high) + mm(placed[:cols], basis_low)
            skel_ref[i] = skel.astype(bf16)
            total += mm3(skel, transfer_ref[i])
        upper_ref[c] = total.astype(bf16)
        return carry

    lax.fori_loop(0, leaf_count // KIDS, cluster, 0)


def place(src, rank, arrived, basis, transfer):
    leaf_count, leaf_size, rank_size = basis.shape
    group_count, height, pair = arrived.shape
    cols = height - 16
    whole = pl.BlockSpec(memory_space=pltpu.VMEM)
    return pl.pallas_call(
        place_body,
        in_specs=[whole] * 5,
        out_specs=(whole, whole, whole),
        out_shape=(
            jax.ShapeDtypeStruct((leaf_count, height, leaf_size), bf16),
            jax.ShapeDtypeStruct((leaf_count, cols, rank_size), bf16),
            jax.ShapeDtypeStruct((leaf_count // KIDS, cols, rank_size), bf16),
        ),
        compiler_params=pltpu.CompilerParams(vmem_limit_bytes=VMEM_LIMIT),
        cost_estimate=pl.CostEstimate(flops=8 * 10**9, bytes_accessed=9 * 10**6, transcendentals=0),
        name="place",
    )(
        src.reshape(leaf_count, 1, leaf_size),
        rank.reshape(leaf_count, 1, leaf_size),
        arrived.reshape(group_count * height, pair),
        basis,
        transfer,
    )


def near_body(list_ref, low_ref, own_ref, high_ref, out_ref, rows, values):
    leaf_count, height, leaf_size = own_ref.shape
    cols = height - 16
    for part, ref in enumerate((low_ref, own_ref, high_ref)):

        def fill(n, carry, part=part, ref=ref):
            values[part * leaf_count + n] = ref[n, :cols]
            tail = ref[n, cols:].astype(f32)
            rows[part * leaf_count + n] = source_rows(tail[:8], tail[8:])
            return carry

        lax.fori_loop(0, leaf_count, fill, 0)

    def leaf(i, carry):
        tail = own_ref[i, cols:].astype(f32)
        target = target_rows(tail[:8], tail[8:])
        total = jnp.zeros((leaf_size, cols), f32)
        for q in range(list_ref.shape[1]):
            j = list_ref[i, q]
            total += mm(matern(mm(target, rows[j])), values[j], NT)
        out_ref[i] = total
        return carry

    lax.fori_loop(0, leaf_count, leaf, 0)


def near_sums(lists, low, own, high):
    leaf_count, near = lists.shape
    height, leaf_size = own.shape[1:]
    cols = height - 16
    whole = pl.BlockSpec(memory_space=pltpu.VMEM)
    pairs = leaf_count * near * leaf_size * leaf_size
    return pl.pallas_call(
        near_body,
        in_specs=[pl.BlockSpec(memory_space=pltpu.SMEM), whole, whole, whole],
        out_specs=whole,
        out_shape=jax.ShapeDtypeStruct((leaf_count, leaf_size, cols), f32),
        scratch_shapes=[
            pltpu.VMEM((3 * leaf_count, AUG, leaf_size), bf16),
            pltpu.VMEM((3 * leaf_count, cols, leaf_size), bf16),
        ],
        compiler_params=pltpu.CompilerParams(vmem_limit_bytes=VMEM_LIMIT),
        cost_estimate=pl.CostEstimate(
            flops=pairs * 230, bytes_accessed=6 * 10**6, transcendentals=2 * pairs
        ),
        name="near_sums",
    )(lists, low, own, high)


def far_rows_body(points_ref, rows_ref):
    step = 8

    def fill(n, carry):
        for k in range(step):
            rows_ref[n * step + k] = source_rows(*f32_halves(points_ref[n * step + k]))
        return carry

    lax.fori_loop(0, points_ref.shape[0] // step, fill, 0)


def far_rows(points):
    count, _, rank_size = points.shape
    whole = pl.BlockSpec(memory_space=pltpu.VMEM)
    return pl.pallas_call(
        far_rows_body,
        in_specs=[whole],
        out_specs=whole,
        out_shape=jax.ShapeDtypeStruct((count, AUG, rank_size), bf16),
        compiler_params=pltpu.CompilerParams(vmem_limit_bytes=VMEM_LIMIT),
        cost_estimate=pl.CostEstimate(flops=10**8, bytes_accessed=6 * 10**6, transcendentals=0),
        name="far_rows",
    )(points)


def far_body(first, list_ref, target_ref, rows_ref, weights_ref, out_ref, even, odd):
    count = out_ref.shape[0]
    rank_size = weights_ref.shape[2]
    far = list_ref.shape[1]
    batch = 4

    def listed(ref, i, q, n):
        return jnp.concatenate([ref[list_ref[i, q + k]] for k in range(n)], axis=1)

    def fill(n, kernel):
        i = first + n
        target = target_rows(*f32_halves(target_ref[i]))
        for q in range(0, far, batch):
            kernel[:, q * rank_size : (q + batch) * rank_size] = matern(
                mm(target, listed(rows_ref, i, q, batch))
            )

    def apply(n, kernel):
        out_ref[n] = mm(kernel[...], listed(weights_ref, first + n, 0, far), NT)

    fill(0, even)

    def two(n, carry):
        fill(2 * n + 1, odd)
        apply(2 * n, even)
        fill(jnp.minimum(2 * n + 2, count - 1), even)
        apply(2 * n + 1, odd)
        return carry

    lax.fori_loop(0, count // 2, two, 0)


def far_sums(first, count, lists, targets, rows, weights):
    far = lists.shape[1]
    cols, rank_size = weights.shape[1:]
    whole = pl.BlockSpec(memory_space=pltpu.VMEM)
    pairs = count * far * rank_size * rank_size
    return pl.pallas_call(
        functools.partial(far_body, first),
        in_specs=[pl.BlockSpec(memory_space=pltpu.SMEM), whole, whole, whole],
        out_specs=whole,
        out_shape=jax.ShapeDtypeStruct((count, rank_size, cols), f32),
        scratch_shapes=[pltpu.VMEM((rank_size, far * rank_size), bf16)] * 2,
        compiler_params=pltpu.CompilerParams(vmem_limit_bytes=VMEM_LIMIT),
        cost_estimate=pl.CostEstimate(
            flops=pairs * 230, bytes_accessed=12 * 10**6, transcendentals=2 * pairs
        ),
        name="far_sums",
    )(lists, targets, rows, weights)


def upper_body(list_ref, own_ref, chip_ref, across_ref, out_ref, every_ref):
    dims, rank_size = own_ref.shape[1:]
    cols = out_ref.shape[2]
    batch = 4
    half = chip_ref.shape[0]

    def fetch(k, carry):
        far = list_ref.shape[1]
        place = list_ref[k // far, k % far]

        @pl.when(place < half)
        def _():
            every_ref[k] = chip_ref[jnp.minimum(place, half - 1)]

        @pl.when(place >= half)
        def _():
            every_ref[k] = across_ref[jnp.maximum(place - half, 0)]

        return carry

    lax.fori_loop(0, every_ref.shape[0], fetch, 0)
    for c in range(own_ref.shape[0]):
        target = target_rows(*scaled_halves(own_ref[c]))
        total = jnp.zeros((rank_size, cols), f32)
        for q in range(0, list_ref.shape[1], batch):
            blocks = [every_ref[c * list_ref.shape[1] + q + k] for k in range(batch)]
            values = jnp.concatenate([x[:cols] for x in blocks], axis=1)
            points = jnp.concatenate([x[cols:].astype(f32)[:dims] for x in blocks], axis=1)
            kernel = matern(mm(target, source_rows(*scaled_halves(points))))
            total += mm(kernel, values, NT)
        out_ref[c] = total


def upper_sums(lists, own, chip, across):
    count, dims, rank_size = own.shape
    cols = chip.shape[1] - 2 * dims
    whole = pl.BlockSpec(memory_space=pltpu.VMEM)
    pairs = count * lists.shape[1] * rank_size * rank_size
    return pl.pallas_call(
        upper_body,
        in_specs=[pl.BlockSpec(memory_space=pltpu.SMEM), whole, whole, whole],
        out_specs=whole,
        out_shape=jax.ShapeDtypeStruct((count, rank_size, cols), f32),
        scratch_shapes=[pltpu.VMEM((count * lists.shape[1],) + chip.shape[1:], bf16)],
        compiler_params=pltpu.CompilerParams(vmem_limit_bytes=VMEM_LIMIT),
        cost_estimate=pl.CostEstimate(
            flops=pairs * 230, bytes_accessed=8 * 10**6, transcendentals=2 * pairs
        ),
        name="upper_sums",
    )(lists, own, chip, across)


def final_body(first_ref, second_ref, upper_ref, transfer_ref, basis_ref, near_ref, out_ref):
    leaf_size = basis_ref.shape[1]
    step = 4
    for part, far_ref in enumerate((first_ref, second_ref)):
        count = far_ref.shape[0]

        def leaves(n, carry, far_ref=far_ref, start=part * count):
            upper = upper_ref[(start + n * step) // KIDS]
            for k in range(step):
                i = start + n * step + k
                skeleton = far_ref[n * step + k] + mm3(transfer_ref[i], upper)
                potential = mm3(basis_ref[i], skeleton) + near_ref[i]
                at = pl.ds(pl.multiple_of(i * leaf_size, leaf_size), leaf_size)
                out_ref[:, at] = jnp.transpose(potential)
            return carry

        lax.fori_loop(0, count // step, leaves, 0)


def final(first, second, upper, transfer, basis, near):
    leaf_count, leaf_size, rank_size = basis.shape
    cols = near.shape[2]
    whole = pl.BlockSpec(memory_space=pltpu.VMEM)
    return pl.pallas_call(
        final_body,
        in_specs=[whole] * 6,
        out_specs=whole,
        out_shape=jax.ShapeDtypeStruct((cols, leaf_count * leaf_size), f32),
        compiler_params=pltpu.CompilerParams(vmem_limit_bytes=VMEM_LIMIT),
        cost_estimate=pl.CostEstimate(flops=10**9, bytes_accessed=10**7, transcendentals=0),
        name="final",
    )(first, second, upper, transfer, basis, near)


def shifted(block, axis, move, count):
    return lax.ppermute(block, axis, [(i, move(i)) for i in range(count)])


def group_upper(block):
    for bit in (1, 2, 4, 8):
        block = jnp.concatenate([block, shifted(block, "group", lambda i, bit=bit: i ^ bit, 16)], axis=0)
    return block


def after(x):
    return jnp.where(jnp.isnan(x[(0,) * x.ndim]), 1, 0)


def upper_places(clusters, count):
    owner = clusters // count
    group = (owner % 16) ^ lax.axis_index("group")
    bulk = owner // 16
    mine = lax.axis_index("bulk")
    core = (bulk ^ mine) & 1
    hops = (bulk // 2 - mine // 2) & 3
    turn = hops
    return (((core * 4 + turn) * 16) + group) * count + clusters % count


def local(
    points,
    weights,
    leaf_order,
    basis,
    transfer,
    skel_leaf,
    skel_upper,
    near_list,
    leaf_interaction_list,
    far_upper,
):
    row_count = leaf_order.shape[0]
    group_count = lax.axis_size("group")
    device_count = group_count * lax.axis_size("bulk")
    pair = row_count // group_count
    leaf_count = basis.shape[0]

    src = (leaf_order // row_count % group_count).reshape(-1, 128)
    row = (leaf_order % row_count).reshape(-1, 128)
    scaled = skel_leaf.astype(f32) * POINT_SCALE
    subtree_points = lax.all_gather(scaled, "group", axis=0, tiled=True)
    want, rank = index_lists(src, row, group_count, pair)
    wanted = lax.all_to_all(want, "group", split_axis=0, concat_axis=0, tiled=True)
    picked = pick(wanted, points, weights)
    arrived = lax.all_to_all(picked, "group", split_axis=0, concat_axis=0, tiled=True)

    far_local = leaf_interaction_list - lax.axis_index("bulk") * (group_count * leaf_count)
    source_points = far_rows(subtree_points)

    own, skel_wb, upper_wb = place(src, rank, arrived, basis, transfer)
    sub_w = lax.all_gather(skel_wb, "group", axis=0, tiled=True)
    forward = [(i, i + 1) for i in range(device_count - 1)]
    backward = [(i + 1, i) for i in range(device_count - 1)]
    low = lax.ppermute(own, ("bulk", "group"), forward)
    high = lax.ppermute(own, ("bulk", "group"), backward)

    blank = jnp.zeros(skel_upper.shape, bf16)
    block = group_upper(jnp.concatenate([upper_wb, skel_upper, blank], axis=1))
    ring = [shifted(block, "bulk", lambda i, hops=hops: (i - 2 * hops) % 8, 8) for hops in (1, 2, 3)]
    device = lax.axis_index(("bulk", "group"))
    near_local = near_list - (device - 1) * leaf_count
    near = near_sums(near_local + after(block), low, own, high)
    part = leaf_count // 2
    far_local = far_local + after(near)
    first = far_sums(0, part, far_local, scaled, source_points, sub_w)
    chip = jnp.concatenate([block + after(first).astype(bf16)] + ring, axis=0)
    across = shifted(chip, "bulk", lambda i: i ^ 1, 8)
    second = far_sums(part, part, far_local + after(first), scaled, source_points, sub_w)
    upper = upper_sums(upper_places(far_upper, skel_upper.shape[0]), skel_upper, chip, across)
    return final(first, second, upper, transfer, basis, near)


def solution(mesh):
    placed = (
        P(None, ("bulk", "group")),
        P(None, ("bulk", "group")),
        P(("bulk", "group")),
        P(("bulk", "group"), None, None),
        P(("bulk", "group"), None, None),
        P(("bulk", "group"), None, None),
        P(("bulk", "group"), None, None),
        P(("bulk", "group"), None),
        P(("bulk", "group"), None),
        P(("bulk", "group"), None),
    )
    return jax.shard_map(
        local, mesh=mesh, in_specs=placed, out_specs=P(None, ("bulk", "group")), check_vma=False
    )
```

```python
import functools
import math

import jax
import jax.numpy as jnp
from jax import lax
from jax.experimental import pallas as pl
from jax.experimental.pallas import tpu as pltpu
from jax.sharding import PartitionSpec as P

KIDS = 8

POINT_SCALE = math.sqrt(5.0) / 2.0 / math.log(2.0)
POLY_A = 3.0 / math.log(2.0)
POLY_B = 3.0 / math.log(2.0) ** 2
POLY_LOG = math.log2(math.log(2.0) ** 2 / 3.0)
AUG = 48
VMEM_LIMIT = 56 * 1024 * 1024

f32 = jnp.float32
bf16 = jnp.bfloat16
TICK = jax.ShapeDtypeStruct((8, 128), f32)
NN = (((1,), (0,)), ((), ()))
NT = (((1,), (1,)), ((), ()))


def mm(a, b, dims=NN):
    return lax.dot_general(a, b, dims, preferred_element_type=f32)


def halves(x):
    high = x.astype(bf16)
    return high, (x - high.astype(f32)).astype(bf16)


def mm3(a, b):
    a_high, a_low = halves(a)
    b_high, b_low = halves(b)
    return mm(a_high, b_high) + (mm(a_high, b_low) + mm(a_low, b_high))


def squares(high, low):
    x = high + low
    norm = jnp.sum(x * x, axis=0, keepdims=True)
    first = norm.astype(bf16).astype(f32)
    second = (norm - first).astype(bf16).astype(f32)
    third = norm - first - second
    row = lax.broadcasted_iota(jnp.int32, high.shape, 0)
    parts = jnp.where(row % 3 == 0, first, jnp.where(row % 3 == 1, second, third))
    return row, parts


def source_rows(high, low):
    row, parts = squares(high, low)
    last = jnp.where(row < 3, 1.0, jnp.where(row < 6, parts, 0.0))
    high, low = -2.0 * high, -2.0 * low
    return jnp.concatenate([high, low, high, low, last, jnp.zeros_like(last)], axis=0).astype(bf16)


def target_rows(high, low):
    row, parts = squares(high, low)
    last = jnp.where(row < 3, parts, jnp.where(row < 6, 1.0, 0.0))
    rows = jnp.concatenate([high, high, low, low, last, jnp.zeros_like(last)], axis=0)
    return jnp.transpose(rows).astype(bf16)


def f32_halves(points):
    high, low = halves(points)
    return high.astype(f32), low.astype(f32)


def scaled_halves(points):
    return f32_halves(points.astype(f32) * POINT_SCALE)


def matern(square):
    square = jnp.maximum(square, 1e-30)
    t = square * lax.rsqrt(square)
    return (((t + POLY_A) * t + POLY_B) * jnp.exp2(POLY_LOG - t)).astype(bf16)


def index_body(src_ref, row_ref, want_ref, rank_ref):
    group_count, pair = want_ref.shape
    lines = src_ref.shape[0]
    src = src_ref[...]
    row = row_ref[...]
    before = (
        lax.broadcasted_iota(jnp.int32, (128, 128), 0)
        < lax.broadcasted_iota(jnp.int32, (128, 128), 1)
    ).astype(f32).astype(bf16)
    above = (
        lax.broadcasted_iota(jnp.int32, (lines, lines), 1)
        < lax.broadcasted_iota(jnp.int32, (lines, lines), 0)
    ).astype(f32).astype(bf16)
    all_ones = jnp.ones((128, 128), bf16)
    rank = jnp.zeros(src.shape, f32)
    for g in range(group_count):
        here = src == g
        mask = here.astype(f32).astype(bf16)
        total = mm(mask, all_ones).astype(bf16)
        rank = jnp.where(here, mm(mask, before) + mm(above, total), rank)
    rank = rank.astype(jnp.int32)
    rank_ref[...] = rank
    place = lax.broadcasted_iota(jnp.int32, (pair, 256), 0)
    owner = lax.broadcasted_iota(jnp.int32, (group_count, 256), 0)
    total = jnp.zeros((2 * group_count, pair), f32)
    for k in range(0, lines, 2):
        line = lambda x: jnp.concatenate([x[k : k + 1], x[k + 1 : k + 2]], axis=1)
        rank_line, src_line, row_line = line(rank), line(src), line(row)
        spots = (place == rank_line).astype(f32).astype(bf16)
        mine = owner == src_line
        high = jnp.where(mine, (row_line >> 7).astype(f32), 0.0)
        low = jnp.where(mine, (row_line & 127).astype(f32), 0.0)
        total += mm(jnp.concatenate([high, low], axis=0).astype(bf16), spots, NT)
    want_ref[...] = (total[:group_count] * 128.0 + total[group_count:]).astype(jnp.int32)


def index_lists(src, row, group_count, pair):
    lines = src.shape[0]
    return pl.pallas_call(
        index_body,
        out_shape=(
            jax.ShapeDtypeStruct((group_count, pair), jnp.int32),
            jax.ShapeDtypeStruct((lines, 128), jnp.int32),
        ),
        compiler_params=pltpu.CompilerParams(vmem_limit_bytes=VMEM_LIMIT),
        cost_estimate=pl.CostEstimate(flops=2 * 10**9, bytes_accessed=10**5, transcendentals=0),
        name="index_lists",
    )(src, row)


def pick_body(want_ref, points_ref, weights_ref, out_ref, table):
    row_count = points_ref.shape[1]
    high_count = row_count // 256
    group_count, height, pair = out_ref.shape
    for h in range(high_count):
        at = slice(h * 256, (h + 1) * 256)
        high, low = scaled_halves(points_ref[:, at])
        table[h * height : (h + 1) * height, :] = jnp.concatenate(
            [weights_ref[:, at], high, low], axis=0
        ).astype(bf16)
    batch = 4

    def device(d, carry):
        want = want_ref[d]
        low = want & 255
        high = want >> 8
        spots = (lax.broadcasted_iota(jnp.int32, (256, pair), 0) == low).astype(f32).astype(bf16)
        picked = jnp.zeros((height, pair), f32)
        for h in range(0, high_count, batch):
            found = mm(table[h * height : (h + batch) * height, :], spots)
            for k in range(batch):
                picked = jnp.where(high == h + k, found[k * height : (k + 1) * height], picked)
        out_ref[d] = picked.astype(bf16)
        return carry

    lax.fori_loop(0, group_count, device, 0)


def pick(want, points, weights):
    group_count, pair = want.shape
    row_count = points.shape[1]
    height = weights.shape[0] + 2 * points.shape[0]
    whole = pl.BlockSpec(memory_space=pltpu.VMEM)
    return pl.pallas_call(
        pick_body,
        in_specs=[whole, whole, whole],
        out_specs=whole,
        out_shape=jax.ShapeDtypeStruct((group_count, height, pair), bf16),
        scratch_shapes=[pltpu.VMEM((row_count // 256 * height, 256), bf16)],
        compiler_params=pltpu.CompilerParams(vmem_limit_bytes=VMEM_LIMIT),
        cost_estimate=pl.CostEstimate(flops=6 * 10**9, bytes_accessed=3 * 10**6, transcendentals=0),
        name="pick",
    )(want.reshape(group_count, 1, pair), points, weights)


def place_body(src_ref, rank_ref, arrived_ref, basis_ref, transfer_ref, leaf_ref, skel_ref, upper_ref):
    leaf_count, height, leaf_size = leaf_ref.shape
    pair = arrived_ref.shape[1]
    group_count = arrived_ref.shape[0] // height
    cols = skel_ref.shape[1]
    batch = 4

    def cluster(c, carry):
        total = jnp.zeros(upper_ref.shape[1:], f32)
        for n in range(KIDS):
            i = c * KIDS + n
            src = src_ref[i]
            spots = (
                lax.broadcasted_iota(jnp.int32, (pair, leaf_size), 0) == rank_ref[i]
            ).astype(f32).astype(bf16)
            placed = jnp.zeros((height, leaf_size), f32)
            for g in range(0, group_count, batch):
                found = mm(arrived_ref[g * height : (g + batch) * height, :], spots)
                for k in range(batch):
                    placed = jnp.where(src == g + k, found[k * height : (k + 1) * height], placed)
            placed = placed.astype(bf16)
            leaf_ref[i] = placed
            basis_high, basis_low = halves(basis_ref[i])
            skel = mm(placed[:cols], basis_high) + mm(placed[:cols], basis_low)
            skel_ref[i] = skel.astype(bf16)
            total += mm3(skel, transfer_ref[i])
        upper_ref[c] = total.astype(bf16)
        return carry

    lax.fori_loop(0, leaf_count // KIDS, cluster, 0)


def place(src, rank, arrived, basis, transfer):
    leaf_count, leaf_size, rank_size = basis.shape
    group_count, height, pair = arrived.shape
    cols = height - 16
    whole = pl.BlockSpec(memory_space=pltpu.VMEM)
    return pl.pallas_call(
        place_body,
        in_specs=[whole] * 5,
        out_specs=(whole, whole, whole),
        out_shape=(
            jax.ShapeDtypeStruct((leaf_count, height, leaf_size), bf16),
            jax.ShapeDtypeStruct((leaf_count, cols, rank_size), bf16),
            jax.ShapeDtypeStruct((leaf_count // KIDS, cols, rank_size), bf16),
        ),
        compiler_params=pltpu.CompilerParams(vmem_limit_bytes=VMEM_LIMIT),
        cost_estimate=pl.CostEstimate(flops=8 * 10**9, bytes_accessed=9 * 10**6, transcendentals=0),
        name="place",
    )(
        src.reshape(leaf_count, 1, leaf_size),
        rank.reshape(leaf_count, 1, leaf_size),
        arrived.reshape(group_count * height, pair),
        basis,
        transfer,
    )


def near_body(list_ref, low_ref, own_ref, high_ref, after_ref, out_ref, tick_ref, rows, values):
    tick_ref[...] = jnp.zeros_like(tick_ref)
    leaf_count, height, leaf_size = own_ref.shape
    cols = height - 16
    for part, ref in enumerate((low_ref, own_ref, high_ref)):

        def fill(n, carry, part=part, ref=ref):
            values[part * leaf_count + n] = ref[n, :cols]
            tail = ref[n, cols:].astype(f32)
            rows[part * leaf_count + n] = source_rows(tail[:8], tail[8:])
            return carry

        lax.fori_loop(0, leaf_count, fill, 0)

    def leaf(i, carry):
        tail = own_ref[i, cols:].astype(f32)
        target = target_rows(tail[:8], tail[8:])
        total = jnp.zeros((leaf_size, cols), f32)
        for q in range(list_ref.shape[1]):
            j = list_ref[i, q]
            total += mm(matern(mm(target, rows[j])), values[j], NT)
        out_ref[i] = total
        return carry

    lax.fori_loop(0, leaf_count, leaf, 0)


def near_sums(lists, low, own, high, after):
    leaf_count, near = lists.shape
    height, leaf_size = own.shape[1:]
    cols = height - 16
    whole = pl.BlockSpec(memory_space=pltpu.VMEM)
    pairs = leaf_count * near * leaf_size * leaf_size
    return pl.pallas_call(
        near_body,
        in_specs=[pl.BlockSpec(memory_space=pltpu.SMEM), whole, whole, whole]
        + [pl.BlockSpec(memory_space=pl.ANY)],
        out_specs=(whole, whole),
        out_shape=(jax.ShapeDtypeStruct((leaf_count, leaf_size, cols), f32), TICK),
        scratch_shapes=[
            pltpu.VMEM((3 * leaf_count, AUG, leaf_size), bf16),
            pltpu.VMEM((3 * leaf_count, cols, leaf_size), bf16),
        ],
        compiler_params=pltpu.CompilerParams(vmem_limit_bytes=VMEM_LIMIT),
        cost_estimate=pl.CostEstimate(
            flops=pairs * 2500, bytes_accessed=6 * 10**6, transcendentals=2 * pairs
        ),
        name="near_sums",
    )(lists, low, own, high, after)


def far_rows_body(points_ref, rows_ref, tick_ref):
    step = 8

    def fill(n, carry):
        for k in range(step):
            rows_ref[n * step + k] = source_rows(*f32_halves(points_ref[n * step + k]))
        return carry

    lax.fori_loop(0, points_ref.shape[0] // step, fill, 0)
    tick_ref[...] = jnp.zeros_like(tick_ref)


def far_rows(points):
    count, _, rank_size = points.shape
    whole = pl.BlockSpec(memory_space=pltpu.VMEM)
    return pl.pallas_call(
        far_rows_body,
        in_specs=[whole],
        out_specs=(whole, whole),
        out_shape=(jax.ShapeDtypeStruct((count, AUG, rank_size), bf16), TICK),
        compiler_params=pltpu.CompilerParams(vmem_limit_bytes=VMEM_LIMIT),
        cost_estimate=pl.CostEstimate(flops=6 * 10**9, bytes_accessed=6 * 10**6, transcendentals=0),
        name="far_rows",
    )(points)


FAR_STEP = 2


def far_body(first, after_count, list_ref, target_ref, rows_ref, *refs):
    out_ref, tick_ref = refs[after_count:]
    rank_size = rows_ref.shape[2]
    far = list_ref.shape[1]
    batch = 4
    for n in range(FAR_STEP):
        i = first + pl.program_id(0) * FAR_STEP + n
        target = target_rows(*f32_halves(target_ref[i]))
        for q in range(0, far, batch):
            rows = jnp.concatenate([rows_ref[list_ref[i, q + k]] for k in range(batch)], axis=1)
            out_ref[n, :, q * rank_size : (q + batch) * rank_size] = matern(mm(target, rows))
    tick_ref[...] = jnp.zeros_like(tick_ref)


def far_kernels(first, count, lists, targets, rows, *after):
    far = lists.shape[1]
    rank_size = rows.shape[2]
    pairs = count * far * rank_size * rank_size
    anywhere = pl.BlockSpec(memory_space=pl.ANY)
    return pl.pallas_call(
        functools.partial(far_body, first, len(after)),
        grid_spec=pltpu.PrefetchScalarGridSpec(
            num_scalar_prefetch=1,
            grid=(count // FAR_STEP,),
            in_specs=[
                pl.BlockSpec(targets.shape, lambda i, s: (0, 0, 0)),
                pl.BlockSpec(rows.shape, lambda i, s: (0, 0, 0)),
            ]
            + [anywhere] * len(after),
            out_specs=(
                pl.BlockSpec((FAR_STEP, rank_size, far * rank_size), lambda i, s: (i, 0, 0)),
                pl.BlockSpec(TICK.shape, lambda i, s: (0, 0)),
            ),
        ),
        out_shape=(jax.ShapeDtypeStruct((count, rank_size, far * rank_size), bf16), TICK),
        compiler_params=pltpu.CompilerParams(vmem_limit_bytes=VMEM_LIMIT),
        cost_estimate=pl.CostEstimate(
            flops=pairs * 2500, bytes_accessed=pairs * 2, transcendentals=2 * pairs
        ),
        name="far_kernels",
    )(lists, targets, rows, *after)


def apply_body(list_ref, *refs):
    *parts, weights_ref, _, out_ref = refs
    far = list_ref.shape[1]
    i = pl.program_id(0)
    count = pl.num_programs(0)
    for p, kernel_ref in enumerate(parts):
        leaf = p * count + i
        weights = jnp.concatenate([weights_ref[list_ref[leaf, q]] for q in range(far)], axis=1)
        out_ref[p, 0] = mm(kernel_ref[0], weights, NT)


def far_sums(lists, parts, weights, after):
    count, rank_size, wide = parts[0].shape
    cols = weights.shape[1]
    total = count * len(parts)
    out = pl.pallas_call(
        apply_body,
        grid_spec=pltpu.PrefetchScalarGridSpec(
            num_scalar_prefetch=1,
            grid=(count,),
            in_specs=[pl.BlockSpec((1, rank_size, wide), lambda i, s: (i, 0, 0))] * len(parts)
            + [
                pl.BlockSpec(weights.shape, lambda i, s: (0, 0, 0)),
                pl.BlockSpec(memory_space=pl.ANY),
            ],
            out_specs=pl.BlockSpec((len(parts), 1, rank_size, cols), lambda i, s: (0, i, 0, 0)),
        ),
        out_shape=jax.ShapeDtypeStruct((len(parts), count, rank_size, cols), f32),
        compiler_params=pltpu.CompilerParams(vmem_limit_bytes=VMEM_LIMIT),
        cost_estimate=pl.CostEstimate(
            flops=total * wide * rank_size * 1000, bytes_accessed=32 * 10**6, transcendentals=0
        ),
        name="far_sums",
    )(lists, *parts, weights, after)
    return out.reshape(total, rank_size, cols)


def upper_body(list_ref, own_ref, chip_ref, across_ref, after_ref, out_ref, every_ref):
    dims, rank_size = own_ref.shape[1:]
    cols = out_ref.shape[2]
    batch = 4
    half = chip_ref.shape[0]

    def fetch(k, carry):
        far = list_ref.shape[1]
        place = list_ref[k // far, k % far]

        @pl.when(place < half)
        def _():
            every_ref[k] = chip_ref[jnp.minimum(place, half - 1)]

        @pl.when(place >= half)
        def _():
            every_ref[k] = across_ref[jnp.maximum(place - half, 0)]

        return carry

    lax.fori_loop(0, every_ref.shape[0], fetch, 0)
    for c in range(own_ref.shape[0]):
        target = target_rows(*scaled_halves(own_ref[c]))
        total = jnp.zeros((rank_size, cols), f32)
        for q in range(0, list_ref.shape[1], batch):
            blocks = [every_ref[c * list_ref.shape[1] + q + k] for k in range(batch)]
            values = jnp.concatenate([x[:cols] for x in blocks], axis=1)
            points = jnp.concatenate([x[cols:].astype(f32)[:dims] for x in blocks], axis=1)
            kernel = matern(mm(target, source_rows(*scaled_halves(points))))
            total += mm(kernel, values, NT)
        out_ref[c] = total


def upper_sums(lists, own, chip, across, after):
    count, dims, rank_size = own.shape
    cols = chip.shape[1] - 2 * dims
    whole = pl.BlockSpec(memory_space=pltpu.VMEM)
    pairs = count * lists.shape[1] * rank_size * rank_size
    return pl.pallas_call(
        upper_body,
        in_specs=[pl.BlockSpec(memory_space=pltpu.SMEM), whole, whole, whole]
        + [pl.BlockSpec(memory_space=pl.ANY)],
        out_specs=whole,
        out_shape=jax.ShapeDtypeStruct((count, rank_size, cols), f32),
        scratch_shapes=[pltpu.VMEM((count * lists.shape[1],) + chip.shape[1:], bf16)],
        compiler_params=pltpu.CompilerParams(vmem_limit_bytes=VMEM_LIMIT),
        cost_estimate=pl.CostEstimate(
            flops=pairs * 230, bytes_accessed=8 * 10**6, transcendentals=2 * pairs
        ),
        name="upper_sums",
    )(lists, own, chip, across, after)


def final_body(far_ref, upper_ref, transfer_ref, basis_ref, near_ref, out_ref):
    leaf_count, leaf_size, _ = basis_ref.shape
    step = 4

    def leaves(n, carry):
        upper = upper_ref[n * step // KIDS]
        for k in range(step):
            i = n * step + k
            skeleton = far_ref[i] + mm3(transfer_ref[i], upper)
            potential = mm3(basis_ref[i], skeleton) + near_ref[i]
            at = pl.ds(pl.multiple_of(i * leaf_size, leaf_size), leaf_size)
            out_ref[:, at] = jnp.transpose(potential)
        return carry

    lax.fori_loop(0, leaf_count // step, leaves, 0)


def final(far, upper, transfer, basis, near):
    leaf_count, leaf_size, rank_size = basis.shape
    cols = near.shape[2]
    whole = pl.BlockSpec(memory_space=pltpu.VMEM)
    return pl.pallas_call(
        final_body,
        in_specs=[whole] * 5,
        out_specs=whole,
        out_shape=jax.ShapeDtypeStruct((cols, leaf_count * leaf_size), f32),
        compiler_params=pltpu.CompilerParams(vmem_limit_bytes=VMEM_LIMIT),
        cost_estimate=pl.CostEstimate(flops=10**9, bytes_accessed=10**7, transcendentals=0),
        name="final",
    )(far, upper, transfer, basis, near)


def shifted(block, axis, move, count):
    return lax.ppermute(block, axis, [(i, move(i)) for i in range(count)])


def upper_places(clusters, count):
    owner = clusters // count
    group = (owner % 16) ^ lax.axis_index("group")
    bulk = owner // 16
    mine = lax.axis_index("bulk")
    core = (bulk ^ mine) & 1
    hops = (bulk // 2 - mine // 2) & 3
    turn = jnp.where(hops == 3, 1, jnp.where(hops == 0, 0, hops + 1))
    return (((core * 4 + turn) * 16) + group) * count + clusters % count


def local(
    points,
    weights,
    leaf_order,
    basis,
    transfer,
    skel_leaf,
    skel_upper,
    near_list,
    leaf_interaction_list,
    far_upper,
):
    row_count = leaf_order.shape[0]
    group_count = lax.axis_size("group")
    bulk_count = lax.axis_size("bulk")
    device_count = group_count * bulk_count
    pair = row_count // group_count
    leaf_count = basis.shape[0]

    src = (leaf_order // row_count % group_count).reshape(-1, 128)
    row = (leaf_order % row_count).reshape(-1, 128)
    scaled = skel_leaf.astype(f32) * POINT_SCALE
    subtree_points = lax.all_gather(scaled, "group", axis=0, tiled=True)
    want, rank = index_lists(src, row, group_count, pair)
    wanted = lax.all_to_all(want, "group", split_axis=0, concat_axis=0, tiled=True)
    picked = pick(wanted, points, weights)
    arrived = lax.all_to_all(picked, "group", split_axis=0, concat_axis=0, tiled=True)

    far_local = leaf_interaction_list - lax.axis_index("bulk") * (group_count * leaf_count)

    own, skel_wb, upper_wb = place(src, rank, arrived, basis, transfer)
    sub_w = lax.all_gather(skel_wb, "group", axis=0, tiled=True)
    forward = [(i, i + 1) for i in range(device_count - 1)]
    backward = [(i + 1, i) for i in range(device_count - 1)]
    low = lax.ppermute(own, ("bulk", "group"), forward)
    high = lax.ppermute(own, ("bulk", "group"), backward)

    def joined(tick, *blocks):
        return jnp.concatenate(blocks, axis=0) + tick[0].astype(bf16)

    def across(block, bit):
        return shifted(block, "group", lambda i: i ^ bit, group_count)

    def ahead(block):
        return shifted(block, "bulk", lambda i: (i + 2) % bulk_count, bulk_count)

    def back(block):
        return shifted(block, "bulk", lambda i: (i - 2) % bulk_count, bulk_count)

    part = leaf_count // 4
    block = jnp.concatenate([upper_wb, skel_upper, jnp.zeros(skel_upper.shape, bf16)], axis=1)
    beside = across(block, 1)
    source_points, tick = far_rows(subtree_points)
    block = joined(tick, block, beside)
    parts = []
    for n, bit in enumerate((2, 4, 8)):
        beside = across(block, bit)
        waits = (block, low, high) if n == 2 else (block,)
        kernels, tick = far_kernels(n * part, part, far_local, scaled, source_points, *waits)
        parts.append(kernels)
        block = joined(tick, block, beside)
    from_low, from_high = ahead(block), back(block)
    device = lax.axis_index(("bulk", "group"))
    near, tick = near_sums(near_list - (device - 1) * leaf_count, low, own, high, block)
    half = block.shape[0] // 2
    first = joined(tick, from_low[:half])
    second = joined(tick, from_high[half:])
    far_first, far_second = ahead(first), back(second)
    kernels, tick = far_kernels(3 * part, part, far_local, scaled, source_points, first, second)
    parts.append(kernels)
    chip = joined(tick, block, from_low, from_high, far_first, far_second)
    other = shifted(chip, "bulk", lambda i: i ^ 1, bulk_count)
    far = far_sums(far_local, parts, sub_w, chip)
    upper = upper_sums(upper_places(far_upper, skel_upper.shape[0]), skel_upper, chip, other, far)
    return final(far, upper, transfer, basis, near)


def solution(mesh):
    placed = (
        P(None, ("bulk", "group")),
        P(None, ("bulk", "group")),
        P(("bulk", "group")),
        P(("bulk", "group"), None, None),
        P(("bulk", "group"), None, None),
        P(("bulk", "group"), None, None),
        P(("bulk", "group"), None, None),
        P(("bulk", "group"), None),
        P(("bulk", "group"), None),
        P(("bulk", "group"), None),
    )
    return jax.shard_map(
        local, mesh=mesh, in_specs=placed, out_specs=P(None, ("bulk", "group")), check_vma=False
    )
```

```python
import functools
import math

import jax
import jax.numpy as jnp
from jax import lax
from jax.experimental import pallas as pl
from jax.experimental.pallas import tpu as pltpu
from jax.sharding import PartitionSpec as P

KIDS = 8

POINT_SCALE = math.sqrt(5.0) / 2.0 / math.log(2.0)
POLY_A = 3.0 / math.log(2.0)
POLY_B = 3.0 / math.log(2.0) ** 2
POLY_LOG = math.log2(math.log(2.0) ** 2 / 3.0)
AUG = 48
VMEM_LIMIT = 56 * 1024 * 1024

f32 = jnp.float32
bf16 = jnp.bfloat16
TICK = jax.ShapeDtypeStruct((8, 128), f32)
NN = (((1,), (0,)), ((), ()))
NT = (((1,), (1,)), ((), ()))


def mm(a, b, dims=NN):
    return lax.dot_general(a, b, dims, preferred_element_type=f32)


def halves(x):
    high = x.astype(bf16)
    return high, (x - high.astype(f32)).astype(bf16)


def mm3(a, b):
    a_high, a_low = halves(a)
    b_high, b_low = halves(b)
    return mm(a_high, b_high) + (mm(a_high, b_low) + mm(a_low, b_high))


def squares(high, low):
    x = high + low
    norm = jnp.sum(x * x, axis=0, keepdims=True)
    first = norm.astype(bf16).astype(f32)
    second = (norm - first).astype(bf16).astype(f32)
    third = norm - first - second
    row = lax.broadcasted_iota(jnp.int32, high.shape, 0)
    parts = jnp.where(row % 3 == 0, first, jnp.where(row % 3 == 1, second, third))
    return row, parts


def source_rows(high, low):
    row, parts = squares(high, low)
    last = jnp.where(row < 3, 1.0, jnp.where(row < 6, parts, 0.0))
    high, low = -2.0 * high, -2.0 * low
    return jnp.concatenate([high, low, high, low, last, jnp.zeros_like(last)], axis=0).astype(bf16)


def target_rows(high, low):
    row, parts = squares(high, low)
    last = jnp.where(row < 3, parts, jnp.where(row < 6, 1.0, 0.0))
    rows = jnp.concatenate([high, high, low, low, last, jnp.zeros_like(last)], axis=0)
    return jnp.transpose(rows).astype(bf16)


def f32_halves(points):
    high, low = halves(points)
    return high.astype(f32), low.astype(f32)


def scaled_halves(points):
    return f32_halves(points.astype(f32) * POINT_SCALE)


def matern(square):
    square = jnp.maximum(square, 1e-30)
    t = square * lax.rsqrt(square)
    return (((t + POLY_A) * t + POLY_B) * jnp.exp2(POLY_LOG - t)).astype(bf16)


def index_body(src_ref, row_ref, want_ref, rank_ref):
    group_count, pair = want_ref.shape
    lines = src_ref.shape[0]
    src = src_ref[...]
    row = row_ref[...]
    before = (
        lax.broadcasted_iota(jnp.int32, (128, 128), 0)
        < lax.broadcasted_iota(jnp.int32, (128, 128), 1)
    ).astype(f32).astype(bf16)
    above = (
        lax.broadcasted_iota(jnp.int32, (lines, lines), 1)
        < lax.broadcasted_iota(jnp.int32, (lines, lines), 0)
    ).astype(f32).astype(bf16)
    all_ones = jnp.ones((128, 128), bf16)
    rank = jnp.zeros(src.shape, f32)
    for g in range(group_count):
        here = src == g
        mask = here.astype(f32).astype(bf16)
        total = mm(mask, all_ones).astype(bf16)
        rank = jnp.where(here, mm(mask, before) + mm(above, total), rank)
    rank = rank.astype(jnp.int32)
    rank_ref[...] = rank
    place = lax.broadcasted_iota(jnp.int32, (pair, 256), 0)
    owner = lax.broadcasted_iota(jnp.int32, (group_count, 256), 0)
    total = jnp.zeros((2 * group_count, pair), f32)
    for k in range(0, lines, 2):
        line = lambda x: jnp.concatenate([x[k : k + 1], x[k + 1 : k + 2]], axis=1)
        rank_line, src_line, row_line = line(rank), line(src), line(row)
        spots = (place == rank_line).astype(f32).astype(bf16)
        mine = owner == src_line
        high = jnp.where(mine, (row_line >> 7).astype(f32), 0.0)
        low = jnp.where(mine, (row_line & 127).astype(f32), 0.0)
        total += mm(jnp.concatenate([high, low], axis=0).astype(bf16), spots, NT)
    want_ref[...] = (total[:group_count] * 128.0 + total[group_count:]).astype(jnp.int32)


def index_lists(src, row, group_count, pair):
    lines = src.shape[0]
    return pl.pallas_call(
        index_body,
        out_shape=(
            jax.ShapeDtypeStruct((group_count, pair), jnp.int32),
            jax.ShapeDtypeStruct((lines, 128), jnp.int32),
        ),
        compiler_params=pltpu.CompilerParams(vmem_limit_bytes=VMEM_LIMIT),
        cost_estimate=pl.CostEstimate(flops=2 * 10**9, bytes_accessed=10**5, transcendentals=0),
        name="index_lists",
    )(src, row)


def table_body(points_ref, weights_ref, table_ref):
    height = weights_ref.shape[0] + 2 * points_ref.shape[0]
    for h in range(points_ref.shape[1] // 256):
        at = slice(h * 256, (h + 1) * 256)
        high, low = scaled_halves(points_ref[:, at])
        table_ref[h * height : (h + 1) * height, :] = jnp.concatenate(
            [weights_ref[:, at], high, low], axis=0
        ).astype(bf16)


def pick_table(points, weights):
    height = weights.shape[0] + 2 * points.shape[0]
    whole = pl.BlockSpec(memory_space=pltpu.VMEM)
    return pl.pallas_call(
        table_body,
        in_specs=[whole, whole],
        out_specs=whole,
        out_shape=jax.ShapeDtypeStruct((points.shape[1] // 256 * height, 256), bf16),
        compiler_params=pltpu.CompilerParams(vmem_limit_bytes=VMEM_LIMIT),
        cost_estimate=pl.CostEstimate(flops=3 * 10**9, bytes_accessed=3 * 10**6, transcendentals=0),
        name="pick_table",
    )(points, weights)


def pick_body(want_ref, table_ref, out_ref):
    group_count, height, pair = out_ref.shape
    high_count = table_ref.shape[0] // height
    batch = 4

    def device(d, carry):
        want = want_ref[d]
        low = want & 255
        high = want >> 8
        spots = (lax.broadcasted_iota(jnp.int32, (256, pair), 0) == low).astype(f32).astype(bf16)
        picked = jnp.zeros((height, pair), f32)
        for h in range(0, high_count, batch):
            found = mm(table_ref[h * height : (h + batch) * height, :], spots)
            for k in range(batch):
                picked = jnp.where(high == h + k, found[k * height : (k + 1) * height], picked)
        out_ref[d] = picked.astype(bf16)
        return carry

    lax.fori_loop(0, group_count, device, 0)


def pick(want, table, row_count):
    group_count, pair = want.shape
    height = table.shape[0] * 256 // row_count
    whole = pl.BlockSpec(memory_space=pltpu.VMEM)
    return pl.pallas_call(
        pick_body,
        in_specs=[whole, whole],
        out_specs=whole,
        out_shape=jax.ShapeDtypeStruct((group_count, height, pair), bf16),
        compiler_params=pltpu.CompilerParams(vmem_limit_bytes=VMEM_LIMIT),
        cost_estimate=pl.CostEstimate(flops=6 * 10**9, bytes_accessed=3 * 10**6, transcendentals=0),
        name="pick",
    )(want.reshape(group_count, 1, pair), table)


def place_body(src_ref, rank_ref, arrived_ref, basis_ref, transfer_ref, leaf_ref, skel_ref, upper_ref):
    leaf_count, height, leaf_size = leaf_ref.shape
    pair = arrived_ref.shape[1]
    group_count = arrived_ref.shape[0] // height
    cols = skel_ref.shape[1]
    batch = 4

    def cluster(c, carry):
        total = jnp.zeros(upper_ref.shape[1:], f32)
        for n in range(KIDS):
            i = c * KIDS + n
            src = src_ref[i]
            spots = (
                lax.broadcasted_iota(jnp.int32, (pair, leaf_size), 0) == rank_ref[i]
            ).astype(f32).astype(bf16)
            placed = jnp.zeros((height, leaf_size), f32)
            for g in range(0, group_count, batch):
                found = mm(arrived_ref[g * height : (g + batch) * height, :], spots)
                for k in range(batch):
                    placed = jnp.where(src == g + k, found[k * height : (k + 1) * height], placed)
            placed = placed.astype(bf16)
            leaf_ref[i] = placed
            basis_high, basis_low = halves(basis_ref[i])
            skel = mm(placed[:cols], basis_high) + mm(placed[:cols], basis_low)
            skel_ref[i] = skel.astype(bf16)
            total += mm3(skel, transfer_ref[i])
        upper_ref[c] = total.astype(bf16)
        return carry

    lax.fori_loop(0, leaf_count // KIDS, cluster, 0)


def place(src, rank, arrived, basis, transfer):
    leaf_count, leaf_size, rank_size = basis.shape
    group_count, height, pair = arrived.shape
    cols = height - 16
    whole = pl.BlockSpec(memory_space=pltpu.VMEM)
    return pl.pallas_call(
        place_body,
        in_specs=[whole] * 5,
        out_specs=(whole, whole, whole),
        out_shape=(
            jax.ShapeDtypeStruct((leaf_count, height, leaf_size), bf16),
            jax.ShapeDtypeStruct((leaf_count, cols, rank_size), bf16),
            jax.ShapeDtypeStruct((leaf_count // KIDS, cols, rank_size), bf16),
        ),
        compiler_params=pltpu.CompilerParams(vmem_limit_bytes=VMEM_LIMIT),
        cost_estimate=pl.CostEstimate(flops=8 * 10**9, bytes_accessed=9 * 10**6, transcendentals=0),
        name="place",
    )(
        src.reshape(leaf_count, 1, leaf_size),
        rank.reshape(leaf_count, 1, leaf_size),
        arrived.reshape(group_count * height, pair),
        basis,
        transfer,
    )


def near_body(list_ref, low_ref, own_ref, high_ref, after_ref, out_ref, tick_ref, rows, values):
    tick_ref[...] = jnp.zeros_like(tick_ref)
    leaf_count, height, leaf_size = own_ref.shape
    cols = height - 16
    for part, ref in enumerate((low_ref, own_ref, high_ref)):

        def fill(n, carry, part=part, ref=ref):
            values[part * leaf_count + n] = ref[n, :cols]
            tail = ref[n, cols:].astype(f32)
            rows[part * leaf_count + n] = source_rows(tail[:8], tail[8:])
            return carry

        lax.fori_loop(0, leaf_count, fill, 0)

    def leaf(i, carry):
        tail = own_ref[i, cols:].astype(f32)
        target = target_rows(tail[:8], tail[8:])
        total = jnp.zeros((leaf_size, cols), f32)
        for q in range(list_ref.shape[1]):
            j = list_ref[i, q]
            total += mm(matern(mm(target, rows[j])), values[j], NT)
        out_ref[i] = total
        return carry

    lax.fori_loop(0, leaf_count, leaf, 0)


def near_sums(lists, low, own, high, after):
    leaf_count, near = lists.shape
    height, leaf_size = own.shape[1:]
    cols = height - 16
    whole = pl.BlockSpec(memory_space=pltpu.VMEM)
    pairs = leaf_count * near * leaf_size * leaf_size
    return pl.pallas_call(
        near_body,
        in_specs=[pl.BlockSpec(memory_space=pltpu.SMEM), whole, whole, whole]
        + [pl.BlockSpec(memory_space=pl.ANY)],
        out_specs=(whole, whole),
        out_shape=(jax.ShapeDtypeStruct((leaf_count, leaf_size, cols), f32), TICK),
        scratch_shapes=[
            pltpu.VMEM((3 * leaf_count, AUG, leaf_size), bf16),
            pltpu.VMEM((3 * leaf_count, cols, leaf_size), bf16),
        ],
        compiler_params=pltpu.CompilerParams(vmem_limit_bytes=VMEM_LIMIT),
        cost_estimate=pl.CostEstimate(
            flops=pairs * 2500, bytes_accessed=6 * 10**6, transcendentals=2 * pairs
        ),
        name="near_sums",
    )(lists, low, own, high, after)


def far_rows_body(points_ref, rows_ref):
    step = 8

    def fill(n, carry):
        for k in range(step):
            rows_ref[n * step + k] = source_rows(*f32_halves(points_ref[n * step + k]))
        return carry

    lax.fori_loop(0, points_ref.shape[0] // step, fill, 0)


def far_rows(points):
    count, _, rank_size = points.shape
    whole = pl.BlockSpec(memory_space=pltpu.VMEM)
    return pl.pallas_call(
        far_rows_body,
        in_specs=[whole],
        out_specs=whole,
        out_shape=jax.ShapeDtypeStruct((count, AUG, rank_size), bf16),
        compiler_params=pltpu.CompilerParams(vmem_limit_bytes=VMEM_LIMIT),
        cost_estimate=pl.CostEstimate(flops=6 * 10**9, bytes_accessed=6 * 10**6, transcendentals=0),
        name="far_rows",
    )(points)


FAR_STEP = 4


def far_body(first, after_count, list_ref, target_ref, rows_ref, *refs):
    out_ref, tick_ref = refs[after_count:]
    rank_size = rows_ref.shape[2]
    far = list_ref.shape[1]
    batch = 4
    for n in range(FAR_STEP):
        i = first + pl.program_id(0) * FAR_STEP + n
        target = target_rows(*f32_halves(target_ref[i]))
        for q in range(0, far, batch):
            rows = jnp.concatenate([rows_ref[list_ref[i, q + k]] for k in range(batch)], axis=1)
            out_ref[n, :, q * rank_size : (q + batch) * rank_size] = matern(mm(target, rows))
    tick_ref[...] = jnp.zeros_like(tick_ref)


def far_kernels(first, count, lists, targets, rows, *after):
    far = lists.shape[1]
    rank_size = rows.shape[2]
    pairs = count * far * rank_size * rank_size
    anywhere = pl.BlockSpec(memory_space=pl.ANY)
    return pl.pallas_call(
        functools.partial(far_body, first, len(after)),
        grid_spec=pltpu.PrefetchScalarGridSpec(
            num_scalar_prefetch=1,
            grid=(count // FAR_STEP,),
            in_specs=[
                pl.BlockSpec(targets.shape, lambda i, s: (0, 0, 0)),
                pl.BlockSpec(rows.shape, lambda i, s: (0, 0, 0)),
            ]
            + [anywhere] * len(after),
            out_specs=(
                pl.BlockSpec((FAR_STEP, rank_size, far * rank_size), lambda i, s: (i, 0, 0)),
                pl.BlockSpec(TICK.shape, lambda i, s: (0, 0)),
            ),
        ),
        out_shape=(jax.ShapeDtypeStruct((count, rank_size, far * rank_size), bf16), TICK),
        compiler_params=pltpu.CompilerParams(vmem_limit_bytes=VMEM_LIMIT),
        cost_estimate=pl.CostEstimate(
            flops=pairs * 2500, bytes_accessed=pairs * 2, transcendentals=2 * pairs
        ),
        name="far_kernels",
    )(lists, targets, rows, *after)


APPLY_STEP = 4


def apply_body(list_ref, kernel_ref, weights_ref, _, out_ref):
    far = list_ref.shape[1]
    for n in range(APPLY_STEP):
        leaf = pl.program_id(0) * APPLY_STEP + n
        weights = jnp.concatenate([weights_ref[list_ref[leaf, q]] for q in range(far)], axis=1)
        out_ref[n] = mm(kernel_ref[n], weights, NT)


def far_sums(lists, kernels, weights, after):
    count, rank_size, wide = kernels.shape
    cols = weights.shape[1]
    return pl.pallas_call(
        apply_body,
        grid_spec=pltpu.PrefetchScalarGridSpec(
            num_scalar_prefetch=1,
            grid=(count // APPLY_STEP,),
            in_specs=[
                pl.BlockSpec((APPLY_STEP, rank_size, wide), lambda i, s: (i, 0, 0)),
                pl.BlockSpec(weights.shape, lambda i, s: (0, 0, 0)),
                pl.BlockSpec(memory_space=pl.ANY),
            ],
            out_specs=pl.BlockSpec((APPLY_STEP, rank_size, cols), lambda i, s: (i, 0, 0)),
        ),
        out_shape=jax.ShapeDtypeStruct((count, rank_size, cols), f32),
        compiler_params=pltpu.CompilerParams(vmem_limit_bytes=VMEM_LIMIT),
        cost_estimate=pl.CostEstimate(
            flops=count * wide * rank_size * 1000, bytes_accessed=20 * 10**6, transcendentals=0
        ),
        name="far_sums",
    )(lists, kernels, weights, after)


def fused_body(first, list_ref, target_ref, rows_ref, weights_ref, after_ref, out_ref, tick_ref, even, odd):
    tick_ref[...] = jnp.zeros_like(tick_ref)
    count = out_ref.shape[0]
    rank_size = weights_ref.shape[2]
    far = list_ref.shape[1]
    batch = 4

    def listed(ref, i, q, n):
        return jnp.concatenate([ref[list_ref[i, q + k]] for k in range(n)], axis=1)

    def fill(n, kernel):
        i = first + n
        target = target_rows(*f32_halves(target_ref[i]))
        for q in range(0, far, batch):
            kernel[:, q * rank_size : (q + batch) * rank_size] = matern(
                mm(target, listed(rows_ref, i, q, batch))
            )

    def apply(n, kernel):
        out_ref[n] = mm(kernel[...], listed(weights_ref, first + n, 0, far), NT)

    fill(0, even)

    def two(n, carry):
        fill(2 * n + 1, odd)
        apply(2 * n, even)
        fill(jnp.minimum(2 * n + 2, count - 1), even)
        apply(2 * n + 1, odd)
        return carry

    lax.fori_loop(0, count // 2, two, 0)


def fused_sums(first, count, lists, targets, rows, weights, after):
    far = lists.shape[1]
    cols, rank_size = weights.shape[1:]
    whole = pl.BlockSpec(memory_space=pltpu.VMEM)
    pairs = count * far * rank_size * rank_size
    return pl.pallas_call(
        functools.partial(fused_body, first),
        in_specs=[pl.BlockSpec(memory_space=pltpu.SMEM), whole, whole, whole]
        + [pl.BlockSpec(memory_space=pl.ANY)],
        out_specs=(whole, whole),
        out_shape=(jax.ShapeDtypeStruct((count, rank_size, cols), f32), TICK),
        scratch_shapes=[pltpu.VMEM((rank_size, far * rank_size), bf16)] * 2,
        compiler_params=pltpu.CompilerParams(vmem_limit_bytes=VMEM_LIMIT),
        cost_estimate=pl.CostEstimate(
            flops=pairs * 2500, bytes_accessed=12 * 10**6, transcendentals=2 * pairs
        ),
        name="fused_sums",
    )(lists, targets, rows, weights, after)


def upper_body(list_ref, own_ref, chip_ref, across_ref, after_ref, out_ref, every_ref):
    dims, rank_size = own_ref.shape[1:]
    cols = out_ref.shape[2]
    batch = 4
    half = chip_ref.shape[0]

    def fetch(k, carry):
        far = list_ref.shape[1]
        place = list_ref[k // far, k % far]

        @pl.when(place < half)
        def _():
            every_ref[k] = chip_ref[jnp.minimum(place, half - 1)]

        @pl.when(place >= half)
        def _():
            every_ref[k] = across_ref[jnp.maximum(place - half, 0)]

        return carry

    lax.fori_loop(0, every_ref.shape[0], fetch, 0)
    for c in range(own_ref.shape[0]):
        target = target_rows(*scaled_halves(own_ref[c]))
        total = jnp.zeros((rank_size, cols), f32)
        for q in range(0, list_ref.shape[1], batch):
            blocks = [every_ref[c * list_ref.shape[1] + q + k] for k in range(batch)]
            values = jnp.concatenate([x[:cols] for x in blocks], axis=1)
            points = jnp.concatenate([x[cols:].astype(f32)[:dims] for x in blocks], axis=1)
            kernel = matern(mm(target, source_rows(*scaled_halves(points))))
            total += mm(kernel, values, NT)
        out_ref[c] = total


def upper_sums(lists, own, chip, across, after):
    count, dims, rank_size = own.shape
    cols = chip.shape[1] - 2 * dims
    whole = pl.BlockSpec(memory_space=pltpu.VMEM)
    pairs = count * lists.shape[1] * rank_size * rank_size
    return pl.pallas_call(
        upper_body,
        in_specs=[pl.BlockSpec(memory_space=pltpu.SMEM), whole, whole, whole]
        + [pl.BlockSpec(memory_space=pl.ANY)],
        out_specs=whole,
        out_shape=jax.ShapeDtypeStruct((count, rank_size, cols), f32),
        scratch_shapes=[pltpu.VMEM((count * lists.shape[1],) + chip.shape[1:], bf16)],
        compiler_params=pltpu.CompilerParams(vmem_limit_bytes=VMEM_LIMIT),
        cost_estimate=pl.CostEstimate(
            flops=pairs * 230, bytes_accessed=8 * 10**6, transcendentals=2 * pairs
        ),
        name="upper_sums",
    )(lists, own, chip, across, after)


def final_body(first_ref, second_ref, upper_ref, transfer_ref, basis_ref, near_ref, out_ref):
    leaf_size = basis_ref.shape[1]
    step = 4
    for part, far_ref in enumerate((first_ref, second_ref)):
        count = far_ref.shape[0]

        def leaves(n, carry, far_ref=far_ref, start=part * count):
            upper = upper_ref[(start + n * step) // KIDS]
            for k in range(step):
                i = start + n * step + k
                skeleton = far_ref[n * step + k] + mm3(transfer_ref[i], upper)
                potential = mm3(basis_ref[i], skeleton) + near_ref[i]
                at = pl.ds(pl.multiple_of(i * leaf_size, leaf_size), leaf_size)
                out_ref[:, at] = jnp.transpose(potential)
            return carry

        lax.fori_loop(0, count // step, leaves, 0)


def final(first, second, upper, transfer, basis, near):
    leaf_count, leaf_size, rank_size = basis.shape
    cols = near.shape[2]
    whole = pl.BlockSpec(memory_space=pltpu.VMEM)
    return pl.pallas_call(
        final_body,
        in_specs=[whole] * 6,
        out_specs=whole,
        out_shape=jax.ShapeDtypeStruct((cols, leaf_count * leaf_size), f32),
        compiler_params=pltpu.CompilerParams(vmem_limit_bytes=VMEM_LIMIT),
        cost_estimate=pl.CostEstimate(flops=10**9, bytes_accessed=10**7, transcendentals=0),
        name="final",
    )(first, second, upper, transfer, basis, near)


def shifted(block, axis, move, count):
    return lax.ppermute(block, axis, [(i, move(i)) for i in range(count)])


def upper_places(clusters, count):
    owner = clusters // count
    group = owner % 16
    bulk = owner // 16
    mine = lax.axis_index("bulk")
    core = (bulk ^ mine) & 1
    hops = (bulk // 2 - mine // 2) & 3
    turn = jnp.where(hops == 3, 1, jnp.where(hops == 0, 0, hops + 1))
    return (((core * 4 + turn) * 16) + group) * count + clusters % count


def local(
    points,
    weights,
    leaf_order,
    basis,
    transfer,
    skel_leaf,
    skel_upper,
    near_list,
    leaf_interaction_list,
    far_upper,
):
    row_count = leaf_order.shape[0]
    group_count = lax.axis_size("group")
    bulk_count = lax.axis_size("bulk")
    device_count = group_count * bulk_count
    pair = row_count // group_count
    leaf_count = basis.shape[0]

    src = (leaf_order // row_count % group_count).reshape(-1, 128)
    row = (leaf_order % row_count).reshape(-1, 128)
    scaled = skel_leaf.astype(f32) * POINT_SCALE
    subtree_points = lax.all_gather(scaled, "group", axis=0, tiled=True)
    want, rank = index_lists(src, row, group_count, pair)
    wanted = lax.all_to_all(want, "group", split_axis=0, concat_axis=0, tiled=True)
    picked = pick(wanted, pick_table(points, weights), row_count)
    arrived = lax.all_to_all(picked, "group", split_axis=0, concat_axis=0, tiled=True)

    far_local = leaf_interaction_list - lax.axis_index("bulk") * (group_count * leaf_count)

    own, skel_wb, upper_wb = place(src, rank, arrived, basis, transfer)
    sub_w = lax.all_gather(skel_wb, "group", axis=0, tiled=True)
    forward = [(i, i + 1) for i in range(device_count - 1)]
    backward = [(i + 1, i) for i in range(device_count - 1)]
    low = lax.ppermute(own, ("bulk", "group"), forward)
    high = lax.ppermute(own, ("bulk", "group"), backward)

    def joined(tick, *blocks):
        return jnp.concatenate(blocks, axis=0) + tick[0].astype(bf16)

    def ahead(block):
        return shifted(block, "bulk", lambda i: (i + 2) % bulk_count, bulk_count)

    def back(block):
        return shifted(block, "bulk", lambda i: (i - 2) % bulk_count, bulk_count)

    mine = jnp.concatenate([upper_wb, skel_upper, jnp.zeros(skel_upper.shape, bf16)], axis=1)
    copies = jnp.tile(mine, (group_count, 1, 1))
    block = lax.all_to_all(copies, "group", split_axis=0, concat_axis=0, tiled=True)
    part = leaf_count // 2
    source_points = far_rows(subtree_points)
    kernels, tick = far_kernels(0, part, far_local, scaled, source_points, copies)
    block = joined(tick, block)
    from_low, from_high = ahead(block), back(block)
    device = lax.axis_index(("bulk", "group"))
    near, tick = near_sums(near_list - (device - 1) * leaf_count, low, own, high, block)
    half = block.shape[0] // 2
    first = joined(tick, from_low[:half])
    second = joined(tick, from_high[half:])
    far_first, far_second = ahead(first), back(second)
    far_late, tick = fused_sums(part, part, far_local, scaled, source_points, sub_w, first)
    chip = jnp.concatenate([block, from_low, from_high, joined(tick, far_first, far_second)], axis=0)
    other = shifted(chip, "bulk", lambda i: i ^ 1, bulk_count)
    far_early = far_sums(far_local, kernels, sub_w, chip)
    upper = upper_sums(upper_places(far_upper, skel_upper.shape[0]), skel_upper, chip, other, far_early)
    return final(far_early, far_late, upper, transfer, basis, near)


def solution(mesh):
    placed = (
        P(None, ("bulk", "group")),
        P(None, ("bulk", "group")),
        P(("bulk", "group")),
        P(("bulk", "group"), None, None),
        P(("bulk", "group"), None, None),
        P(("bulk", "group"), None, None),
        P(("bulk", "group"), None, None),
        P(("bulk", "group"), None),
        P(("bulk", "group"), None),
        P(("bulk", "group"), None),
    )
    return jax.shard_map(
        local, mesh=mesh, in_specs=placed, out_specs=P(None, ("bulk", "group")), check_vma=False
    )
```

```python
import functools
import math

import jax
import jax.numpy as jnp
from jax import lax
from jax.experimental import pallas as pl
from jax.experimental.pallas import tpu as pltpu
from jax.sharding import PartitionSpec as P

KIDS = 8

POINT_SCALE = math.sqrt(5.0) / 2.0 / math.log(2.0)
POLY_A = 3.0 / math.log(2.0)
POLY_B = 3.0 / math.log(2.0) ** 2
POLY_LOG = math.log2(math.log(2.0) ** 2 / 3.0)
AUG = 48
MIB = 1024 * 1024

f32 = jnp.float32
bf16 = jnp.bfloat16
TICK = jax.ShapeDtypeStruct((8, 128), f32)
NN = (((1,), (0,)), ((), ()))
NT = (((1,), (1,)), ((), ()))


def mm(a, b, dims=NN):
    return lax.dot_general(a, b, dims, preferred_element_type=f32)


def halves(x):
    high = x.astype(bf16)
    return high, (x - high.astype(f32)).astype(bf16)


def mm3(a, b):
    a_high, a_low = halves(a)
    b_high, b_low = halves(b)
    return mm(a_high, b_high) + (mm(a_high, b_low) + mm(a_low, b_high))


def squares(high, low):
    x = high + low
    norm = jnp.sum(x * x, axis=0, keepdims=True)
    first = norm.astype(bf16).astype(f32)
    second = (norm - first).astype(bf16).astype(f32)
    third = norm - first - second
    row = lax.broadcasted_iota(jnp.int32, high.shape, 0)
    parts = jnp.where(row % 3 == 0, first, jnp.where(row % 3 == 1, second, third))
    return row, parts


def source_rows(high, low):
    row, parts = squares(high, low)
    last = jnp.where(row < 3, 1.0, jnp.where(row < 6, parts, 0.0))
    high, low = -2.0 * high, -2.0 * low
    return jnp.concatenate([high, low, high, low, last, jnp.zeros_like(last)], axis=0).astype(bf16)


def target_rows(high, low):
    row, parts = squares(high, low)
    last = jnp.where(row < 3, parts, jnp.where(row < 6, 1.0, 0.0))
    rows = jnp.concatenate([high, high, low, low, last, jnp.zeros_like(last)], axis=0)
    return jnp.transpose(rows).astype(bf16)


def f32_halves(points):
    high, low = halves(points)
    return high.astype(f32), low.astype(f32)


def scaled_halves(points):
    return f32_halves(points.astype(f32) * POINT_SCALE)


def matern(square):
    square = jnp.maximum(square, 1e-30)
    t = square * lax.rsqrt(square)
    return (((t + POLY_A) * t + POLY_B) * jnp.exp2(POLY_LOG - t)).astype(bf16)


def index_body(order_ref, want_ref, src_ref, rank_ref):
    group_count, _, pair = want_ref.shape
    lines = order_ref.shape[0]
    row_count = group_count * pair
    order = order_ref[...]
    owner = ((order.astype(f32) + 0.5) * (1.0 / row_count)).astype(jnp.int32)
    src = owner % group_count
    row = order - owner * row_count
    before = (
        lax.broadcasted_iota(jnp.int32, (128, 128), 0)
        < lax.broadcasted_iota(jnp.int32, (128, 128), 1)
    ).astype(f32).astype(bf16)
    above = (
        lax.broadcasted_iota(jnp.int32, (lines, lines), 1)
        < lax.broadcasted_iota(jnp.int32, (lines, lines), 0)
    ).astype(f32).astype(bf16)
    all_ones = jnp.ones((128, 128), bf16)
    rank = jnp.zeros(src.shape, f32)
    for g in range(group_count):
        here = src == g
        mask = here.astype(f32).astype(bf16)
        total = mm(mask, all_ones).astype(bf16)
        rank = jnp.where(here, mm(mask, before) + mm(above, total), rank)
    rank = rank.astype(jnp.int32)
    for i in range(lines // 2):
        for ref, x in ((src_ref, src), (rank_ref, rank)):
            ref[i] = jnp.concatenate([x[2 * i : 2 * i + 1], x[2 * i + 1 : 2 * i + 2]], axis=1)
    place = lax.broadcasted_iota(jnp.int32, (pair, 256), 0)
    owner = lax.broadcasted_iota(jnp.int32, (group_count, 256), 0)
    total = jnp.zeros((2 * group_count, pair), f32)
    for k in range(0, lines, 2):
        line = lambda x: jnp.concatenate([x[k : k + 1], x[k + 1 : k + 2]], axis=1)
        rank_line, src_line, row_line = line(rank), line(src), line(row)
        spots = (place == rank_line).astype(f32).astype(bf16)
        mine = owner == src_line
        high = jnp.where(mine, (row_line >> 7).astype(f32), 0.0)
        low = jnp.where(mine, (row_line & 127).astype(f32), 0.0)
        total += mm(jnp.concatenate([high, low], axis=0).astype(bf16), spots, NT)
    want = (total[:group_count] * 128.0 + total[group_count:]).astype(jnp.int32)
    for g in range(group_count):
        want_ref[g] = want[g : g + 1]


def index_lists(order, group_count, leaf_size):
    row_count = order.shape[0]
    assert leaf_size == 256
    return pl.pallas_call(
        index_body,
        out_shape=(
            jax.ShapeDtypeStruct((group_count, 1, row_count // group_count), jnp.int32),
            jax.ShapeDtypeStruct((row_count // leaf_size, 1, leaf_size), jnp.int32),
            jax.ShapeDtypeStruct((row_count // leaf_size, 1, leaf_size), jnp.int32),
        ),
        compiler_params=pltpu.CompilerParams(vmem_limit_bytes=8 * MIB),
        cost_estimate=pl.CostEstimate(flops=2 * 10**9, bytes_accessed=10**5, transcendentals=0),
        name="index_lists",
    )(order.reshape(-1, 128))


def table_body(points_ref, weights_ref, table_ref):
    height = weights_ref.shape[0] + 2 * points_ref.shape[0]
    for h in range(points_ref.shape[1] // 256):
        at = slice(h * 256, (h + 1) * 256)
        high, low = scaled_halves(points_ref[:, at])
        table_ref[h * height : (h + 1) * height, :] = jnp.concatenate(
            [weights_ref[:, at], high, low], axis=0
        ).astype(bf16)


def pick_table(points, weights):
    height = weights.shape[0] + 2 * points.shape[0]
    whole = pl.BlockSpec(memory_space=pltpu.VMEM)
    return pl.pallas_call(
        table_body,
        in_specs=[whole, whole],
        out_specs=whole,
        out_shape=jax.ShapeDtypeStruct((points.shape[1] // 256 * height, 256), bf16),
        compiler_params=pltpu.CompilerParams(vmem_limit_bytes=10 * MIB),
        cost_estimate=pl.CostEstimate(flops=3 * 10**9, bytes_accessed=3 * 10**6, transcendentals=0),
        name="pick_table",
    )(points, weights)


def pick_body(want_ref, table_ref, out_ref):
    group_count, height, pair = out_ref.shape
    high_count = table_ref.shape[0] // height
    batch = 4

    def device(d, carry):
        want = want_ref[d]
        low = want & 255
        high = want >> 8
        spots = (lax.broadcasted_iota(jnp.int32, (256, pair), 0) == low).astype(f32).astype(bf16)
        picked = jnp.zeros((height, pair), f32)
        for h in range(0, high_count, batch):
            found = mm(table_ref[h * height : (h + batch) * height, :], spots)
            for k in range(batch):
                picked = jnp.where(high == h + k, found[k * height : (k + 1) * height], picked)
        out_ref[d] = picked.astype(bf16)
        return carry

    lax.fori_loop(0, group_count, device, 0)


def pick(want, table, row_count):
    group_count, _, pair = want.shape
    height = table.shape[0] * 256 // row_count
    whole = pl.BlockSpec(memory_space=pltpu.VMEM)
    return pl.pallas_call(
        pick_body,
        in_specs=[whole, whole],
        out_specs=whole,
        out_shape=jax.ShapeDtypeStruct((group_count, height, pair), bf16),
        compiler_params=pltpu.CompilerParams(vmem_limit_bytes=14 * MIB),
        cost_estimate=pl.CostEstimate(flops=6 * 10**9, bytes_accessed=3 * 10**6, transcendentals=0),
        name="pick",
    )(want, table)


def place_body(src_ref, rank_ref, arrived_ref, leaf_ref):
    leaf_count, height, leaf_size = leaf_ref.shape
    pair = arrived_ref.shape[1]
    group_count = arrived_ref.shape[0] // height
    batch = 4
    step = 4

    def leaves(c, carry):
        for n in range(step):
            i = c * step + n
            src = src_ref[i]
            spots = (
                lax.broadcasted_iota(jnp.int32, (pair, leaf_size), 0) == rank_ref[i]
            ).astype(f32).astype(bf16)
            placed = jnp.zeros((height, leaf_size), f32)
            for g in range(0, group_count, batch):
                found = mm(arrived_ref[g * height : (g + batch) * height, :], spots)
                for k in range(batch):
                    placed = jnp.where(src == g + k, found[k * height : (k + 1) * height], placed)
            leaf_ref[i] = placed.astype(bf16)
        return carry

    lax.fori_loop(0, leaf_count // step, leaves, 0)


def place(src, rank, arrived):
    group_count, height, pair = arrived.shape
    leaf_count, _, leaf_size = src.shape
    whole = pl.BlockSpec(memory_space=pltpu.VMEM)
    return pl.pallas_call(
        place_body,
        in_specs=[whole] * 3,
        out_specs=whole,
        out_shape=jax.ShapeDtypeStruct((leaf_count, height, leaf_size), bf16),
        compiler_params=pltpu.CompilerParams(vmem_limit_bytes=12 * MIB),
        cost_estimate=pl.CostEstimate(flops=8 * 10**9, bytes_accessed=2 * 10**6, transcendentals=0),
        name="place",
    )(src, rank, arrived.reshape(group_count * height, pair))


def skeleton_body(leaf_ref, basis_ref, transfer_ref, skel_ref, upper_ref):
    leaf_count, cols, _ = skel_ref.shape

    def cluster(c, carry):
        total = jnp.zeros(upper_ref.shape[1:], f32)
        for n in range(KIDS):
            i = c * KIDS + n
            values = leaf_ref[i, :cols]
            basis_high, basis_low = halves(basis_ref[i])
            skel = mm(values, basis_high) + mm(values, basis_low)
            skel_ref[i] = skel.astype(bf16)
            total += mm3(skel, transfer_ref[i])
        upper_ref[c] = total.astype(bf16)
        return carry

    lax.fori_loop(0, leaf_count // KIDS, cluster, 0)


def skeleton(leaves, basis, transfer):
    leaf_count, _, rank_size = basis.shape
    cols = leaves.shape[1] - 16
    whole = pl.BlockSpec(memory_space=pltpu.VMEM)
    return pl.pallas_call(
        skeleton_body,
        in_specs=[whole] * 3,
        out_specs=(whole, whole),
        out_shape=(
            jax.ShapeDtypeStruct((leaf_count, cols, rank_size), bf16),
            jax.ShapeDtypeStruct((leaf_count // KIDS, cols, rank_size), bf16),
        ),
        compiler_params=pltpu.CompilerParams(vmem_limit_bytes=14 * MIB),
        cost_estimate=pl.CostEstimate(flops=10**9, bytes_accessed=7 * 10**6, transcendentals=0),
        name="skeleton",
    )(leaves, basis, transfer)


def near_body(list_ref, low_ref, own_ref, high_ref, after_ref, out_ref, tick_ref, rows, values):
    tick_ref[...] = jnp.zeros_like(tick_ref)
    leaf_count, height, leaf_size = own_ref.shape
    cols = height - 16
    for part, ref in enumerate((low_ref, own_ref, high_ref)):

        def fill(n, carry, part=part, ref=ref):
            values[part * leaf_count + n] = ref[n, :cols]
            tail = ref[n, cols:].astype(f32)
            rows[part * leaf_count + n] = source_rows(tail[:8], tail[8:])
            return carry

        lax.fori_loop(0, leaf_count, fill, 0)

    def leaf(i, carry):
        tail = own_ref[i, cols:].astype(f32)
        target = target_rows(tail[:8], tail[8:])
        total = jnp.zeros((leaf_size, cols), f32)
        for q in range(list_ref.shape[1]):
            j = list_ref[i, q]
            total += mm(matern(mm(target, rows[j])), values[j], NT)
        out_ref[i] = total
        return carry

    lax.fori_loop(0, leaf_count, leaf, 0)


def near_sums(lists, low, own, high, after):
    leaf_count, near = lists.shape
    height, leaf_size = own.shape[1:]
    cols = height - 16
    whole = pl.BlockSpec(memory_space=pltpu.VMEM)
    pairs = leaf_count * near * leaf_size * leaf_size
    return pl.pallas_call(
        near_body,
        in_specs=[pl.BlockSpec(memory_space=pltpu.SMEM), whole, whole, whole]
        + [pl.BlockSpec(memory_space=pl.ANY)],
        out_specs=(whole, whole),
        out_shape=(jax.ShapeDtypeStruct((leaf_count, leaf_size, cols), f32), TICK),
        scratch_shapes=[
            pltpu.VMEM((3 * leaf_count, AUG, leaf_size), bf16),
            pltpu.VMEM((3 * leaf_count, cols, leaf_size), bf16),
        ],
        compiler_params=pltpu.CompilerParams(vmem_limit_bytes=20 * MIB),
        cost_estimate=pl.CostEstimate(
            flops=pairs * 2500, bytes_accessed=6 * 10**6, transcendentals=2 * pairs
        ),
        name="near_sums",
    )(lists, low, own, high, after)


def far_rows_body(points_ref, rows_ref):
    step = 8

    def fill(n, carry):
        for k in range(step):
            rows_ref[n * step + k] = source_rows(*f32_halves(points_ref[n * step + k]))
        return carry

    lax.fori_loop(0, points_ref.shape[0] // step, fill, 0)


def far_rows(points):
    count, _, rank_size = points.shape
    whole = pl.BlockSpec(memory_space=pltpu.VMEM)
    return pl.pallas_call(
        far_rows_body,
        in_specs=[whole],
        out_specs=whole,
        out_shape=jax.ShapeDtypeStruct((count, AUG, rank_size), bf16),
        compiler_params=pltpu.CompilerParams(vmem_limit_bytes=14 * MIB),
        cost_estimate=pl.CostEstimate(flops=10**8, bytes_accessed=10**6, transcendentals=0),
        name="far_rows",
    )(points)


FAR_STEP = 4


def far_body(first, after_count, list_ref, target_ref, rows_ref, *refs):
    out_ref, tick_ref = refs[after_count:]
    rank_size = rows_ref.shape[2]
    far = list_ref.shape[1]
    batch = 4
    for n in range(FAR_STEP):
        i = first + pl.program_id(0) * FAR_STEP + n
        target = target_rows(*f32_halves(target_ref[i]))
        for q in range(0, far, batch):
            rows = jnp.concatenate([rows_ref[list_ref[i, q + k]] for k in range(batch)], axis=1)
            out_ref[n, :, q * rank_size : (q + batch) * rank_size] = matern(mm(target, rows))
    tick_ref[...] = jnp.zeros_like(tick_ref)


def far_kernels(first, count, lists, targets, rows, *after):
    far = lists.shape[1]
    rank_size = rows.shape[2]
    pairs = count * far * rank_size * rank_size
    anywhere = pl.BlockSpec(memory_space=pl.ANY)
    return pl.pallas_call(
        functools.partial(far_body, first, len(after)),
        grid_spec=pltpu.PrefetchScalarGridSpec(
            num_scalar_prefetch=1,
            grid=(count // FAR_STEP,),
            in_specs=[
                pl.BlockSpec(targets.shape, lambda i, s: (0, 0, 0)),
                pl.BlockSpec(rows.shape, lambda i, s: (0, 0, 0)),
            ]
            + [anywhere] * len(after),
            out_specs=(
                pl.BlockSpec((FAR_STEP, rank_size, far * rank_size), lambda i, s: (i, 0, 0)),
                pl.BlockSpec(TICK.shape, lambda i, s: (0, 0)),
            ),
        ),
        out_shape=(jax.ShapeDtypeStruct((count, rank_size, far * rank_size), bf16), TICK),
        compiler_params=pltpu.CompilerParams(vmem_limit_bytes=30 * MIB),
        cost_estimate=pl.CostEstimate(
            flops=pairs * 20, bytes_accessed=10**6, transcendentals=0
        ),
        name="far_kernels",
    )(lists, targets, rows, *after)


APPLY_STEP = 4


def apply_body(list_ref, kernel_ref, weights_ref, _, out_ref):
    far = list_ref.shape[1]
    for n in range(APPLY_STEP):
        leaf = pl.program_id(0) * APPLY_STEP + n
        weights = jnp.concatenate([weights_ref[list_ref[leaf, q]] for q in range(far)], axis=1)
        out_ref[n] = mm(kernel_ref[n], weights, NT)


def far_sums(lists, kernels, weights, after):
    count, rank_size, wide = kernels.shape
    cols = weights.shape[1]
    return pl.pallas_call(
        apply_body,
        grid_spec=pltpu.PrefetchScalarGridSpec(
            num_scalar_prefetch=1,
            grid=(count // APPLY_STEP,),
            in_specs=[
                pl.BlockSpec((APPLY_STEP, rank_size, wide), lambda i, s: (i, 0, 0)),
                pl.BlockSpec(weights.shape, lambda i, s: (0, 0, 0)),
                pl.BlockSpec(memory_space=pl.ANY),
            ],
            out_specs=pl.BlockSpec((APPLY_STEP, rank_size, cols), lambda i, s: (i, 0, 0)),
        ),
        out_shape=jax.ShapeDtypeStruct((count, rank_size, cols), f32),
        compiler_params=pltpu.CompilerParams(vmem_limit_bytes=28 * MIB),
        cost_estimate=pl.CostEstimate(
            flops=count * wide * rank_size * 1000, bytes_accessed=20 * 10**6, transcendentals=0
        ),
        name="far_sums",
    )(lists, kernels, weights, after)


def fused_body(first, list_ref, target_ref, rows_ref, weights_ref, after_ref, out_ref, tick_ref, even, odd):
    tick_ref[...] = jnp.zeros_like(tick_ref)
    count = out_ref.shape[0]
    rank_size = weights_ref.shape[2]
    far = list_ref.shape[1]
    batch = 4

    def listed(ref, i, q, n):
        return jnp.concatenate([ref[list_ref[i, q + k]] for k in range(n)], axis=1)

    def fill(n, kernel):
        i = first + n
        target = target_rows(*f32_halves(target_ref[i]))
        for q in range(0, far, batch):
            kernel[:, q * rank_size : (q + batch) * rank_size] = matern(
                mm(target, listed(rows_ref, i, q, batch))
            )

    def apply(n, kernel):
        out_ref[n] = mm(kernel[...], listed(weights_ref, first + n, 0, far), NT)

    fill(0, even)

    def two(n, carry):
        fill(2 * n + 1, odd)
        apply(2 * n, even)
        fill(jnp.minimum(2 * n + 2, count - 1), even)
        apply(2 * n + 1, odd)
        return carry

    lax.fori_loop(0, count // 2, two, 0)


def fused_sums(first, count, lists, targets, rows, weights, after):
    far = lists.shape[1]
    cols, rank_size = weights.shape[1:]
    whole = pl.BlockSpec(memory_space=pltpu.VMEM)
    pairs = count * far * rank_size * rank_size
    return pl.pallas_call(
        functools.partial(fused_body, first),
        in_specs=[pl.BlockSpec(memory_space=pltpu.SMEM), whole, whole, whole]
        + [pl.BlockSpec(memory_space=pl.ANY)],
        out_specs=(whole, whole),
        out_shape=(jax.ShapeDtypeStruct((count, rank_size, cols), f32), TICK),
        scratch_shapes=[pltpu.VMEM((rank_size, far * rank_size), bf16)] * 2,
        compiler_params=pltpu.CompilerParams(vmem_limit_bytes=24 * MIB),
        cost_estimate=pl.CostEstimate(
            flops=pairs * 2500, bytes_accessed=12 * 10**6, transcendentals=2 * pairs
        ),
        name="fused_sums",
    )(lists, targets, rows, weights, after)


def upper_body(list_ref, own_ref, chip_ref, across_ref, after_ref, out_ref, every_ref):
    dims, rank_size = own_ref.shape[1:]
    cols = out_ref.shape[2]
    batch = 4
    half = chip_ref.shape[0]

    def fetch(k, carry):
        far = list_ref.shape[1]
        place = list_ref[k // far, k % far]

        @pl.when(place < half)
        def _():
            every_ref[k] = chip_ref[jnp.minimum(place, half - 1)]

        @pl.when(place >= half)
        def _():
            every_ref[k] = across_ref[jnp.maximum(place - half, 0)]

        return carry

    lax.fori_loop(0, every_ref.shape[0], fetch, 0)
    for c in range(own_ref.shape[0]):
        target = target_rows(*scaled_halves(own_ref[c]))
        total = jnp.zeros((rank_size, cols), f32)
        for q in range(0, list_ref.shape[1], batch):
            blocks = [every_ref[c * list_ref.shape[1] + q + k] for k in range(batch)]
            values = jnp.concatenate([x[:cols] for x in blocks], axis=1)
            points = jnp.concatenate([x[cols:].astype(f32)[:dims] for x in blocks], axis=1)
            kernel = matern(mm(target, source_rows(*scaled_halves(points))))
            total += mm(kernel, values, NT)
        out_ref[c] = total


def upper_sums(lists, own, chip, across, after):
    count, dims, rank_size = own.shape
    cols = chip.shape[1] - 2 * dims
    whole = pl.BlockSpec(memory_space=pltpu.VMEM)
    pairs = count * lists.shape[1] * rank_size * rank_size
    return pl.pallas_call(
        upper_body,
        in_specs=[pl.BlockSpec(memory_space=pltpu.SMEM), whole, whole, whole]
        + [pl.BlockSpec(memory_space=pl.ANY)],
        out_specs=whole,
        out_shape=jax.ShapeDtypeStruct((count, rank_size, cols), f32),
        scratch_shapes=[pltpu.VMEM((count * lists.shape[1],) + chip.shape[1:], bf16)],
        compiler_params=pltpu.CompilerParams(vmem_limit_bytes=16 * MIB),
        cost_estimate=pl.CostEstimate(
            flops=pairs * 230, bytes_accessed=8 * 10**6, transcendentals=2 * pairs
        ),
        name="upper_sums",
    )(lists, own, chip, across, after)


def final_body(first_ref, second_ref, upper_ref, transfer_ref, basis_ref, near_ref, out_ref):
    leaf_size = basis_ref.shape[1]
    step = 4
    for part, far_ref in enumerate((first_ref, second_ref)):
        count = far_ref.shape[0]

        def leaves(n, carry, far_ref=far_ref, start=part * count):
            upper = upper_ref[(start + n * step) // KIDS]
            for k in range(step):
                i = start + n * step + k
                skeleton = far_ref[n * step + k] + mm3(transfer_ref[i], upper)
                potential = mm3(basis_ref[i], skeleton) + near_ref[i]
                at = pl.ds(pl.multiple_of(i * leaf_size, leaf_size), leaf_size)
                out_ref[:, at] = jnp.transpose(potential)
            return carry

        lax.fori_loop(0, count // step, leaves, 0)


def final(first, second, upper, transfer, basis, near):
    leaf_count, leaf_size, rank_size = basis.shape
    cols = near.shape[2]
    whole = pl.BlockSpec(memory_space=pltpu.VMEM)
    return pl.pallas_call(
        final_body,
        in_specs=[whole] * 6,
        out_specs=whole,
        out_shape=jax.ShapeDtypeStruct((cols, leaf_count * leaf_size), f32),
        compiler_params=pltpu.CompilerParams(vmem_limit_bytes=20 * MIB),
        cost_estimate=pl.CostEstimate(flops=10**9, bytes_accessed=10**7, transcendentals=0),
        name="final",
    )(first, second, upper, transfer, basis, near)


def shifted(block, axis, move, count):
    return lax.ppermute(block, axis, [(i, move(i)) for i in range(count)])


def upper_places(clusters, count):
    owner = clusters // count
    group = owner % 16
    bulk = owner // 16
    mine = lax.axis_index("bulk")
    core = (bulk ^ mine) & 1
    hops = (bulk // 2 - mine // 2) & 3
    turn = jnp.where(hops == 3, 1, jnp.where(hops == 0, 0, hops + 1))
    return (((core * 4 + turn) * 16) + group) * count + clusters % count


def local(
    points,
    weights,
    leaf_order,
    basis,
    transfer,
    skel_leaf,
    skel_upper,
    near_list,
    leaf_interaction_list,
    far_upper,
):
    row_count = leaf_order.shape[0]
    group_count = lax.axis_size("group")
    bulk_count = lax.axis_size("bulk")
    device_count = group_count * bulk_count
    leaf_count = basis.shape[0]

    scaled = skel_leaf.astype(f32) * POINT_SCALE
    subtree_points = lax.all_gather(scaled, "group", axis=0, tiled=True)
    want, src, rank = index_lists(leaf_order, group_count, basis.shape[1])
    wanted = lax.all_to_all(want, "group", split_axis=0, concat_axis=0, tiled=True)
    picked = pick(wanted, pick_table(points, weights), row_count)
    arrived = lax.all_to_all(picked, "group", split_axis=0, concat_axis=0, tiled=True)

    far_local = leaf_interaction_list - lax.axis_index("bulk") * (group_count * leaf_count)

    own = place(src, rank, arrived)
    skel_wb, upper_wb = skeleton(own, basis, transfer)
    sub_w = lax.all_gather(skel_wb, "group", axis=0, tiled=True)
    forward = [(i, i + 1) for i in range(device_count - 1)]
    backward = [(i + 1, i) for i in range(device_count - 1)]
    low = lax.ppermute(own, ("bulk", "group"), forward)
    high = lax.ppermute(own, ("bulk", "group"), backward)

    def joined(tick, *blocks):
        return jnp.concatenate(blocks, axis=0) + tick[0].astype(bf16)

    def ahead(block):
        return shifted(block, "bulk", lambda i: (i + 2) % bulk_count, bulk_count)

    def back(block):
        return shifted(block, "bulk", lambda i: (i - 2) % bulk_count, bulk_count)

    mine = jnp.concatenate([upper_wb, skel_upper, jnp.zeros(skel_upper.shape, bf16)], axis=1)
    copies = jnp.tile(mine, (group_count, 1, 1))
    block = lax.all_to_all(copies, "group", split_axis=0, concat_axis=0, tiled=True)
    part = leaf_count // 2
    source_points = far_rows(subtree_points)
    kernels, tick = far_kernels(0, part, far_local, scaled, source_points, copies)
    block = joined(tick, block)
    from_low, from_high = ahead(block), back(block)
    device = lax.axis_index(("bulk", "group"))
    near, tick = near_sums(near_list - (device - 1) * leaf_count, low, own, high, block)
    half = block.shape[0] // 2
    first = joined(tick, from_low[:half])
    second = joined(tick, from_high[half:])
    far_first, far_second = ahead(first), back(second)
    far_late, tick = fused_sums(part, part, far_local, scaled, source_points, sub_w, first)
    chip = jnp.concatenate([block, from_low, from_high, joined(tick, far_first, far_second)], axis=0)
    other = shifted(chip, "bulk", lambda i: i ^ 1, bulk_count)
    far_early = far_sums(far_local, kernels, sub_w, chip)
    upper = upper_sums(upper_places(far_upper, skel_upper.shape[0]), skel_upper, chip, other, far_early)
    return final(far_early, far_late, upper, transfer, basis, near)


def solution(mesh):
    placed = (
        P(None, ("bulk", "group")),
        P(None, ("bulk", "group")),
        P(("bulk", "group")),
        P(("bulk", "group"), None, None),
        P(("bulk", "group"), None, None),
        P(("bulk", "group"), None, None),
        P(("bulk", "group"), None, None),
        P(("bulk", "group"), None),
        P(("bulk", "group"), None),
        P(("bulk", "group"), None),
    )
    return jax.shard_map(
        local, mesh=mesh, in_specs=placed, out_specs=P(None, ("bulk", "group")), check_vma=False
    )
```

```python
import functools
import math

import jax
import jax.numpy as jnp
from jax import lax
from jax.experimental import pallas as pl
from jax.experimental.pallas import tpu as pltpu
from jax.sharding import PartitionSpec as P

KIDS = 8

POINT_SCALE = math.sqrt(5.0) / 2.0 / math.log(2.0)
POLY_A = 3.0 / math.log(2.0)
POLY_B = 3.0 / math.log(2.0) ** 2
POLY_LOG = math.log2(math.log(2.0) ** 2 / 3.0)
AUG = 48
MIB = 1024 * 1024

f32 = jnp.float32
bf16 = jnp.bfloat16
TICK = jax.ShapeDtypeStruct((8, 128), f32)
NN = (((1,), (0,)), ((), ()))
NT = (((1,), (1,)), ((), ()))


def mm(a, b, dims=NN):
    return lax.dot_general(a, b, dims, preferred_element_type=f32)


def halves(x):
    high = x.astype(bf16)
    return high, (x - high.astype(f32)).astype(bf16)


def mm3(a, b):
    a_high, a_low = halves(a)
    b_high, b_low = halves(b)
    return mm(a_high, b_high) + (mm(a_high, b_low) + mm(a_low, b_high))


def squares(high, low):
    x = high + low
    norm = jnp.sum(x * x, axis=0, keepdims=True)
    first = norm.astype(bf16).astype(f32)
    second = (norm - first).astype(bf16).astype(f32)
    third = norm - first - second
    row = lax.broadcasted_iota(jnp.int32, high.shape, 0)
    parts = jnp.where(row % 3 == 0, first, jnp.where(row % 3 == 1, second, third))
    return row, parts


def source_rows(high, low):
    row, parts = squares(high, low)
    last = jnp.where(row < 3, 1.0, jnp.where(row < 6, parts, 0.0))
    high, low = -2.0 * high, -2.0 * low
    return jnp.concatenate([high, low, high, low, last, jnp.zeros_like(last)], axis=0).astype(bf16)


def target_rows(high, low):
    row, parts = squares(high, low)
    last = jnp.where(row < 3, parts, jnp.where(row < 6, 1.0, 0.0))
    rows = jnp.concatenate([high, high, low, low, last, jnp.zeros_like(last)], axis=0)
    return jnp.transpose(rows).astype(bf16)


def f32_halves(points):
    high, low = halves(points)
    return high.astype(f32), low.astype(f32)


def scaled_halves(points):
    return f32_halves(points.astype(f32) * POINT_SCALE)


def matern(square):
    square = jnp.maximum(square, 1e-30)
    t = square * lax.rsqrt(square)
    return (((t + POLY_A) * t + POLY_B) * jnp.exp2(POLY_LOG - t)).astype(bf16)


def index_body(order_ref, want_ref, src_ref, rank_ref, tick_ref):
    tick_ref[...] = jnp.zeros_like(tick_ref)
    group_count, _, pair = want_ref.shape
    lines = order_ref.shape[0]
    row_count = group_count * pair
    order = order_ref[...]
    owner = ((order.astype(f32) + 0.5) * (1.0 / row_count)).astype(jnp.int32)
    src = owner % group_count
    row = order - owner * row_count
    before = (
        lax.broadcasted_iota(jnp.int32, (128, 128), 0)
        < lax.broadcasted_iota(jnp.int32, (128, 128), 1)
    ).astype(f32).astype(bf16)
    above = (
        lax.broadcasted_iota(jnp.int32, (lines, lines), 1)
        < lax.broadcasted_iota(jnp.int32, (lines, lines), 0)
    ).astype(f32).astype(bf16)
    all_ones = jnp.ones((128, 128), bf16)
    rank = jnp.zeros(src.shape, f32)
    for g in range(group_count):
        here = src == g
        mask = here.astype(f32).astype(bf16)
        total = mm(mask, all_ones).astype(bf16)
        rank = jnp.where(here, mm(mask, before) + mm(above, total), rank)
    rank = rank.astype(jnp.int32)
    for i in range(lines // 2):
        for ref, x in ((src_ref, src), (rank_ref, rank)):
            ref[i] = jnp.concatenate([x[2 * i : 2 * i + 1], x[2 * i + 1 : 2 * i + 2]], axis=1)
    place = lax.broadcasted_iota(jnp.int32, (pair, 256), 0)
    owner = lax.broadcasted_iota(jnp.int32, (group_count, 256), 0)
    total = jnp.zeros((2 * group_count, pair), f32)
    for k in range(0, lines, 2):
        line = lambda x: jnp.concatenate([x[k : k + 1], x[k + 1 : k + 2]], axis=1)
        rank_line, src_line, row_line = line(rank), line(src), line(row)
        spots = (place == rank_line).astype(f32).astype(bf16)
        mine = owner == src_line
        high = jnp.where(mine, (row_line >> 7).astype(f32), 0.0)
        low = jnp.where(mine, (row_line & 127).astype(f32), 0.0)
        total += mm(jnp.concatenate([high, low], axis=0).astype(bf16), spots, NT)
    want = (total[:group_count] * 128.0 + total[group_count:]).astype(jnp.int32)
    for g in range(group_count):
        want_ref[g] = want[g : g + 1]


def index_lists(order, group_count, leaf_size):
    row_count = order.shape[0]
    assert leaf_size == 256
    return pl.pallas_call(
        index_body,
        out_shape=(
            jax.ShapeDtypeStruct((group_count, 1, row_count // group_count), jnp.int32),
            jax.ShapeDtypeStruct((row_count // leaf_size, 1, leaf_size), jnp.int32),
            jax.ShapeDtypeStruct((row_count // leaf_size, 1, leaf_size), jnp.int32),
            TICK,
        ),
        compiler_params=pltpu.CompilerParams(vmem_limit_bytes=8 * MIB),
        cost_estimate=pl.CostEstimate(flops=2 * 10**9, bytes_accessed=10**5, transcendentals=0),
        name="index_lists",
    )(order.reshape(-1, 128))


def table_body(points_ref, weights_ref, table_ref):
    height = weights_ref.shape[0] + 2 * points_ref.shape[0]
    for h in range(points_ref.shape[1] // 256):
        at = slice(h * 256, (h + 1) * 256)
        high, low = scaled_halves(points_ref[:, at])
        table_ref[h * height : (h + 1) * height, :] = jnp.concatenate(
            [weights_ref[:, at], high, low], axis=0
        ).astype(bf16)


def pick_table(points, weights):
    height = weights.shape[0] + 2 * points.shape[0]
    whole = pl.BlockSpec(memory_space=pltpu.VMEM)
    return pl.pallas_call(
        table_body,
        in_specs=[whole, whole],
        out_specs=whole,
        out_shape=jax.ShapeDtypeStruct((points.shape[1] // 256 * height, 256), bf16),
        compiler_params=pltpu.CompilerParams(vmem_limit_bytes=10 * MIB),
        cost_estimate=pl.CostEstimate(flops=3 * 10**9, bytes_accessed=3 * 10**6, transcendentals=0),
        name="pick_table",
    )(points, weights)


def pick_body(want_ref, table_ref, out_ref):
    group_count, height, pair = out_ref.shape
    high_count = table_ref.shape[0] // height
    batch = 4

    def device(d, carry):
        want = want_ref[d]
        low = want & 255
        high = want >> 8
        spots = (lax.broadcasted_iota(jnp.int32, (256, pair), 0) == low).astype(f32).astype(bf16)
        picked = jnp.zeros((height, pair), f32)
        for h in range(0, high_count, batch):
            found = mm(table_ref[h * height : (h + batch) * height, :], spots)
            for k in range(batch):
                picked = jnp.where(high == h + k, found[k * height : (k + 1) * height], picked)
        out_ref[d] = picked.astype(bf16)
        return carry

    lax.fori_loop(0, group_count, device, 0)


def pick(want, table, row_count):
    group_count, _, pair = want.shape
    height = table.shape[0] * 256 // row_count
    whole = pl.BlockSpec(memory_space=pltpu.VMEM)
    return pl.pallas_call(
        pick_body,
        in_specs=[whole, whole],
        out_specs=whole,
        out_shape=jax.ShapeDtypeStruct((group_count, height, pair), bf16),
        compiler_params=pltpu.CompilerParams(vmem_limit_bytes=14 * MIB),
        cost_estimate=pl.CostEstimate(flops=6 * 10**9, bytes_accessed=3 * 10**6, transcendentals=0),
        name="pick",
    )(want, table)


def place_body(src_ref, rank_ref, arrived_ref, leaf_ref):
    leaf_count, height, leaf_size = leaf_ref.shape
    pair = arrived_ref.shape[1]
    group_count = arrived_ref.shape[0] // height
    batch = 4
    step = 4

    def leaves(c, carry):
        for n in range(step):
            i = c * step + n
            src = src_ref[i]
            spots = (
                lax.broadcasted_iota(jnp.int32, (pair, leaf_size), 0) == rank_ref[i]
            ).astype(f32).astype(bf16)
            placed = jnp.zeros((height, leaf_size), f32)
            for g in range(0, group_count, batch):
                found = mm(arrived_ref[g * height : (g + batch) * height, :], spots)
                for k in range(batch):
                    placed = jnp.where(src == g + k, found[k * height : (k + 1) * height], placed)
            leaf_ref[i] = placed.astype(bf16)
        return carry

    lax.fori_loop(0, leaf_count // step, leaves, 0)


def place(src, rank, arrived):
    group_count, height, pair = arrived.shape
    leaf_count, _, leaf_size = src.shape
    whole = pl.BlockSpec(memory_space=pltpu.VMEM)
    return pl.pallas_call(
        place_body,
        in_specs=[whole] * 3,
        out_specs=whole,
        out_shape=jax.ShapeDtypeStruct((leaf_count, height, leaf_size), bf16),
        compiler_params=pltpu.CompilerParams(vmem_limit_bytes=12 * MIB),
        cost_estimate=pl.CostEstimate(flops=8 * 10**9, bytes_accessed=2 * 10**6, transcendentals=0),
        name="place",
    )(src, rank, arrived.reshape(group_count * height, pair))


def skeleton_body(leaf_ref, basis_ref, transfer_ref, skel_ref, upper_ref):
    leaf_count, cols, _ = skel_ref.shape

    def cluster(c, carry):
        total = jnp.zeros(upper_ref.shape[1:], f32)
        for n in range(KIDS):
            i = c * KIDS + n
            values = leaf_ref[i, :cols]
            basis_high, basis_low = halves(basis_ref[i])
            skel = mm(values, basis_high) + mm(values, basis_low)
            skel_ref[i] = skel.astype(bf16)
            total += mm3(skel, transfer_ref[i])
        upper_ref[c] = total.astype(bf16)
        return carry

    lax.fori_loop(0, leaf_count // KIDS, cluster, 0)


def skeleton(leaves, basis, transfer):
    leaf_count, _, rank_size = basis.shape
    cols = leaves.shape[1] - 16
    whole = pl.BlockSpec(memory_space=pltpu.VMEM)
    return pl.pallas_call(
        skeleton_body,
        in_specs=[whole] * 3,
        out_specs=(whole, whole),
        out_shape=(
            jax.ShapeDtypeStruct((leaf_count, cols, rank_size), bf16),
            jax.ShapeDtypeStruct((leaf_count // KIDS, cols, rank_size), bf16),
        ),
        compiler_params=pltpu.CompilerParams(vmem_limit_bytes=14 * MIB),
        cost_estimate=pl.CostEstimate(flops=10**9, bytes_accessed=7 * 10**6, transcendentals=0),
        name="skeleton",
    )(leaves, basis, transfer)


def near_body(list_ref, low_ref, own_ref, high_ref, after_ref, out_ref, tick_ref, rows, values):
    tick_ref[...] = jnp.zeros_like(tick_ref)
    leaf_count, height, leaf_size = own_ref.shape
    cols = height - 16
    for part, ref in enumerate((low_ref, own_ref, high_ref)):

        def fill(n, carry, part=part, ref=ref):
            values[part * leaf_count + n] = ref[n, :cols]
            tail = ref[n, cols:].astype(f32)
            rows[part * leaf_count + n] = source_rows(tail[:8], tail[8:])
            return carry

        lax.fori_loop(0, leaf_count, fill, 0)

    def leaf(i, carry):
        tail = own_ref[i, cols:].astype(f32)
        target = target_rows(tail[:8], tail[8:])
        total = jnp.zeros((leaf_size, cols), f32)
        for q in range(list_ref.shape[1]):
            j = list_ref[i, q]
            total += mm(matern(mm(target, rows[j])), values[j], NT)
        out_ref[i] = total
        return carry

    lax.fori_loop(0, leaf_count, leaf, 0)


def near_sums(lists, low, own, high, after):
    leaf_count, near = lists.shape
    height, leaf_size = own.shape[1:]
    cols = height - 16
    whole = pl.BlockSpec(memory_space=pltpu.VMEM)
    pairs = leaf_count * near * leaf_size * leaf_size
    return pl.pallas_call(
        near_body,
        in_specs=[pl.BlockSpec(memory_space=pltpu.SMEM), whole, whole, whole]
        + [pl.BlockSpec(memory_space=pl.ANY)],
        out_specs=(whole, whole),
        out_shape=(jax.ShapeDtypeStruct((leaf_count, leaf_size, cols), f32), TICK),
        scratch_shapes=[
            pltpu.VMEM((3 * leaf_count, AUG, leaf_size), bf16),
            pltpu.VMEM((3 * leaf_count, cols, leaf_size), bf16),
        ],
        compiler_params=pltpu.CompilerParams(vmem_limit_bytes=20 * MIB),
        cost_estimate=pl.CostEstimate(
            flops=pairs * 2500, bytes_accessed=6 * 10**6, transcendentals=2 * pairs
        ),
        name="near_sums",
    )(lists, low, own, high, after)


def far_rows_body(points_ref, rows_ref):
    step = 8

    def fill(n, carry):
        for k in range(step):
            rows_ref[n * step + k] = source_rows(*f32_halves(points_ref[n * step + k]))
        return carry

    lax.fori_loop(0, points_ref.shape[0] // step, fill, 0)


def far_rows(points):
    count, _, rank_size = points.shape
    whole = pl.BlockSpec(memory_space=pltpu.VMEM)
    return pl.pallas_call(
        far_rows_body,
        in_specs=[whole],
        out_specs=whole,
        out_shape=jax.ShapeDtypeStruct((count, AUG, rank_size), bf16),
        compiler_params=pltpu.CompilerParams(vmem_limit_bytes=14 * MIB),
        cost_estimate=pl.CostEstimate(flops=10**8, bytes_accessed=10**6, transcendentals=0),
        name="far_rows",
    )(points)


FAR_STEP = 4


def far_body(first, after_count, list_ref, target_ref, rows_ref, *refs):
    out_ref, tick_ref = refs[after_count:]
    rank_size = rows_ref.shape[2]
    far = list_ref.shape[1]
    batch = 4
    for n in range(FAR_STEP):
        i = first + pl.program_id(0) * FAR_STEP + n
        target = target_rows(*f32_halves(target_ref[i]))
        for q in range(0, far, batch):
            rows = jnp.concatenate([rows_ref[list_ref[i, q + k]] for k in range(batch)], axis=1)
            out_ref[n, :, q * rank_size : (q + batch) * rank_size] = matern(mm(target, rows))
    tick_ref[...] = jnp.zeros_like(tick_ref)


def far_kernels(first, count, lists, targets, rows, *after):
    far = lists.shape[1]
    rank_size = rows.shape[2]
    pairs = count * far * rank_size * rank_size
    anywhere = pl.BlockSpec(memory_space=pl.ANY)
    return pl.pallas_call(
        functools.partial(far_body, first, len(after)),
        grid_spec=pltpu.PrefetchScalarGridSpec(
            num_scalar_prefetch=1,
            grid=(count // FAR_STEP,),
            in_specs=[
                pl.BlockSpec(targets.shape, lambda i, s: (0, 0, 0)),
                pl.BlockSpec(rows.shape, lambda i, s: (0, 0, 0)),
            ]
            + [anywhere] * len(after),
            out_specs=(
                pl.BlockSpec((FAR_STEP, rank_size, far * rank_size), lambda i, s: (i, 0, 0)),
                pl.BlockSpec(TICK.shape, lambda i, s: (0, 0)),
            ),
        ),
        out_shape=(jax.ShapeDtypeStruct((count, rank_size, far * rank_size), bf16), TICK),
        compiler_params=pltpu.CompilerParams(vmem_limit_bytes=30 * MIB),
        cost_estimate=pl.CostEstimate(
            flops=pairs * 20, bytes_accessed=10**6, transcendentals=0
        ),
        name="far_kernels",
    )(lists, targets, rows, *after)


STREAM_STEP = 4


def far_sums_body(list_ref, target_ref, rows_ref, weights_ref, stored_ref, after_ref, out_ref, even, odd, stream, sems):
    early = stored_ref.shape[0]
    late = out_ref.shape[0] - early
    rank_size = weights_ref.shape[2]
    far = list_ref.shape[1]
    batch = 4
    blocks = early // STREAM_STEP
    copies = [
        pltpu.make_async_copy(
            stored_ref.at[pl.ds(k * STREAM_STEP, STREAM_STEP)], stream.at[k % 2], sems.at[k % 2]
        )
        for k in range(blocks)
    ]

    def listed(ref, i, q, n):
        return jnp.concatenate([ref[list_ref[i, q + k]] for k in range(n)], axis=1)

    def fill(i, kernel):
        target = target_rows(*f32_halves(target_ref[i]))
        for q in range(0, far, batch):
            kernel[:, q * rank_size : (q + batch) * rank_size] = matern(
                mm(target, listed(rows_ref, i, q, batch))
            )

    def apply(i, kernel):
        out_ref[i] = mm(kernel, listed(weights_ref, i, 0, far), NT)

    for copy in copies[:2]:
        copy.start()
    fill(early, even)

    def two(n, carry):
        i = early + 2 * n
        fill(i + 1, odd)
        apply(i, even[...])
        fill(jnp.minimum(i + 2, early + late - 1), even)
        apply(i + 1, odd[...])
        return carry

    lax.fori_loop(0, late // 2, two, 0)
    for k, copy in enumerate(copies):
        copy.wait()
        for n in range(STREAM_STEP):
            apply(k * STREAM_STEP + n, stream[k % 2, n])
        if k + 2 < blocks:
            copies[k + 2].start()


def far_sums(lists, targets, rows, weights, stored, after):
    count, far = lists.shape
    cols, rank_size = weights.shape[1:]
    whole = pl.BlockSpec(memory_space=pltpu.VMEM)
    anywhere = pl.BlockSpec(memory_space=pl.ANY)
    pairs = count * far * rank_size * rank_size
    return pl.pallas_call(
        far_sums_body,
        in_specs=[pl.BlockSpec(memory_space=pltpu.SMEM), whole, whole, whole, anywhere, anywhere],
        out_specs=whole,
        out_shape=jax.ShapeDtypeStruct((count, rank_size, cols), f32),
        scratch_shapes=[pltpu.VMEM((rank_size, far * rank_size), bf16)] * 2
        + [
            pltpu.VMEM((2, STREAM_STEP, rank_size, far * rank_size), bf16),
            pltpu.SemaphoreType.DMA((2,)),
        ],
        compiler_params=pltpu.CompilerParams(vmem_limit_bytes=32 * MIB),
        cost_estimate=pl.CostEstimate(
            flops=pairs * 2500, bytes_accessed=24 * 10**6, transcendentals=2 * pairs
        ),
        name="far_sums",
    )(lists, targets, rows, weights, stored, after)


def upper_body(list_ref, own_ref, chip_ref, across_ref, after_ref, out_ref):
    dims, rank_size = own_ref.shape[1:]
    cols = out_ref.shape[2]
    batch = 4
    half = chip_ref.shape[0]

    def block_of(place):
        here = chip_ref[jnp.minimum(place, half - 1)]
        there = across_ref[jnp.maximum(place - half, 0)]
        return jnp.where(place < half, here, there)

    for c in range(own_ref.shape[0]):
        target = target_rows(*scaled_halves(own_ref[c]))
        total = jnp.zeros((rank_size, cols), f32)
        for q in range(0, list_ref.shape[1], batch):
            blocks = [block_of(list_ref[c, q + k]) for k in range(batch)]
            values = jnp.concatenate([x[:cols] for x in blocks], axis=1)
            points = jnp.concatenate([x[cols:].astype(f32)[:dims] for x in blocks], axis=1)
            kernel = matern(mm(target, source_rows(*scaled_halves(points))))
            total += mm(kernel, values, NT)
        out_ref[c] = total


def upper_sums(lists, own, chip, across, after):
    count, dims, rank_size = own.shape
    cols = chip.shape[1] - 2 * dims
    whole = pl.BlockSpec(memory_space=pltpu.VMEM)
    pairs = count * lists.shape[1] * rank_size * rank_size
    return pl.pallas_call(
        upper_body,
        in_specs=[pl.BlockSpec(memory_space=pltpu.SMEM), whole, whole, whole]
        + [pl.BlockSpec(memory_space=pl.ANY)],
        out_specs=whole,
        out_shape=jax.ShapeDtypeStruct((count, rank_size, cols), f32),
        compiler_params=pltpu.CompilerParams(vmem_limit_bytes=16 * MIB),
        cost_estimate=pl.CostEstimate(
            flops=pairs * 230, bytes_accessed=8 * 10**6, transcendentals=2 * pairs
        ),
        name="upper_sums",
    )(lists, own, chip, across, after)


def final_body(far_ref, upper_ref, transfer_ref, basis_ref, near_ref, out_ref):
    leaf_count, leaf_size, _ = basis_ref.shape
    step = 4

    def leaves(n, carry):
        upper = upper_ref[n * step // KIDS]
        for k in range(step):
            i = n * step + k
            skeleton = far_ref[i] + mm3(transfer_ref[i], upper)
            potential = mm3(basis_ref[i], skeleton) + near_ref[i]
            at = pl.ds(pl.multiple_of(i * leaf_size, leaf_size), leaf_size)
            out_ref[:, at] = jnp.transpose(potential)
        return carry

    lax.fori_loop(0, leaf_count // step, leaves, 0)


def final(far, upper, transfer, basis, near):
    leaf_count, leaf_size, rank_size = basis.shape
    cols = near.shape[2]
    whole = pl.BlockSpec(memory_space=pltpu.VMEM)
    return pl.pallas_call(
        final_body,
        in_specs=[whole] * 5,
        out_specs=whole,
        out_shape=jax.ShapeDtypeStruct((cols, leaf_count * leaf_size), f32),
        compiler_params=pltpu.CompilerParams(vmem_limit_bytes=20 * MIB),
        cost_estimate=pl.CostEstimate(flops=10**9, bytes_accessed=10**7, transcendentals=0),
        name="final",
    )(far, upper, transfer, basis, near)


def shifted(block, axis, move, count):
    return lax.ppermute(block, axis, [(i, move(i)) for i in range(count)])


def upper_places(clusters, count):
    owner = clusters // count
    group = owner % 16
    bulk = owner // 16
    mine = lax.axis_index("bulk")
    core = (bulk ^ mine) & 1
    hops = (bulk // 2 - mine // 2) & 3
    turn = hops
    return (((core * 4 + turn) * 16) + group) * count + clusters % count


def local(
    points,
    weights,
    leaf_order,
    basis,
    transfer,
    skel_leaf,
    skel_upper,
    near_list,
    leaf_interaction_list,
    far_upper,
):
    row_count = leaf_order.shape[0]
    group_count = lax.axis_size("group")
    bulk_count = lax.axis_size("bulk")
    device_count = group_count * bulk_count
    leaf_count = basis.shape[0]

    want, src, rank, tick = index_lists(leaf_order, group_count, basis.shape[1])
    scaled = skel_leaf.astype(f32) * POINT_SCALE + tick[0]
    subtree_points = lax.all_gather(scaled, "group", axis=0, tiled=True)
    wanted = lax.all_to_all(want, "group", split_axis=0, concat_axis=0, tiled=True)
    picked = pick(wanted, pick_table(points, weights), row_count)
    arrived = lax.all_to_all(picked, "group", split_axis=0, concat_axis=0, tiled=True)

    far_local = leaf_interaction_list - lax.axis_index("bulk") * (group_count * leaf_count)

    own = place(src, rank, arrived)
    skel_wb, upper_wb = skeleton(own, basis, transfer)
    sub_w = lax.all_gather(skel_wb, "group", axis=0, tiled=True)
    forward = [(i, i + 1) for i in range(device_count - 1)]
    backward = [(i + 1, i) for i in range(device_count - 1)]
    low = lax.ppermute(own, ("bulk", "group"), forward)
    high = lax.ppermute(own, ("bulk", "group"), backward)

    def joined(tick, *blocks):
        return jnp.concatenate(blocks, axis=0) + tick[0].astype(bf16)

    mine = jnp.concatenate([upper_wb, skel_upper, jnp.zeros(skel_upper.shape, bf16)], axis=1)
    copies = jnp.tile(mine, (group_count, 1, 1))
    block = lax.all_to_all(copies, "group", split_axis=0, concat_axis=0, tiled=True)
    part = leaf_count // 2
    source_points = far_rows(subtree_points)
    kernels, tick = far_kernels(0, part, far_local, scaled, source_points, copies)
    block = joined(tick, block)
    ring = [shifted(block, "bulk", lambda i, hops=hops: (i - 2 * hops) % bulk_count, bulk_count) for hops in (1, 2, 3)]
    device = lax.axis_index(("bulk", "group"))
    near, tick = near_sums(near_list - (device - 1) * leaf_count, low, own, high, block)
    chip = joined(tick, block, *ring)
    other = shifted(chip, "bulk", lambda i: i ^ 1, bulk_count)
    far = far_sums(far_local, scaled, source_points, sub_w, kernels, chip)
    upper = upper_sums(upper_places(far_upper, skel_upper.shape[0]), skel_upper, chip, other, far)
    return final(far, upper, transfer, basis, near)


def solution(mesh):
    placed = (
        P(None, ("bulk", "group")),
        P(None, ("bulk", "group")),
        P(("bulk", "group")),
        P(("bulk", "group"), None, None),
        P(("bulk", "group"), None, None),
        P(("bulk", "group"), None, None),
        P(("bulk", "group"), None, None),
        P(("bulk", "group"), None),
        P(("bulk", "group"), None),
        P(("bulk", "group"), None),
    )
    return jax.shard_map(
        local, mesh=mesh, in_specs=placed, out_specs=P(None, ("bulk", "group")), check_vma=False
    )
```

```python
import functools
import math

import jax
import jax.numpy as jnp
from jax import lax
from jax.experimental import pallas as pl
from jax.experimental.pallas import tpu as pltpu
from jax.sharding import PartitionSpec as P

KIDS = 8

POINT_SCALE = math.sqrt(5.0) / 2.0 / math.log(2.0)
POLY_A = 3.0 / math.log(2.0)
POLY_B = 3.0 / math.log(2.0) ** 2
POLY_LOG = math.log2(math.log(2.0) ** 2 / 3.0)
AUG = 48
MIB = 1024 * 1024

f32 = jnp.float32
bf16 = jnp.bfloat16
TICK = jax.ShapeDtypeStruct((8, 128), f32)
NN = (((1,), (0,)), ((), ()))
NT = (((1,), (1,)), ((), ()))


def mm(a, b, dims=NN):
    return lax.dot_general(a, b, dims, preferred_element_type=f32)


def halves(x):
    high = x.astype(bf16)
    return high, (x - high.astype(f32)).astype(bf16)


def mm3(a, b):
    (a_high, a_low), (b_high, b_low) = a, b
    return mm(a_high, b_high) + (mm(a_high, b_low) + mm(a_low, b_high))


def squares(high, low):
    x = high + low
    norm = jnp.sum(x * x, axis=0, keepdims=True)
    first = norm.astype(bf16).astype(f32)
    second = (norm - first).astype(bf16).astype(f32)
    third = norm - first - second
    row = lax.broadcasted_iota(jnp.int32, high.shape, 0)
    parts = jnp.where(row % 3 == 0, first, jnp.where(row % 3 == 1, second, third))
    return row, parts


def source_rows(high, low):
    row, parts = squares(high, low)
    last = jnp.where(row < 3, 1.0, jnp.where(row < 6, parts, 0.0))
    high, low = -2.0 * high, -2.0 * low
    return jnp.concatenate([high, low, high, low, last, jnp.zeros_like(last)], axis=0).astype(bf16)


def target_rows(high, low):
    row, parts = squares(high, low)
    last = jnp.where(row < 3, parts, jnp.where(row < 6, 1.0, 0.0))
    rows = jnp.concatenate([high, high, low, low, last, jnp.zeros_like(last)], axis=0)
    return jnp.transpose(rows).astype(bf16)


def f32_halves(points):
    high, low = halves(points)
    return high.astype(f32), low.astype(f32)


def scaled_halves(points):
    return f32_halves(points.astype(f32) * POINT_SCALE)


def matern(square):
    square = jnp.maximum(square, 1e-30)
    t = square * lax.rsqrt(square)
    return (((t + POLY_A) * t + POLY_B) * jnp.exp2(POLY_LOG - t)).astype(bf16)


def index_body(order_ref, want_ref, src_ref, rank_ref, tick_ref):
    tick_ref[...] = jnp.zeros_like(tick_ref)
    group_count, _, pair = want_ref.shape
    lines = order_ref.shape[0]
    row_count = group_count * pair
    order = order_ref[...]
    owner = ((order.astype(f32) + 0.5) * (1.0 / row_count)).astype(jnp.int32)
    src = owner % group_count
    row = order - owner * row_count
    before = (
        lax.broadcasted_iota(jnp.int32, (128, 128), 0)
        < lax.broadcasted_iota(jnp.int32, (128, 128), 1)
    ).astype(f32).astype(bf16)
    above = (
        lax.broadcasted_iota(jnp.int32, (lines, lines), 1)
        < lax.broadcasted_iota(jnp.int32, (lines, lines), 0)
    ).astype(f32).astype(bf16)
    all_ones = jnp.ones((128, 128), bf16)
    rank = jnp.zeros(src.shape, f32)
    for g in range(group_count):
        here = src == g
        mask = here.astype(f32).astype(bf16)
        total = mm(mask, all_ones).astype(bf16)
        rank = jnp.where(here, mm(mask, before) + mm(above, total), rank)
    rank = rank.astype(jnp.int32)
    for i in range(lines // 2):
        for ref, x in ((src_ref, src), (rank_ref, rank)):
            ref[i] = jnp.concatenate([x[2 * i : 2 * i + 1], x[2 * i + 1 : 2 * i + 2]], axis=1)
    place = lax.broadcasted_iota(jnp.int32, (pair, 256), 0)
    owner = lax.broadcasted_iota(jnp.int32, (group_count, 256), 0)
    total = jnp.zeros((2 * group_count, pair), f32)
    for k in range(0, lines, 2):
        line = lambda x: jnp.concatenate([x[k : k + 1], x[k + 1 : k + 2]], axis=1)
        rank_line, src_line, row_line = line(rank), line(src), line(row)
        spots = (place == rank_line).astype(f32).astype(bf16)
        mine = owner == src_line
        high = jnp.where(mine, (row_line >> 7).astype(f32), 0.0)
        low = jnp.where(mine, (row_line & 127).astype(f32), 0.0)
        total += mm(jnp.concatenate([high, low], axis=0).astype(bf16), spots, NT)
    want = (total[:group_count] * 128.0 + total[group_count:]).astype(jnp.int32)
    for g in range(group_count):
        want_ref[g] = want[g : g + 1]


def index_lists(order, group_count, leaf_size):
    row_count = order.shape[0]
    assert leaf_size == 256
    return pl.pallas_call(
        index_body,
        out_shape=(
            jax.ShapeDtypeStruct((group_count, 1, row_count // group_count), jnp.int32),
            jax.ShapeDtypeStruct((row_count // leaf_size, 1, leaf_size), jnp.int32),
            jax.ShapeDtypeStruct((row_count // leaf_size, 1, leaf_size), jnp.int32),
            TICK,
        ),
        compiler_params=pltpu.CompilerParams(vmem_limit_bytes=8 * MIB),
        cost_estimate=pl.CostEstimate(flops=2 * 10**9, bytes_accessed=10**5, transcendentals=0),
        name="index_lists",
    )(order.reshape(-1, 128))


def table_body(points_ref, weights_ref, table_ref):
    height = weights_ref.shape[0] + 2 * points_ref.shape[0]
    for h in range(points_ref.shape[1] // 256):
        at = slice(h * 256, (h + 1) * 256)
        high, low = scaled_halves(points_ref[:, at])
        table_ref[h * height : (h + 1) * height, :] = jnp.concatenate(
            [weights_ref[:, at], high, low], axis=0
        ).astype(bf16)


def pick_table(points, weights):
    height = weights.shape[0] + 2 * points.shape[0]
    whole = pl.BlockSpec(memory_space=pltpu.VMEM)
    return pl.pallas_call(
        table_body,
        in_specs=[whole, whole],
        out_specs=whole,
        out_shape=jax.ShapeDtypeStruct((points.shape[1] // 256 * height, 256), bf16),
        compiler_params=pltpu.CompilerParams(vmem_limit_bytes=10 * MIB),
        cost_estimate=pl.CostEstimate(flops=3 * 10**9, bytes_accessed=3 * 10**6, transcendentals=0),
        name="pick_table",
    )(points, weights)


def pick_body(want_ref, table_ref, out_ref):
    group_count, height, pair = out_ref.shape
    high_count = table_ref.shape[0] // height
    batch = 4

    def device(d, carry):
        want = want_ref[d]
        low = want & 255
        high = want >> 8
        spots = (lax.broadcasted_iota(jnp.int32, (256, pair), 0) == low).astype(f32).astype(bf16)
        picked = jnp.zeros((height, pair), f32)
        for h in range(0, high_count, batch):
            found = mm(table_ref[h * height : (h + batch) * height, :], spots)
            for k in range(batch):
                picked = jnp.where(high == h + k, found[k * height : (k + 1) * height], picked)
        out_ref[d] = picked.astype(bf16)
        return carry

    lax.fori_loop(0, group_count, device, 0)


def pick(want, table, row_count):
    group_count, _, pair = want.shape
    height = table.shape[0] * 256 // row_count
    whole = pl.BlockSpec(memory_space=pltpu.VMEM)
    return pl.pallas_call(
        pick_body,
        in_specs=[whole, whole],
        out_specs=whole,
        out_shape=jax.ShapeDtypeStruct((group_count, height, pair), bf16),
        compiler_params=pltpu.CompilerParams(vmem_limit_bytes=14 * MIB),
        cost_estimate=pl.CostEstimate(flops=6 * 10**9, bytes_accessed=3 * 10**6, transcendentals=0),
        name="pick",
    )(want, table)


def split_body(basis_ref, transfer_ref, after_ref, *out_refs):
    for n, ref in enumerate((basis_ref, transfer_ref)):
        high_ref, low_ref = out_refs[2 * n : 2 * n + 2]

        def leaf(i, carry, ref=ref, high_ref=high_ref, low_ref=low_ref):
            high_ref[i], low_ref[i] = halves(ref[i])
            return carry

        lax.fori_loop(0, ref.shape[0], leaf, 0)


def split(basis, transfer, after):
    whole = pl.BlockSpec(memory_space=pltpu.VMEM)
    shapes = [jax.ShapeDtypeStruct(x.shape, bf16) for x in (basis, basis, transfer, transfer)]
    return pl.pallas_call(
        split_body,
        in_specs=[whole, whole, pl.BlockSpec(memory_space=pl.ANY)],
        out_specs=[whole] * 4,
        out_shape=shapes,
        compiler_params=pltpu.CompilerParams(vmem_limit_bytes=14 * MIB),
        cost_estimate=pl.CostEstimate(flops=3 * 10**9, bytes_accessed=10**7, transcendentals=0),
        name="split",
    )(basis, transfer, after)


def place_body(src_ref, rank_ref, arrived_ref, leaf_ref):
    leaf_count, height, leaf_size = leaf_ref.shape
    pair = arrived_ref.shape[1]
    group_count = arrived_ref.shape[0] // height
    batch = 4
    step = 4

    def leaves(c, carry):
        for n in range(step):
            i = c * step + n
            src = src_ref[i]
            spots = (
                lax.broadcasted_iota(jnp.int32, (pair, leaf_size), 0) == rank_ref[i]
            ).astype(f32).astype(bf16)
            placed = jnp.zeros((height, leaf_size), f32)
            for g in range(0, group_count, batch):
                found = mm(arrived_ref[g * height : (g + batch) * height, :], spots)
                for k in range(batch):
                    placed = jnp.where(src == g + k, found[k * height : (k + 1) * height], placed)
            leaf_ref[i] = placed.astype(bf16)
        return carry

    lax.fori_loop(0, leaf_count // step, leaves, 0)


def place(src, rank, arrived):
    group_count, height, pair = arrived.shape
    leaf_count, _, leaf_size = src.shape
    whole = pl.BlockSpec(memory_space=pltpu.VMEM)
    return pl.pallas_call(
        place_body,
        in_specs=[whole] * 3,
        out_specs=whole,
        out_shape=jax.ShapeDtypeStruct((leaf_count, height, leaf_size), bf16),
        compiler_params=pltpu.CompilerParams(vmem_limit_bytes=12 * MIB),
        cost_estimate=pl.CostEstimate(flops=8 * 10**9, bytes_accessed=2 * 10**6, transcendentals=0),
        name="place",
    )(src, rank, arrived.reshape(group_count * height, pair))


def skeleton_body(leaf_ref, basis_high, basis_low, transfer_high, transfer_low, skel_ref, upper_ref):
    leaf_count, cols, _ = skel_ref.shape

    def cluster(c, carry):
        total = jnp.zeros(upper_ref.shape[1:], f32)
        for n in range(KIDS):
            i = c * KIDS + n
            values = leaf_ref[i, :cols]
            skel = mm(values, basis_high[i]) + mm(values, basis_low[i])
            skel_ref[i] = skel.astype(bf16)
            total += mm3(halves(skel), (transfer_high[i], transfer_low[i]))
        upper_ref[c] = total.astype(bf16)
        return carry

    lax.fori_loop(0, leaf_count // KIDS, cluster, 0)


def skeleton(leaves, parts):
    leaf_count, _, rank_size = parts[0].shape
    cols = leaves.shape[1] - 16
    whole = pl.BlockSpec(memory_space=pltpu.VMEM)
    return pl.pallas_call(
        skeleton_body,
        in_specs=[whole] * 5,
        out_specs=(whole, whole),
        out_shape=(
            jax.ShapeDtypeStruct((leaf_count, cols, rank_size), bf16),
            jax.ShapeDtypeStruct((leaf_count // KIDS, cols, rank_size), bf16),
        ),
        compiler_params=pltpu.CompilerParams(vmem_limit_bytes=14 * MIB),
        cost_estimate=pl.CostEstimate(flops=10**9, bytes_accessed=7 * 10**6, transcendentals=0),
        name="skeleton",
    )(leaves, *parts)


def near_body(list_ref, low_ref, own_ref, high_ref, after_ref, out_ref, tick_ref, rows, values):
    tick_ref[...] = jnp.zeros_like(tick_ref)
    leaf_count, height, leaf_size = own_ref.shape
    cols = height - 16
    for part, ref in enumerate((low_ref, own_ref, high_ref)):

        def fill(n, carry, part=part, ref=ref):
            values[part * leaf_count + n] = ref[n, :cols]
            tail = ref[n, cols:].astype(f32)
            rows[part * leaf_count + n] = source_rows(tail[:8], tail[8:])
            return carry

        lax.fori_loop(0, leaf_count, fill, 0)

    def leaf(i, carry):
        tail = own_ref[i, cols:].astype(f32)
        target = target_rows(tail[:8], tail[8:])
        total = jnp.zeros((leaf_size, cols), f32)
        for q in range(list_ref.shape[1]):
            j = list_ref[i, q]
            total += mm(matern(mm(target, rows[j])), values[j], NT)
        out_ref[i] = total
        return carry

    lax.fori_loop(0, leaf_count, leaf, 0)


def near_sums(lists, low, own, high, after):
    leaf_count, near = lists.shape
    height, leaf_size = own.shape[1:]
    cols = height - 16
    whole = pl.BlockSpec(memory_space=pltpu.VMEM)
    pairs = leaf_count * near * leaf_size * leaf_size
    return pl.pallas_call(
        near_body,
        in_specs=[pl.BlockSpec(memory_space=pltpu.SMEM), whole, whole, whole]
        + [pl.BlockSpec(memory_space=pl.ANY)],
        out_specs=(whole, whole),
        out_shape=(jax.ShapeDtypeStruct((leaf_count, leaf_size, cols), f32), TICK),
        scratch_shapes=[
            pltpu.VMEM((3 * leaf_count, AUG, leaf_size), bf16),
            pltpu.VMEM((3 * leaf_count, cols, leaf_size), bf16),
        ],
        compiler_params=pltpu.CompilerParams(vmem_limit_bytes=16 * MIB),
        cost_estimate=pl.CostEstimate(
            flops=pairs * 2500, bytes_accessed=6 * 10**6, transcendentals=2 * pairs
        ),
        name="near_sums",
    )(lists, low, own, high, after)


def far_rows_body(points_ref, rows_ref):
    step = 8

    def fill(n, carry):
        for k in range(step):
            rows_ref[n * step + k] = source_rows(*f32_halves(points_ref[n * step + k]))
        return carry

    lax.fori_loop(0, points_ref.shape[0] // step, fill, 0)


def far_rows(points):
    count, _, rank_size = points.shape
    whole = pl.BlockSpec(memory_space=pltpu.VMEM)
    return pl.pallas_call(
        far_rows_body,
        in_specs=[whole],
        out_specs=whole,
        out_shape=jax.ShapeDtypeStruct((count, AUG, rank_size), bf16),
        compiler_params=pltpu.CompilerParams(vmem_limit_bytes=14 * MIB),
        cost_estimate=pl.CostEstimate(flops=10**8, bytes_accessed=10**6, transcendentals=0),
        name="far_rows",
    )(points)


def far_body(list_ref, target_ref, rows_ref, *refs):
    out_ref, tick_ref = refs[-2:]
    rank_size = rows_ref.shape[2]
    far = list_ref.shape[1]
    batch = 4
    step = 4

    def leaves(n, carry):
        for k in range(step):
            i = n * step + k
            target = target_rows(*f32_halves(target_ref[i]))
            for q in range(0, far, batch):
                rows = jnp.concatenate([rows_ref[list_ref[i, q + r]] for r in range(batch)], axis=1)
                out_ref[i, :, q * rank_size : (q + batch) * rank_size] = matern(mm(target, rows))
        return carry

    lax.fori_loop(0, out_ref.shape[0] // step, leaves, 0)
    tick_ref[...] = jnp.zeros_like(tick_ref)


def far_kernels(count, lists, targets, rows, *after):
    far = lists.shape[1]
    rank_size = rows.shape[2]
    pairs = count * far * rank_size * rank_size
    whole = pl.BlockSpec(memory_space=pltpu.VMEM)
    return pl.pallas_call(
        far_body,
        in_specs=[pl.BlockSpec(memory_space=pltpu.SMEM), whole, whole]
        + [pl.BlockSpec(memory_space=pl.ANY)] * len(after),
        out_specs=(whole, whole),
        out_shape=(jax.ShapeDtypeStruct((count, rank_size, far * rank_size), bf16), TICK),
        compiler_params=pltpu.CompilerParams(vmem_limit_bytes=26 * MIB),
        cost_estimate=pl.CostEstimate(flops=pairs * 20, bytes_accessed=10**6, transcendentals=0),
        name="far_kernels",
    )(lists, targets, rows, *after)


def far_sums_body(list_ref, target_ref, rows_ref, weights_ref, stored_ref, after_ref, out_ref, even, odd):
    early = stored_ref.shape[0]
    late = out_ref.shape[0] - early
    rank_size = weights_ref.shape[2]
    far = list_ref.shape[1]
    batch = 4

    def listed(ref, i, q, n):
        return jnp.concatenate([ref[list_ref[i, q + k]] for k in range(n)], axis=1)

    def fill(i, kernel):
        target = target_rows(*f32_halves(target_ref[i]))
        for q in range(0, far, batch):
            kernel[:, q * rank_size : (q + batch) * rank_size] = matern(
                mm(target, listed(rows_ref, i, q, batch))
            )

    def apply(i, kernel):
        out_ref[i] = mm(kernel, listed(weights_ref, i, 0, far), NT)

    fill(early, even)

    def two(n, carry):
        i = early + 2 * n
        fill(i + 1, odd)
        apply(i, even[...])
        fill(jnp.minimum(i + 2, early + late - 1), even)
        apply(i + 1, odd[...])
        return carry

    lax.fori_loop(0, late // 2, two, 0)

    def four(n, carry):
        for k in range(4):
            apply(4 * n + k, stored_ref[4 * n + k])
        return carry

    lax.fori_loop(0, early // 4, four, 0)


def far_sums(lists, targets, rows, weights, stored, after):
    count, far = lists.shape
    cols, rank_size = weights.shape[1:]
    whole = pl.BlockSpec(memory_space=pltpu.VMEM)
    pairs = count * far * rank_size * rank_size
    return pl.pallas_call(
        far_sums_body,
        in_specs=[pl.BlockSpec(memory_space=pltpu.SMEM), whole, whole, whole, whole]
        + [pl.BlockSpec(memory_space=pl.ANY)],
        out_specs=whole,
        out_shape=jax.ShapeDtypeStruct((count, rank_size, cols), f32),
        scratch_shapes=[pltpu.VMEM((rank_size, far * rank_size), bf16)] * 2,
        compiler_params=pltpu.CompilerParams(vmem_limit_bytes=12 * MIB),
        cost_estimate=pl.CostEstimate(
            flops=pairs * 2500, bytes_accessed=24 * 10**6, transcendentals=2 * pairs
        ),
        name="far_sums",
    )(lists, targets, rows, weights, stored, after)


def upper_body(list_ref, own_ref, chip_ref, across_ref, after_ref, out_ref):
    dims, rank_size = own_ref.shape[1:]
    cols = out_ref.shape[2]
    batch = 4
    half = chip_ref.shape[0]

    def block_of(place):
        here = chip_ref[jnp.minimum(place, half - 1)]
        there = across_ref[jnp.maximum(place - half, 0)]
        return jnp.where(place < half, here, there)

    for c in range(own_ref.shape[0]):
        target = target_rows(*scaled_halves(own_ref[c]))
        total = jnp.zeros((rank_size, cols), f32)
        for q in range(0, list_ref.shape[1], batch):
            blocks = [block_of(list_ref[c, q + k]) for k in range(batch)]
            values = jnp.concatenate([x[:cols] for x in blocks], axis=1)
            points = jnp.concatenate([x[cols:].astype(f32)[:dims] for x in blocks], axis=1)
            kernel = matern(mm(target, source_rows(*scaled_halves(points))))
            total += mm(kernel, values, NT)
        out_ref[c] = total


def upper_sums(lists, own, chip, across, after):
    count, dims, rank_size = own.shape
    cols = chip.shape[1] - 2 * dims
    whole = pl.BlockSpec(memory_space=pltpu.VMEM)
    pairs = count * lists.shape[1] * rank_size * rank_size
    return pl.pallas_call(
        upper_body,
        in_specs=[pl.BlockSpec(memory_space=pltpu.SMEM), whole, whole, whole]
        + [pl.BlockSpec(memory_space=pl.ANY)],
        out_specs=whole,
        out_shape=jax.ShapeDtypeStruct((count, rank_size, cols), f32),
        compiler_params=pltpu.CompilerParams(vmem_limit_bytes=16 * MIB),
        cost_estimate=pl.CostEstimate(
            flops=pairs * 230, bytes_accessed=8 * 10**6, transcendentals=2 * pairs
        ),
        name="upper_sums",
    )(lists, own, chip, across, after)


def final_body(far_ref, upper_ref, basis_high, basis_low, transfer_high, transfer_low, near_ref, out_ref):
    leaf_count, leaf_size, _ = basis_high.shape
    step = 4

    def leaves(n, carry):
        upper = halves(upper_ref[n * step // KIDS])
        for k in range(step):
            i = n * step + k
            skeleton = far_ref[i] + mm3((transfer_high[i], transfer_low[i]), upper)
            potential = mm3((basis_high[i], basis_low[i]), halves(skeleton)) + near_ref[i]
            at = pl.ds(pl.multiple_of(i * leaf_size, leaf_size), leaf_size)
            out_ref[:, at] = jnp.transpose(potential)
        return carry

    lax.fori_loop(0, leaf_count // step, leaves, 0)


def final(far, upper, parts, near):
    leaf_count, leaf_size, rank_size = parts[0].shape
    cols = near.shape[2]
    whole = pl.BlockSpec(memory_space=pltpu.VMEM)
    return pl.pallas_call(
        final_body,
        in_specs=[whole] * 7,
        out_specs=whole,
        out_shape=jax.ShapeDtypeStruct((cols, leaf_count * leaf_size), f32),
        compiler_params=pltpu.CompilerParams(vmem_limit_bytes=16 * MIB),
        cost_estimate=pl.CostEstimate(flops=10**9, bytes_accessed=10**7, transcendentals=0),
        name="final",
    )(far, upper, *parts, near)


def shifted(block, axis, move, count):
    return lax.ppermute(block, axis, [(i, move(i)) for i in range(count)])


def upper_places(clusters, count):
    owner = clusters // count
    group = owner % 16
    bulk = owner // 16
    mine = lax.axis_index("bulk")
    core = (bulk ^ mine) & 1
    hops = (bulk // 2 - mine // 2) & 3
    turn = hops
    return (((core * 4 + turn) * 16) + group) * count + clusters % count


def local(
    points,
    weights,
    leaf_order,
    basis,
    transfer,
    skel_leaf,
    skel_upper,
    near_list,
    leaf_interaction_list,
    far_upper,
):
    row_count = leaf_order.shape[0]
    group_count = lax.axis_size("group")
    bulk_count = lax.axis_size("bulk")
    device_count = group_count * bulk_count
    leaf_count = basis.shape[0]

    want, src, rank, tick = index_lists(leaf_order, group_count, basis.shape[1])
    scaled = skel_leaf.astype(f32) * POINT_SCALE + tick[0]
    subtree_points = lax.all_gather(scaled, "group", axis=0, tiled=True)
    wanted = lax.all_to_all(want, "group", split_axis=0, concat_axis=0, tiled=True)
    parts = split(basis, transfer, wanted)
    picked = pick(wanted, pick_table(points, weights), row_count)
    arrived = lax.all_to_all(picked, "group", split_axis=0, concat_axis=0, tiled=True)

    far_local = leaf_interaction_list - lax.axis_index("bulk") * (group_count * leaf_count)

    own = place(src, rank, arrived)
    skel_wb, upper_wb = skeleton(own, parts)
    sub_w = lax.all_gather(skel_wb, "group", axis=0, tiled=True)
    forward = [(i, i + 1) for i in range(device_count - 1)]
    backward = [(i + 1, i) for i in range(device_count - 1)]
    low = lax.ppermute(own, ("bulk", "group"), forward)
    high = lax.ppermute(own, ("bulk", "group"), backward)

    def joined(tick, *blocks):
        return jnp.concatenate(blocks, axis=0) + tick[0].astype(bf16)

    mine = jnp.concatenate([upper_wb, skel_upper, jnp.zeros(skel_upper.shape, bf16)], axis=1)
    copies = jnp.tile(mine, (group_count, 1, 1))
    block = lax.all_to_all(copies, "group", split_axis=0, concat_axis=0, tiled=True)
    part = leaf_count // 2
    source_points = far_rows(subtree_points)
    kernels, tick = far_kernels(part, far_local, scaled, source_points, copies)
    block = joined(tick, block)
    ring = [shifted(block, "bulk", lambda i, hops=hops: (i - 2 * hops) % bulk_count, bulk_count) for hops in (1, 2, 3)]
    device = lax.axis_index(("bulk", "group"))
    near, tick = near_sums(near_list - (device - 1) * leaf_count, low, own, high, block)
    chip = joined(tick, block, *ring)
    other = shifted(chip, "bulk", lambda i: i ^ 1, bulk_count)
    far = far_sums(far_local, scaled, source_points, sub_w, kernels, chip)
    upper = upper_sums(upper_places(far_upper, skel_upper.shape[0]), skel_upper, chip, other, far)
    return final(far, upper, parts, near)


def solution(mesh):
    placed = (
        P(None, ("bulk", "group")),
        P(None, ("bulk", "group")),
        P(("bulk", "group")),
        P(("bulk", "group"), None, None),
        P(("bulk", "group"), None, None),
        P(("bulk", "group"), None, None),
        P(("bulk", "group"), None, None),
        P(("bulk", "group"), None),
        P(("bulk", "group"), None),
        P(("bulk", "group"), None),
    )
    return jax.shard_map(
        local, mesh=mesh, in_specs=placed, out_specs=P(None, ("bulk", "group")), check_vma=False
    )
```

```python
import functools
import math

import jax
import jax.numpy as jnp
from jax import lax
from jax.experimental import pallas as pl
from jax.experimental.pallas import tpu as pltpu
from jax.sharding import PartitionSpec as P

KIDS = 8

POINT_SCALE = math.sqrt(5.0) / 2.0 / math.log(2.0)
POLY_A = 3.0 / math.log(2.0)
POLY_B = 3.0 / math.log(2.0) ** 2
POLY_LOG = math.log2(math.log(2.0) ** 2 / 3.0)
AUG = 48
MIB = 1024 * 1024

f32 = jnp.float32
bf16 = jnp.bfloat16
TICK = jax.ShapeDtypeStruct((8, 128), f32)
NN = (((1,), (0,)), ((), ()))
NT = (((1,), (1,)), ((), ()))


def mm(a, b, dims=NN):
    return lax.dot_general(a, b, dims, preferred_element_type=f32)


def halves(x):
    high = x.astype(bf16)
    return high, (x - high.astype(f32)).astype(bf16)


def mm3(a, b):
    a_high, a_low = halves(a)
    b_high, b_low = halves(b)
    return mm(a_high, b_high) + (mm(a_high, b_low) + mm(a_low, b_high))


def squares(high, low):
    x = high + low
    norm = jnp.sum(x * x, axis=0, keepdims=True)
    first = norm.astype(bf16).astype(f32)
    second = (norm - first).astype(bf16).astype(f32)
    third = norm - first - second
    row = lax.broadcasted_iota(jnp.int32, high.shape, 0)
    parts = jnp.where(row % 3 == 0, first, jnp.where(row % 3 == 1, second, third))
    return row, parts


def source_rows(high, low):
    row, parts = squares(high, low)
    last = jnp.where(row < 3, 1.0, jnp.where(row < 6, parts, 0.0))
    high, low = -2.0 * high, -2.0 * low
    return jnp.concatenate([high, low, high, low, last, jnp.zeros_like(last)], axis=0).astype(bf16)


def target_rows(high, low):
    row, parts = squares(high, low)
    last = jnp.where(row < 3, parts, jnp.where(row < 6, 1.0, 0.0))
    rows = jnp.concatenate([high, high, low, low, last, jnp.zeros_like(last)], axis=0)
    return jnp.transpose(rows).astype(bf16)


def f32_halves(points):
    high, low = halves(points)
    return high.astype(f32), low.astype(f32)


def scaled_halves(points):
    return f32_halves(points.astype(f32) * POINT_SCALE)


def matern(square):
    square = jnp.maximum(square, 1e-30)
    t = square * lax.rsqrt(square)
    return (((t + POLY_A) * t + POLY_B) * jnp.exp2(POLY_LOG - t)).astype(bf16)


def index_body(order_ref, want_ref, src_ref, rank_ref, tick_ref):
    tick_ref[...] = jnp.zeros_like(tick_ref)
    group_count, _, pair = want_ref.shape
    lines = order_ref.shape[0]
    row_count = group_count * pair
    order = order_ref[...]
    owner = ((order.astype(f32) + 0.5) * (1.0 / row_count)).astype(jnp.int32)
    src = owner % group_count
    row = order - owner * row_count
    before = (
        lax.broadcasted_iota(jnp.int32, (128, 128), 0)
        < lax.broadcasted_iota(jnp.int32, (128, 128), 1)
    ).astype(f32).astype(bf16)
    above = (
        lax.broadcasted_iota(jnp.int32, (lines, lines), 1)
        < lax.broadcasted_iota(jnp.int32, (lines, lines), 0)
    ).astype(f32).astype(bf16)
    all_ones = jnp.ones((128, 128), bf16)
    rank = jnp.zeros(src.shape, f32)
    for g in range(group_count):
        here = src == g
        mask = here.astype(f32).astype(bf16)
        total = mm(mask, all_ones).astype(bf16)
        rank = jnp.where(here, mm(mask, before) + mm(above, total), rank)
    rank = rank.astype(jnp.int32)
    for i in range(lines // 2):
        for ref, x in ((src_ref, src), (rank_ref, rank)):
            ref[i] = jnp.concatenate([x[2 * i : 2 * i + 1], x[2 * i + 1 : 2 * i + 2]], axis=1)
    place = lax.broadcasted_iota(jnp.int32, (pair, 256), 0)
    owner = lax.broadcasted_iota(jnp.int32, (group_count, 256), 0)
    total = jnp.zeros((2 * group_count, pair), f32)
    for k in range(0, lines, 2):
        line = lambda x: jnp.concatenate([x[k : k + 1], x[k + 1 : k + 2]], axis=1)
        rank_line, src_line, row_line = line(rank), line(src), line(row)
        spots = (place == rank_line).astype(f32).astype(bf16)
        mine = owner == src_line
        high = jnp.where(mine, (row_line >> 7).astype(f32), 0.0)
        low = jnp.where(mine, (row_line & 127).astype(f32), 0.0)
        total += mm(jnp.concatenate([high, low], axis=0).astype(bf16), spots, NT)
    want = (total[:group_count] * 128.0 + total[group_count:]).astype(jnp.int32)
    for g in range(group_count):
        want_ref[g] = want[g : g + 1]


def index_lists(order, group_count, leaf_size):
    row_count = order.shape[0]
    assert leaf_size == 256
    return pl.pallas_call(
        index_body,
        out_shape=(
            jax.ShapeDtypeStruct((group_count, 1, row_count // group_count), jnp.int32),
            jax.ShapeDtypeStruct((row_count // leaf_size, 1, leaf_size), jnp.int32),
            jax.ShapeDtypeStruct((row_count // leaf_size, 1, leaf_size), jnp.int32),
            TICK,
        ),
        compiler_params=pltpu.CompilerParams(vmem_limit_bytes=8 * MIB),
        cost_estimate=pl.CostEstimate(flops=2 * 10**9, bytes_accessed=10**5, transcendentals=0),
        name="index_lists",
    )(order.reshape(-1, 128))


def table_body(points_ref, weights_ref, table_ref):
    height = weights_ref.shape[0] + 2 * points_ref.shape[0]
    for h in range(points_ref.shape[1] // 256):
        at = slice(h * 256, (h + 1) * 256)
        high, low = scaled_halves(points_ref[:, at])
        table_ref[h * height : (h + 1) * height, :] = jnp.concatenate(
            [weights_ref[:, at], high, low], axis=0
        ).astype(bf16)


def pick_table(points, weights):
    height = weights.shape[0] + 2 * points.shape[0]
    whole = pl.BlockSpec(memory_space=pltpu.VMEM)
    return pl.pallas_call(
        table_body,
        in_specs=[whole, whole],
        out_specs=whole,
        out_shape=jax.ShapeDtypeStruct((points.shape[1] // 256 * height, 256), bf16),
        compiler_params=pltpu.CompilerParams(vmem_limit_bytes=10 * MIB),
        cost_estimate=pl.CostEstimate(flops=3 * 10**9, bytes_accessed=3 * 10**6, transcendentals=0),
        name="pick_table",
    )(points, weights)


def pick_body(want_ref, table_ref, out_ref):
    group_count, height, pair = out_ref.shape
    high_count = table_ref.shape[0] // height
    batch = 4

    def device(d, carry):
        want = want_ref[d]
        low = want & 255
        high = want >> 8
        spots = (lax.broadcasted_iota(jnp.int32, (256, pair), 0) == low).astype(f32).astype(bf16)
        picked = jnp.zeros((height, pair), f32)
        for h in range(0, high_count, batch):
            found = mm(table_ref[h * height : (h + batch) * height, :], spots)
            for k in range(batch):
                picked = jnp.where(high == h + k, found[k * height : (k + 1) * height], picked)
        out_ref[d] = picked.astype(bf16)
        return carry

    lax.fori_loop(0, group_count, device, 0)


def pick(want, table, row_count):
    group_count, _, pair = want.shape
    height = table.shape[0] * 256 // row_count
    whole = pl.BlockSpec(memory_space=pltpu.VMEM)
    return pl.pallas_call(
        pick_body,
        in_specs=[whole, whole],
        out_specs=whole,
        out_shape=jax.ShapeDtypeStruct((group_count, height, pair), bf16),
        compiler_params=pltpu.CompilerParams(vmem_limit_bytes=14 * MIB),
        cost_estimate=pl.CostEstimate(flops=6 * 10**9, bytes_accessed=3 * 10**6, transcendentals=0),
        name="pick",
    )(want, table)


def place_body(src_ref, rank_ref, arrived_ref, leaf_ref):
    leaf_count, height, leaf_size = leaf_ref.shape
    pair = arrived_ref.shape[1]
    group_count = arrived_ref.shape[0] // height
    batch = 4
    step = 4

    def leaves(c, carry):
        for n in range(step):
            i = c * step + n
            src = src_ref[i]
            spots = (
                lax.broadcasted_iota(jnp.int32, (pair, leaf_size), 0) == rank_ref[i]
            ).astype(f32).astype(bf16)
            placed = jnp.zeros((height, leaf_size), f32)
            for g in range(0, group_count, batch):
                found = mm(arrived_ref[g * height : (g + batch) * height, :], spots)
                for k in range(batch):
                    placed = jnp.where(src == g + k, found[k * height : (k + 1) * height], placed)
            leaf_ref[i] = placed.astype(bf16)
        return carry

    lax.fori_loop(0, leaf_count // step, leaves, 0)


def place(src, rank, arrived):
    group_count, height, pair = arrived.shape
    leaf_count, _, leaf_size = src.shape
    whole = pl.BlockSpec(memory_space=pltpu.VMEM)
    return pl.pallas_call(
        place_body,
        in_specs=[whole] * 3,
        out_specs=whole,
        out_shape=jax.ShapeDtypeStruct((leaf_count, height, leaf_size), bf16),
        compiler_params=pltpu.CompilerParams(vmem_limit_bytes=12 * MIB),
        cost_estimate=pl.CostEstimate(flops=8 * 10**9, bytes_accessed=2 * 10**6, transcendentals=0),
        name="place",
    )(src, rank, arrived.reshape(group_count * height, pair))


def skeleton_body(leaf_ref, basis_ref, transfer_ref, skel_ref, upper_ref):
    leaf_count, cols, _ = skel_ref.shape

    def cluster(c, carry):
        total = jnp.zeros(upper_ref.shape[1:], f32)
        for n in range(KIDS):
            i = c * KIDS + n
            values = leaf_ref[i, :cols]
            basis_high, basis_low = halves(basis_ref[i])
            skel = mm(values, basis_high) + mm(values, basis_low)
            skel_ref[i] = skel.astype(bf16)
            total += mm3(skel, transfer_ref[i])
        upper_ref[c] = total.astype(bf16)
        return carry

    lax.fori_loop(0, leaf_count // KIDS, cluster, 0)


def skeleton(leaves, basis, transfer):
    leaf_count, _, rank_size = basis.shape
    cols = leaves.shape[1] - 16
    whole = pl.BlockSpec(memory_space=pltpu.VMEM)
    return pl.pallas_call(
        skeleton_body,
        in_specs=[whole] * 3,
        out_specs=(whole, whole),
        out_shape=(
            jax.ShapeDtypeStruct((leaf_count, cols, rank_size), bf16),
            jax.ShapeDtypeStruct((leaf_count // KIDS, cols, rank_size), bf16),
        ),
        compiler_params=pltpu.CompilerParams(vmem_limit_bytes=14 * MIB),
        cost_estimate=pl.CostEstimate(flops=10**9, bytes_accessed=7 * 10**6, transcendentals=0),
        name="skeleton",
    )(leaves, basis, transfer)


def near_body(list_ref, low_ref, own_ref, high_ref, after_ref, out_ref, tick_ref, rows, values):
    tick_ref[...] = jnp.zeros_like(tick_ref)
    leaf_count, height, leaf_size = own_ref.shape
    cols = height - 16
    for part, ref in enumerate((low_ref, own_ref, high_ref)):

        def fill(n, carry, part=part, ref=ref):
            values[part * leaf_count + n] = ref[n, :cols]
            tail = ref[n, cols:].astype(f32)
            rows[part * leaf_count + n] = source_rows(tail[:8], tail[8:])
            return carry

        lax.fori_loop(0, leaf_count, fill, 0)

    def leaf(i, carry):
        tail = own_ref[i, cols:].astype(f32)
        target = target_rows(tail[:8], tail[8:])
        total = jnp.zeros((leaf_size, cols), f32)
        for q in range(list_ref.shape[1]):
            j = list_ref[i, q]
            total += mm(matern(mm(target, rows[j])), values[j], NT)
        out_ref[i] = total
        return carry

    lax.fori_loop(0, leaf_count, leaf, 0)


def near_sums(lists, low, own, high, after):
    leaf_count, near = lists.shape
    height, leaf_size = own.shape[1:]
    cols = height - 16
    whole = pl.BlockSpec(memory_space=pltpu.VMEM)
    pairs = leaf_count * near * leaf_size * leaf_size
    return pl.pallas_call(
        near_body,
        in_specs=[pl.BlockSpec(memory_space=pltpu.SMEM), whole, whole, whole]
        + [pl.BlockSpec(memory_space=pl.ANY)],
        out_specs=(whole, whole),
        out_shape=(jax.ShapeDtypeStruct((leaf_count, leaf_size, cols), f32), TICK),
        scratch_shapes=[
            pltpu.VMEM((3 * leaf_count, AUG, leaf_size), bf16),
            pltpu.VMEM((3 * leaf_count, cols, leaf_size), bf16),
        ],
        compiler_params=pltpu.CompilerParams(vmem_limit_bytes=20 * MIB),
        cost_estimate=pl.CostEstimate(
            flops=pairs * 2500, bytes_accessed=6 * 10**6, transcendentals=2 * pairs
        ),
        name="near_sums",
    )(lists, low, own, high, after)


def fill_rows(points_ref, rows_ref):
    step = 8

    def fill(n, carry):
        for k in range(step):
            rows_ref[n * step + k] = source_rows(*f32_halves(points_ref[n * step + k]))
        return carry

    lax.fori_loop(0, rows_ref.shape[0] // step, fill, 0)


FAR_STEP = 4


def far_body(first, after_count, list_ref, target_ref, points_ref, *refs):
    out_ref, tick_ref, rows_ref = refs[after_count:]

    @pl.when(pl.program_id(0) == 0)
    def _():
        fill_rows(points_ref, rows_ref)

    rank_size = rows_ref.shape[2]
    far = list_ref.shape[1]
    batch = 4
    for n in range(FAR_STEP):
        i = first + pl.program_id(0) * FAR_STEP + n
        target = target_rows(*f32_halves(target_ref[i]))
        for q in range(0, far, batch):
            rows = jnp.concatenate([rows_ref[list_ref[i, q + k]] for k in range(batch)], axis=1)
            out_ref[n, :, q * rank_size : (q + batch) * rank_size] = matern(mm(target, rows))
    tick_ref[...] = jnp.zeros_like(tick_ref)


def far_kernels(first, count, lists, targets, points, *after):
    far = lists.shape[1]
    rank_size = points.shape[2]
    pairs = count * far * rank_size * rank_size
    anywhere = pl.BlockSpec(memory_space=pl.ANY)
    return pl.pallas_call(
        functools.partial(far_body, first, len(after)),
        grid_spec=pltpu.PrefetchScalarGridSpec(
            num_scalar_prefetch=1,
            grid=(count // FAR_STEP,),
            in_specs=[
                pl.BlockSpec(targets.shape, lambda i, s: (0, 0, 0)),
                pl.BlockSpec(points.shape, lambda i, s: (0, 0, 0)),
            ]
            + [anywhere] * len(after),
            out_specs=(
                pl.BlockSpec((FAR_STEP, rank_size, far * rank_size), lambda i, s: (i, 0, 0)),
                pl.BlockSpec(TICK.shape, lambda i, s: (0, 0)),
            ),
            scratch_shapes=[pltpu.VMEM((points.shape[0], AUG, rank_size), bf16)],
        ),
        out_shape=(jax.ShapeDtypeStruct((count, rank_size, far * rank_size), bf16), TICK),
        compiler_params=pltpu.CompilerParams(vmem_limit_bytes=52 * MIB),
        cost_estimate=pl.CostEstimate(
            flops=pairs * 20, bytes_accessed=10**6, transcendentals=0
        ),
        name="far_kernels",
    )(lists, targets, points, *after)


STREAM_STEP = 4


def far_sums_body(
    list_ref, target_ref, points_ref, gathered_ref, stored_ref, after_ref, out_ref, even, odd, stream, rows_ref, weights_ref, sems
):
    early = stored_ref.shape[0]
    late = out_ref.shape[0] - early
    rank_size = weights_ref.shape[2]
    far = list_ref.shape[1]
    batch = 4
    blocks = early // STREAM_STEP
    copies = [
        pltpu.make_async_copy(
            stored_ref.at[pl.ds(k * STREAM_STEP, STREAM_STEP)], stream.at[k % 2], sems.at[k % 2]
        )
        for k in range(blocks)
    ]

    def listed(ref, i, q, n):
        return jnp.concatenate([ref[list_ref[i, q + k]] for k in range(n)], axis=1)

    def fill(i, kernel):
        target = target_rows(*f32_halves(target_ref[i]))
        for q in range(0, far, batch):
            kernel[:, q * rank_size : (q + batch) * rank_size] = matern(
                mm(target, listed(rows_ref, i, q, batch))
            )

    def apply(i, kernel):
        out_ref[i] = mm(kernel, listed(weights_ref, i, 0, far), NT)

    weights_copy = pltpu.make_async_copy(gathered_ref, weights_ref, sems.at[2])
    weights_copy.start()
    for copy in copies[:2]:
        copy.start()
    fill_rows(points_ref, rows_ref)
    fill(early, even)
    weights_copy.wait()

    def two(n, carry):
        i = early + 2 * n
        fill(i + 1, odd)
        apply(i, even[...])
        fill(jnp.minimum(i + 2, early + late - 1), even)
        apply(i + 1, odd[...])
        return carry

    lax.fori_loop(0, late // 2, two, 0)
    for k, copy in enumerate(copies):
        copy.wait()
        for n in range(STREAM_STEP):
            apply(k * STREAM_STEP + n, stream[k % 2, n])
        if k + 2 < blocks:
            copies[k + 2].start()


def far_sums(lists, targets, points, weights, stored, after):
    count, far = lists.shape
    cols, rank_size = weights.shape[1:]
    whole = pl.BlockSpec(memory_space=pltpu.VMEM)
    anywhere = pl.BlockSpec(memory_space=pl.ANY)
    pairs = count * far * rank_size * rank_size
    return pl.pallas_call(
        far_sums_body,
        in_specs=[pl.BlockSpec(memory_space=pltpu.SMEM), whole, whole, anywhere, anywhere, anywhere],
        out_specs=whole,
        out_shape=jax.ShapeDtypeStruct((count, rank_size, cols), f32),
        scratch_shapes=[pltpu.VMEM((rank_size, far * rank_size), bf16)] * 2
        + [
            pltpu.VMEM((2, STREAM_STEP, rank_size, far * rank_size), bf16),
            pltpu.VMEM((points.shape[0], AUG, rank_size), bf16),
            pltpu.VMEM(weights.shape, bf16),
            pltpu.SemaphoreType.DMA((3,)),
        ],
        compiler_params=pltpu.CompilerParams(vmem_limit_bytes=58 * MIB),
        cost_estimate=pl.CostEstimate(
            flops=pairs * 2500, bytes_accessed=24 * 10**6, transcendentals=2 * pairs
        ),
        name="far_sums",
    )(lists, targets, points, weights, stored, after)


def upper_body(list_ref, own_ref, chip_ref, across_ref, after_ref, out_ref):
    dims, rank_size = own_ref.shape[1:]
    cols = out_ref.shape[2]
    batch = 4
    half = chip_ref.shape[0]

    def block_of(place):
        here = chip_ref[jnp.minimum(place, half - 1)]
        there = across_ref[jnp.maximum(place - half, 0)]
        return jnp.where(place < half, here, there)

    for c in range(own_ref.shape[0]):
        target = target_rows(*scaled_halves(own_ref[c]))
        total = jnp.zeros((rank_size, cols), f32)
        for q in range(0, list_ref.shape[1], batch):
            blocks = [block_of(list_ref[c, q + k]) for k in range(batch)]
            values = jnp.concatenate([x[:cols] for x in blocks], axis=1)
            points = jnp.concatenate([x[cols:].astype(f32)[:dims] for x in blocks], axis=1)
            kernel = matern(mm(target, source_rows(*scaled_halves(points))))
            total += mm(kernel, values, NT)
        out_ref[c] = total


def upper_sums(lists, own, chip, across, after):
    count, dims, rank_size = own.shape
    cols = chip.shape[1] - 2 * dims
    whole = pl.BlockSpec(memory_space=pltpu.VMEM)
    pairs = count * lists.shape[1] * rank_size * rank_size
    return pl.pallas_call(
        upper_body,
        in_specs=[pl.BlockSpec(memory_space=pltpu.SMEM), whole, whole, whole]
        + [pl.BlockSpec(memory_space=pl.ANY)],
        out_specs=whole,
        out_shape=jax.ShapeDtypeStruct((count, rank_size, cols), f32),
        compiler_params=pltpu.CompilerParams(vmem_limit_bytes=16 * MIB),
        cost_estimate=pl.CostEstimate(
            flops=pairs * 230, bytes_accessed=8 * 10**6, transcendentals=2 * pairs
        ),
        name="upper_sums",
    )(lists, own, chip, across, after)


def final_body(far_ref, upper_ref, transfer_ref, basis_ref, near_ref, out_ref):
    leaf_count, leaf_size, _ = basis_ref.shape
    step = 4

    def leaves(n, carry):
        upper = upper_ref[n * step // KIDS]
        for k in range(step):
            i = n * step + k
            skeleton = far_ref[i] + mm3(transfer_ref[i], upper)
            potential = mm3(basis_ref[i], skeleton) + near_ref[i]
            at = pl.ds(pl.multiple_of(i * leaf_size, leaf_size), leaf_size)
            out_ref[:, at] = jnp.transpose(potential)
        return carry

    lax.fori_loop(0, leaf_count // step, leaves, 0)


def final(far, upper, transfer, basis, near):
    leaf_count, leaf_size, rank_size = basis.shape
    cols = near.shape[2]
    whole = pl.BlockSpec(memory_space=pltpu.VMEM)
    return pl.pallas_call(
        final_body,
        in_specs=[whole] * 5,
        out_specs=whole,
        out_shape=jax.ShapeDtypeStruct((cols, leaf_count * leaf_size), f32),
        compiler_params=pltpu.CompilerParams(vmem_limit_bytes=20 * MIB),
        cost_estimate=pl.CostEstimate(flops=10**9, bytes_accessed=10**7, transcendentals=0),
        name="final",
    )(far, upper, transfer, basis, near)


def shifted(block, axis, move, count):
    return lax.ppermute(block, axis, [(i, move(i)) for i in range(count)])


def upper_places(clusters, count):
    owner = clusters // count
    group = owner % 16
    bulk = owner // 16
    mine = lax.axis_index("bulk")
    core = (bulk ^ mine) & 1
    hops = (bulk // 2 - mine // 2) & 3
    turn = hops
    return (((core * 4 + turn) * 16) + group) * count + clusters % count


def local(
    points,
    weights,
    leaf_order,
    basis,
    transfer,
    skel_leaf,
    skel_upper,
    near_list,
    leaf_interaction_list,
    far_upper,
):
    row_count = leaf_order.shape[0]
    group_count = lax.axis_size("group")
    bulk_count = lax.axis_size("bulk")
    device_count = group_count * bulk_count
    leaf_count = basis.shape[0]

    want, src, rank, tick = index_lists(leaf_order, group_count, basis.shape[1])
    scaled = skel_leaf.astype(f32) * POINT_SCALE + tick[0]
    subtree_points = lax.all_gather(scaled, "group", axis=0, tiled=True)
    wanted = lax.all_to_all(want, "group", split_axis=0, concat_axis=0, tiled=True)
    picked = pick(wanted, pick_table(points, weights), row_count)
    arrived = lax.all_to_all(picked, "group", split_axis=0, concat_axis=0, tiled=True)

    far_local = leaf_interaction_list - lax.axis_index("bulk") * (group_count * leaf_count)

    own = place(src, rank, arrived)
    skel_wb, upper_wb = skeleton(own, basis, transfer)
    sub_w = lax.all_gather(skel_wb, "group", axis=0, tiled=True)
    forward = [(i, i + 1) for i in range(device_count - 1)]
    backward = [(i + 1, i) for i in range(device_count - 1)]
    low = lax.ppermute(own, ("bulk", "group"), forward)
    high = lax.ppermute(own, ("bulk", "group"), backward)

    def joined(tick, *blocks):
        return jnp.concatenate(blocks, axis=0) + tick[0].astype(bf16)

    mine = jnp.concatenate([upper_wb, skel_upper, jnp.zeros(skel_upper.shape, bf16)], axis=1)
    copies = jnp.tile(mine, (group_count, 1, 1))
    block = lax.all_to_all(copies, "group", split_axis=0, concat_axis=0, tiled=True)
    part = leaf_count // 2
    kernels, tick = far_kernels(0, part, far_local, scaled, subtree_points, copies)
    block = joined(tick, block)
    ring = [shifted(block, "bulk", lambda i, hops=hops: (i - 2 * hops) % bulk_count, bulk_count) for hops in (1, 2, 3)]
    device = lax.axis_index(("bulk", "group"))
    near, tick = near_sums(near_list - (device - 1) * leaf_count, low, own, high, block)
    chip = joined(tick, block, *ring)
    other = shifted(chip, "bulk", lambda i: i ^ 1, bulk_count)
    far = far_sums(far_local, scaled, subtree_points, sub_w, kernels, chip)
    upper = upper_sums(upper_places(far_upper, skel_upper.shape[0]), skel_upper, chip, other, far)
    return final(far, upper, transfer, basis, near)


def solution(mesh):
    placed = (
        P(None, ("bulk", "group")),
        P(None, ("bulk", "group")),
        P(("bulk", "group")),
        P(("bulk", "group"), None, None),
        P(("bulk", "group"), None, None),
        P(("bulk", "group"), None, None),
        P(("bulk", "group"), None, None),
        P(("bulk", "group"), None),
        P(("bulk", "group"), None),
        P(("bulk", "group"), None),
    )
    return jax.shard_map(
        local, mesh=mesh, in_specs=placed, out_specs=P(None, ("bulk", "group")), check_vma=False
    )
```

```python
import functools
import math

import jax
import jax.numpy as jnp
from jax import lax
from jax.experimental import pallas as pl
from jax.experimental.pallas import tpu as pltpu
from jax.sharding import PartitionSpec as P

KIDS = 8

POINT_SCALE = math.sqrt(5.0) / 2.0 / math.log(2.0)
POLY_A = 3.0 / math.log(2.0)
POLY_B = 3.0 / math.log(2.0) ** 2
POLY_LOG = math.log2(math.log(2.0) ** 2 / 3.0)
AUG = 48
MIB = 1024 * 1024

f32 = jnp.float32
bf16 = jnp.bfloat16
TICK = jax.ShapeDtypeStruct((8, 128), f32)
NN = (((1,), (0,)), ((), ()))
NT = (((1,), (1,)), ((), ()))


def mm(a, b, dims=NN):
    return lax.dot_general(a, b, dims, preferred_element_type=f32)


def halves(x):
    high = x.astype(bf16)
    return high, (x - high.astype(f32)).astype(bf16)


def mm3(a, b):
    a_high, a_low = halves(a)
    b_high, b_low = halves(b)
    return mm(a_high, b_high) + (mm(a_high, b_low) + mm(a_low, b_high))


def squares(high, low):
    x = high + low
    norm = jnp.sum(x * x, axis=0, keepdims=True)
    first = norm.astype(bf16).astype(f32)
    second = (norm - first).astype(bf16).astype(f32)
    third = norm - first - second
    row = lax.broadcasted_iota(jnp.int32, high.shape, 0)
    parts = jnp.where(row % 3 == 0, first, jnp.where(row % 3 == 1, second, third))
    return row, parts


def source_rows(high, low):
    row, parts = squares(high, low)
    last = jnp.where(row < 3, 1.0, jnp.where(row < 6, parts, 0.0))
    high, low = -2.0 * high, -2.0 * low
    return jnp.concatenate([high, low, high, low, last, jnp.zeros_like(last)], axis=0).astype(bf16)


def target_rows(high, low):
    row, parts = squares(high, low)
    last = jnp.where(row < 3, parts, jnp.where(row < 6, 1.0, 0.0))
    rows = jnp.concatenate([high, high, low, low, last, jnp.zeros_like(last)], axis=0)
    return jnp.transpose(rows).astype(bf16)


def f32_halves(points):
    high, low = halves(points)
    return high.astype(f32), low.astype(f32)


def scaled_halves(points):
    return f32_halves(points.astype(f32) * POINT_SCALE)


def matern(square):
    square = jnp.maximum(square, 1e-30)
    t = square * lax.rsqrt(square)
    return (((t + POLY_A) * t + POLY_B) * jnp.exp2(POLY_LOG - t)).astype(bf16)


def index_body(order_ref, want_ref, src_ref, rank_ref, tick_ref):
    tick_ref[...] = jnp.zeros_like(tick_ref)
    group_count, _, pair = want_ref.shape
    lines = order_ref.shape[0]
    row_count = group_count * pair
    order = order_ref[...]
    owner = ((order.astype(f32) + 0.5) * (1.0 / row_count)).astype(jnp.int32)
    src = owner % group_count
    row = order - owner * row_count
    before = (
        lax.broadcasted_iota(jnp.int32, (128, 128), 0)
        < lax.broadcasted_iota(jnp.int32, (128, 128), 1)
    ).astype(f32).astype(bf16)
    above = (
        lax.broadcasted_iota(jnp.int32, (lines, lines), 1)
        < lax.broadcasted_iota(jnp.int32, (lines, lines), 0)
    ).astype(f32).astype(bf16)
    all_ones = jnp.ones((128, 128), bf16)
    rank = jnp.zeros(src.shape, f32)
    for g in range(group_count):
        here = src == g
        mask = here.astype(f32).astype(bf16)
        total = mm(mask, all_ones).astype(bf16)
        rank = jnp.where(here, mm(mask, before) + mm(above, total), rank)
    rank = rank.astype(jnp.int32)
    for i in range(lines // 2):
        for ref, x in ((src_ref, src), (rank_ref, rank)):
            ref[i] = jnp.concatenate([x[2 * i : 2 * i + 1], x[2 * i + 1 : 2 * i + 2]], axis=1)
    place = lax.broadcasted_iota(jnp.int32, (pair, 256), 0)
    owner = lax.broadcasted_iota(jnp.int32, (group_count, 256), 0)
    total = jnp.zeros((2 * group_count, pair), f32)
    for k in range(0, lines, 2):
        line = lambda x: jnp.concatenate([x[k : k + 1], x[k + 1 : k + 2]], axis=1)
        rank_line, src_line, row_line = line(rank), line(src), line(row)
        spots = (place == rank_line).astype(f32).astype(bf16)
        mine = owner == src_line
        high = jnp.where(mine, (row_line >> 7).astype(f32), 0.0)
        low = jnp.where(mine, (row_line & 127).astype(f32), 0.0)
        total += mm(jnp.concatenate([high, low], axis=0).astype(bf16), spots, NT)
    want = (total[:group_count] * 128.0 + total[group_count:]).astype(jnp.int32)
    for g in range(group_count):
        want_ref[g] = want[g : g + 1]


def index_lists(order, group_count, leaf_size):
    row_count = order.shape[0]
    assert leaf_size == 256
    return pl.pallas_call(
        index_body,
        out_shape=(
            jax.ShapeDtypeStruct((group_count, 1, row_count // group_count), jnp.int32),
            jax.ShapeDtypeStruct((row_count // leaf_size, 1, leaf_size), jnp.int32),
            jax.ShapeDtypeStruct((row_count // leaf_size, 1, leaf_size), jnp.int32),
            TICK,
        ),
        compiler_params=pltpu.CompilerParams(vmem_limit_bytes=8 * MIB),
        cost_estimate=pl.CostEstimate(flops=2 * 10**9, bytes_accessed=10**5, transcendentals=0),
        name="index_lists",
    )(order.reshape(-1, 128))


def table_body(points_ref, weights_ref, table_ref):
    height = weights_ref.shape[0] + 2 * points_ref.shape[0]
    for h in range(points_ref.shape[1] // 256):
        at = slice(h * 256, (h + 1) * 256)
        high, low = scaled_halves(points_ref[:, at])
        table_ref[h * height : (h + 1) * height, :] = jnp.concatenate(
            [weights_ref[:, at], high, low], axis=0
        ).astype(bf16)


def pick_table(points, weights):
    height = weights.shape[0] + 2 * points.shape[0]
    whole = pl.BlockSpec(memory_space=pltpu.VMEM)
    return pl.pallas_call(
        table_body,
        in_specs=[whole, whole],
        out_specs=whole,
        out_shape=jax.ShapeDtypeStruct((points.shape[1] // 256 * height, 256), bf16),
        compiler_params=pltpu.CompilerParams(vmem_limit_bytes=10 * MIB),
        cost_estimate=pl.CostEstimate(flops=3 * 10**9, bytes_accessed=3 * 10**6, transcendentals=0),
        name="pick_table",
    )(points, weights)


def pick_body(want_ref, table_ref, out_ref):
    group_count, height, pair = out_ref.shape
    high_count = table_ref.shape[0] // height
    batch = 8

    def devices(d, carry):
        want = jnp.concatenate([want_ref[2 * d], want_ref[2 * d + 1]], axis=1)
        low = want & 255
        high = want >> 8
        spots = (lax.broadcasted_iota(jnp.int32, (256, 2 * pair), 0) == low).astype(f32).astype(bf16)
        picked = jnp.zeros((height, 2 * pair), f32)
        for h in range(0, high_count, batch):
            found = mm(table_ref[h * height : (h + batch) * height, :], spots)
            for k in range(batch):
                picked = jnp.where(high == h + k, found[k * height : (k + 1) * height], picked)
        picked = picked.astype(bf16)
        out_ref[2 * d] = picked[:, :pair]
        out_ref[2 * d + 1] = picked[:, pair:]
        return carry

    lax.fori_loop(0, group_count // 2, devices, 0)


def pick(want, table, row_count):
    group_count, _, pair = want.shape
    height = table.shape[0] * 256 // row_count
    whole = pl.BlockSpec(memory_space=pltpu.VMEM)
    return pl.pallas_call(
        pick_body,
        in_specs=[whole, whole],
        out_specs=whole,
        out_shape=jax.ShapeDtypeStruct((group_count, height, pair), bf16),
        compiler_params=pltpu.CompilerParams(vmem_limit_bytes=16 * MIB),
        cost_estimate=pl.CostEstimate(flops=6 * 10**9, bytes_accessed=3 * 10**6, transcendentals=0),
        name="pick",
    )(want, table)


def place_body(src_ref, rank_ref, arrived_ref, leaf_ref, table):
    leaf_count, height, leaf_size = leaf_ref.shape
    pair = arrived_ref.shape[1]
    group_count = arrived_ref.shape[0] // height
    lines = table.shape[0] // height
    pieces = 2 * lines // group_count
    batch = 4
    step = 4
    for g in range(0, group_count, 2):
        two = jnp.concatenate(
            [arrived_ref[(g + k) * height : (g + k + 1) * height, :] for k in range(2)], axis=1
        )
        for k in range(pieces):
            at = (g // 2 * pieces + k) * height
            table[at : at + height, :] = two[:, k * 256 : (k + 1) * 256]

    def leaves(c, carry):
        for n in range(step):
            i = c * step + n
            slot = src_ref[i] * pair + rank_ref[i]
            low = slot & 255
            high = slot >> 8
            spots = (
                lax.broadcasted_iota(jnp.int32, (256, leaf_size), 0) == low
            ).astype(f32).astype(bf16)
            placed = jnp.zeros((height, leaf_size), f32)
            for h in range(0, lines, batch):
                found = mm(table[h * height : (h + batch) * height, :], spots)
                for k in range(batch):
                    placed = jnp.where(high == h + k, found[k * height : (k + 1) * height], placed)
            leaf_ref[i] = placed.astype(bf16)
        return carry

    lax.fori_loop(0, leaf_count // step, leaves, 0)


def place(src, rank, arrived):
    group_count, height, pair = arrived.shape
    leaf_count, _, leaf_size = src.shape
    whole = pl.BlockSpec(memory_space=pltpu.VMEM)
    return pl.pallas_call(
        place_body,
        in_specs=[whole] * 3,
        out_specs=whole,
        out_shape=jax.ShapeDtypeStruct((leaf_count, height, leaf_size), bf16),
        scratch_shapes=[pltpu.VMEM((group_count * pair // 256 * height, 256), bf16)],
        compiler_params=pltpu.CompilerParams(vmem_limit_bytes=14 * MIB),
        cost_estimate=pl.CostEstimate(flops=8 * 10**9, bytes_accessed=2 * 10**6, transcendentals=0),
        name="place",
    )(src, rank, arrived.reshape(group_count * height, pair))


def skeleton_body(leaf_ref, basis_ref, transfer_ref, skel_ref, upper_ref):
    leaf_count, cols, _ = skel_ref.shape

    def cluster(c, carry):
        total = jnp.zeros(upper_ref.shape[1:], f32)
        for n in range(KIDS):
            i = c * KIDS + n
            values = leaf_ref[i, :cols]
            basis_high, basis_low = halves(basis_ref[i])
            skel = mm(values, basis_high) + mm(values, basis_low)
            skel_ref[i] = skel.astype(bf16)
            total += mm3(skel, transfer_ref[i])
        upper_ref[c] = total.astype(bf16)
        return carry

    lax.fori_loop(0, leaf_count // KIDS, cluster, 0)


def skeleton(leaves, basis, transfer):
    leaf_count, _, rank_size = basis.shape
    cols = leaves.shape[1] - 16
    whole = pl.BlockSpec(memory_space=pltpu.VMEM)
    return pl.pallas_call(
        skeleton_body,
        in_specs=[whole] * 3,
        out_specs=(whole, whole),
        out_shape=(
            jax.ShapeDtypeStruct((leaf_count, cols, rank_size), bf16),
            jax.ShapeDtypeStruct((leaf_count // KIDS, cols, rank_size), bf16),
        ),
        compiler_params=pltpu.CompilerParams(vmem_limit_bytes=14 * MIB),
        cost_estimate=pl.CostEstimate(flops=10**9, bytes_accessed=7 * 10**6, transcendentals=0),
        name="skeleton",
    )(leaves, basis, transfer)


def near_body(list_ref, low_ref, own_ref, high_ref, after_ref, out_ref, tick_ref, rows, values):
    tick_ref[...] = jnp.zeros_like(tick_ref)
    leaf_count, height, leaf_size = own_ref.shape
    cols = height - 16
    for part, ref in enumerate((low_ref, own_ref, high_ref)):

        def fill(n, carry, part=part, ref=ref):
            values[part * leaf_count + n] = ref[n, :cols]
            tail = ref[n, cols:].astype(f32)
            rows[part * leaf_count + n] = source_rows(tail[:8], tail[8:])
            return carry

        lax.fori_loop(0, leaf_count, fill, 0)

    def leaf(i, carry):
        tail = own_ref[i, cols:].astype(f32)
        target = target_rows(tail[:8], tail[8:])
        total = jnp.zeros((leaf_size, cols), f32)
        for q in range(list_ref.shape[1]):
            j = list_ref[i, q]
            total += mm(matern(mm(target, rows[j])), values[j], NT)
        out_ref[i] = total
        return carry

    lax.fori_loop(0, leaf_count, leaf, 0)


def near_sums(lists, low, own, high, after):
    leaf_count, near = lists.shape
    height, leaf_size = own.shape[1:]
    cols = height - 16
    whole = pl.BlockSpec(memory_space=pltpu.VMEM)
    pairs = leaf_count * near * leaf_size * leaf_size
    return pl.pallas_call(
        near_body,
        in_specs=[pl.BlockSpec(memory_space=pltpu.SMEM), whole, whole, whole]
        + [pl.BlockSpec(memory_space=pl.ANY)],
        out_specs=(whole, whole),
        out_shape=(jax.ShapeDtypeStruct((leaf_count, leaf_size, cols), f32), TICK),
        scratch_shapes=[
            pltpu.VMEM((3 * leaf_count, AUG, leaf_size), bf16),
            pltpu.VMEM((3 * leaf_count, cols, leaf_size), bf16),
        ],
        compiler_params=pltpu.CompilerParams(vmem_limit_bytes=20 * MIB),
        cost_estimate=pl.CostEstimate(
            flops=pairs * 2500, bytes_accessed=6 * 10**6, transcendentals=2 * pairs
        ),
        name="near_sums",
    )(lists, low, own, high, after)


def fill_rows(points_ref, rows_ref):
    step = 8

    def fill(n, carry):
        for k in range(step):
            rows_ref[n * step + k] = source_rows(*f32_halves(points_ref[n * step + k]))
        return carry

    lax.fori_loop(0, rows_ref.shape[0] // step, fill, 0)


FAR_STEP = 4


def far_body(first, after_count, list_ref, target_ref, points_ref, *refs):
    out_ref, tick_ref, rows_ref = refs[after_count:]

    @pl.when(pl.program_id(0) == 0)
    def _():
        fill_rows(points_ref, rows_ref)

    rank_size = rows_ref.shape[2]
    far = list_ref.shape[1]
    batch = 4
    for n in range(FAR_STEP):
        i = first + pl.program_id(0) * FAR_STEP + n
        target = target_rows(*f32_halves(target_ref[i]))
        for q in range(0, far, batch):
            rows = jnp.concatenate([rows_ref[list_ref[i, q + k]] for k in range(batch)], axis=1)
            out_ref[n, :, q * rank_size : (q + batch) * rank_size] = matern(mm(target, rows))
    tick_ref[...] = jnp.zeros_like(tick_ref)


def far_kernels(first, count, lists, targets, points, *after):
    far = lists.shape[1]
    rank_size = points.shape[2]
    pairs = count * far * rank_size * rank_size
    anywhere = pl.BlockSpec(memory_space=pl.ANY)
    return pl.pallas_call(
        functools.partial(far_body, first, len(after)),
        grid_spec=pltpu.PrefetchScalarGridSpec(
            num_scalar_prefetch=1,
            grid=(count // FAR_STEP,),
            in_specs=[
                pl.BlockSpec(targets.shape, lambda i, s: (0, 0, 0)),
                pl.BlockSpec(points.shape, lambda i, s: (0, 0, 0)),
            ]
            + [anywhere] * len(after),
            out_specs=(
                pl.BlockSpec((FAR_STEP, rank_size, far * rank_size), lambda i, s: (i, 0, 0)),
                pl.BlockSpec(TICK.shape, lambda i, s: (0, 0)),
            ),
            scratch_shapes=[pltpu.VMEM((points.shape[0], AUG, rank_size), bf16)],
        ),
        out_shape=(jax.ShapeDtypeStruct((count, rank_size, far * rank_size), bf16), TICK),
        compiler_params=pltpu.CompilerParams(vmem_limit_bytes=52 * MIB),
        cost_estimate=pl.CostEstimate(
            flops=pairs * 20, bytes_accessed=10**6, transcendentals=0
        ),
        name="far_kernels",
    )(lists, targets, points, *after)


STREAM_STEP = 4


def far_sums_body(
    list_ref, target_ref, points_ref, gathered_ref, stored_ref, after_ref, out_ref, even, odd, stream, rows_ref, weights_ref, sems
):
    early = stored_ref.shape[0]
    late = out_ref.shape[0] - early
    rank_size = weights_ref.shape[2]
    far = list_ref.shape[1]
    batch = 4
    blocks = early // STREAM_STEP
    copies = [
        pltpu.make_async_copy(
            stored_ref.at[pl.ds(k * STREAM_STEP, STREAM_STEP)], stream.at[k % 2], sems.at[k % 2]
        )
        for k in range(blocks)
    ]

    def listed(ref, i, q, n):
        return jnp.concatenate([ref[list_ref[i, q + k]] for k in range(n)], axis=1)

    def fill(i, kernel):
        target = target_rows(*f32_halves(target_ref[i]))
        for q in range(0, far, batch):
            kernel[:, q * rank_size : (q + batch) * rank_size] = matern(
                mm(target, listed(rows_ref, i, q, batch))
            )

    def apply(i, kernel):
        out_ref[i] = mm(kernel, listed(weights_ref, i, 0, far), NT)

    weights_copy = pltpu.make_async_copy(gathered_ref, weights_ref, sems.at[2])
    weights_copy.start()
    for copy in copies[:2]:
        copy.start()
    fill_rows(points_ref, rows_ref)
    fill(early, even)
    weights_copy.wait()

    def two(n, carry):
        i = early + 2 * n
        fill(i + 1, odd)
        apply(i, even[...])
        fill(jnp.minimum(i + 2, early + late - 1), even)
        apply(i + 1, odd[...])
        return carry

    lax.fori_loop(0, late // 2, two, 0)
    for k, copy in enumerate(copies):
        copy.wait()
        for n in range(STREAM_STEP):
            apply(k * STREAM_STEP + n, stream[k % 2, n])
        if k + 2 < blocks:
            copies[k + 2].start()


def far_sums(lists, targets, points, weights, stored, after):
    count, far = lists.shape
    cols, rank_size = weights.shape[1:]
    whole = pl.BlockSpec(memory_space=pltpu.VMEM)
    anywhere = pl.BlockSpec(memory_space=pl.ANY)
    pairs = count * far * rank_size * rank_size
    return pl.pallas_call(
        far_sums_body,
        in_specs=[pl.BlockSpec(memory_space=pltpu.SMEM), whole, whole, anywhere, anywhere, anywhere],
        out_specs=whole,
        out_shape=jax.ShapeDtypeStruct((count, rank_size, cols), f32),
        scratch_shapes=[pltpu.VMEM((rank_size, far * rank_size), bf16)] * 2
        + [
            pltpu.VMEM((2, STREAM_STEP, rank_size, far * rank_size), bf16),
            pltpu.VMEM((points.shape[0], AUG, rank_size), bf16),
            pltpu.VMEM(weights.shape, bf16),
            pltpu.SemaphoreType.DMA((3,)),
        ],
        compiler_params=pltpu.CompilerParams(vmem_limit_bytes=58 * MIB),
        cost_estimate=pl.CostEstimate(
            flops=pairs * 2500, bytes_accessed=24 * 10**6, transcendentals=2 * pairs
        ),
        name="far_sums",
    )(lists, targets, points, weights, stored, after)


def upper_body(list_ref, own_ref, chip_ref, across_ref, after_ref, out_ref):
    dims, rank_size = own_ref.shape[1:]
    cols = out_ref.shape[2]
    batch = 4
    half = chip_ref.shape[0]

    def block_of(place):
        here = chip_ref[jnp.minimum(place, half - 1)]
        there = across_ref[jnp.maximum(place - half, 0)]
        return jnp.where(place < half, here, there)

    for c in range(own_ref.shape[0]):
        target = target_rows(*scaled_halves(own_ref[c]))
        total = jnp.zeros((rank_size, cols), f32)
        for q in range(0, list_ref.shape[1], batch):
            blocks = [block_of(list_ref[c, q + k]) for k in range(batch)]
            values = jnp.concatenate([x[:cols] for x in blocks], axis=1)
            points = jnp.concatenate([x[cols:].astype(f32)[:dims] for x in blocks], axis=1)
            kernel = matern(mm(target, source_rows(*scaled_halves(points))))
            total += mm(kernel, values, NT)
        out_ref[c] = total


def upper_sums(lists, own, chip, across, after):
    count, dims, rank_size = own.shape
    cols = chip.shape[1] - 2 * dims
    whole = pl.BlockSpec(memory_space=pltpu.VMEM)
    pairs = count * lists.shape[1] * rank_size * rank_size
    return pl.pallas_call(
        upper_body,
        in_specs=[pl.BlockSpec(memory_space=pltpu.SMEM), whole, whole, whole]
        + [pl.BlockSpec(memory_space=pl.ANY)],
        out_specs=whole,
        out_shape=jax.ShapeDtypeStruct((count, rank_size, cols), f32),
        compiler_params=pltpu.CompilerParams(vmem_limit_bytes=16 * MIB),
        cost_estimate=pl.CostEstimate(
            flops=pairs * 230, bytes_accessed=8 * 10**6, transcendentals=2 * pairs
        ),
        name="upper_sums",
    )(lists, own, chip, across, after)


def final_body(far_ref, upper_ref, transfer_ref, basis_ref, near_ref, out_ref):
    leaf_count, leaf_size, _ = basis_ref.shape
    step = 4

    def leaves(n, carry):
        upper = upper_ref[n * step // KIDS]
        for k in range(step):
            i = n * step + k
            skeleton = far_ref[i] + mm3(transfer_ref[i], upper)
            potential = mm3(basis_ref[i], skeleton) + near_ref[i]
            at = pl.ds(pl.multiple_of(i * leaf_size, leaf_size), leaf_size)
            out_ref[:, at] = jnp.transpose(potential)
        return carry

    lax.fori_loop(0, leaf_count // step, leaves, 0)


def final(far, upper, transfer, basis, near):
    leaf_count, leaf_size, rank_size = basis.shape
    cols = near.shape[2]
    whole = pl.BlockSpec(memory_space=pltpu.VMEM)
    return pl.pallas_call(
        final_body,
        in_specs=[whole] * 5,
        out_specs=whole,
        out_shape=jax.ShapeDtypeStruct((cols, leaf_count * leaf_size), f32),
        compiler_params=pltpu.CompilerParams(vmem_limit_bytes=20 * MIB),
        cost_estimate=pl.CostEstimate(flops=10**9, bytes_accessed=10**7, transcendentals=0),
        name="final",
    )(far, upper, transfer, basis, near)


def shifted(block, axis, move, count):
    return lax.ppermute(block, axis, [(i, move(i)) for i in range(count)])


def upper_places(clusters, count):
    owner = clusters // count
    group = owner % 16
    bulk = owner // 16
    mine = lax.axis_index("bulk")
    core = (bulk ^ mine) & 1
    hops = (bulk // 2 - mine // 2) & 3
    turn = hops
    return (((core * 4 + turn) * 16) + group) * count + clusters % count


def local(
    points,
    weights,
    leaf_order,
    basis,
    transfer,
    skel_leaf,
    skel_upper,
    near_list,
    leaf_interaction_list,
    far_upper,
):
    row_count = leaf_order.shape[0]
    group_count = lax.axis_size("group")
    bulk_count = lax.axis_size("bulk")
    device_count = group_count * bulk_count
    leaf_count = basis.shape[0]

    want, src, rank, tick = index_lists(leaf_order, group_count, basis.shape[1])
    scaled = skel_leaf.astype(f32) * POINT_SCALE + tick[0]
    subtree_points = lax.all_gather(scaled, "group", axis=0, tiled=True)
    wanted = lax.all_to_all(want, "group", split_axis=0, concat_axis=0, tiled=True)
    picked = pick(wanted, pick_table(points, weights), row_count)
    arrived = lax.all_to_all(picked, "group", split_axis=0, concat_axis=0, tiled=True)

    far_local = leaf_interaction_list - lax.axis_index("bulk") * (group_count * leaf_count)

    own = place(src, rank, arrived)
    skel_wb, upper_wb = skeleton(own, basis, transfer)
    sub_w = lax.all_gather(skel_wb, "group", axis=0, tiled=True)
    forward = [(i, i + 1) for i in range(device_count - 1)]
    backward = [(i + 1, i) for i in range(device_count - 1)]
    low = lax.ppermute(own, ("bulk", "group"), forward)
    high = lax.ppermute(own, ("bulk", "group"), backward)

    def joined(tick, *blocks):
        return jnp.concatenate(blocks, axis=0) + tick[0].astype(bf16)

    mine = jnp.concatenate([upper_wb, skel_upper, jnp.zeros(skel_upper.shape, bf16)], axis=1)
    copies = jnp.tile(mine, (group_count, 1, 1))
    block = lax.all_to_all(copies, "group", split_axis=0, concat_axis=0, tiled=True)
    part = leaf_count // 2
    kernels, tick = far_kernels(0, part, far_local, scaled, subtree_points, copies)
    block = joined(tick, block)
    ring = [shifted(block, "bulk", lambda i, hops=hops: (i - 2 * hops) % bulk_count, bulk_count) for hops in (1, 2, 3)]
    device = lax.axis_index(("bulk", "group"))
    near, tick = near_sums(near_list - (device - 1) * leaf_count, low, own, high, block)
    chip = joined(tick, block, *ring)
    other = shifted(chip, "bulk", lambda i: i ^ 1, bulk_count)
    far = far_sums(far_local, scaled, subtree_points, sub_w, kernels, chip)
    upper = upper_sums(upper_places(far_upper, skel_upper.shape[0]), skel_upper, chip, other, far)
    return final(far, upper, transfer, basis, near)


def solution(mesh):
    placed = (
        P(None, ("bulk", "group")),
        P(None, ("bulk", "group")),
        P(("bulk", "group")),
        P(("bulk", "group"), None, None),
        P(("bulk", "group"), None, None),
        P(("bulk", "group"), None, None),
        P(("bulk", "group"), None, None),
        P(("bulk", "group"), None),
        P(("bulk", "group"), None),
        P(("bulk", "group"), None),
    )
    return jax.shard_map(
        local, mesh=mesh, in_specs=placed, out_specs=P(None, ("bulk", "group")), check_vma=False
    )
```

```python
import functools
import math

import jax
import jax.numpy as jnp
from jax import lax
from jax.experimental import pallas as pl
from jax.experimental.pallas import tpu as pltpu
from jax.sharding import PartitionSpec as P

KIDS = 8

POINT_SCALE = math.sqrt(5.0) / 2.0 / math.log(2.0)
POLY_A = 3.0 / math.log(2.0)
POLY_B = 3.0 / math.log(2.0) ** 2
POLY_LOG = math.log2(math.log(2.0) ** 2 / 3.0)
AUG = 48
MIB = 1024 * 1024

f32 = jnp.float32
bf16 = jnp.bfloat16
TICK = jax.ShapeDtypeStruct((8, 128), f32)
NN = (((1,), (0,)), ((), ()))
NT = (((1,), (1,)), ((), ()))


def mm(a, b, dims=NN):
    return lax.dot_general(a, b, dims, preferred_element_type=f32)


def halves(x):
    high = x.astype(bf16)
    return high, (x - high.astype(f32)).astype(bf16)


def mm3(a, b):
    a_high, a_low = halves(a)
    b_high, b_low = halves(b)
    return mm(a_high, b_high) + (mm(a_high, b_low) + mm(a_low, b_high))


def squares(high, low):
    x = high + low
    norm = jnp.sum(x * x, axis=0, keepdims=True)
    first = norm.astype(bf16).astype(f32)
    second = (norm - first).astype(bf16).astype(f32)
    third = norm - first - second
    row = lax.broadcasted_iota(jnp.int32, high.shape, 0)
    parts = jnp.where(row % 3 == 0, first, jnp.where(row % 3 == 1, second, third))
    return row, parts


def source_rows(high, low):
    row, parts = squares(high, low)
    last = jnp.where(row < 3, 1.0, jnp.where(row < 6, parts, 0.0))
    high, low = -2.0 * high, -2.0 * low
    return jnp.concatenate([high, low, high, low, last, jnp.zeros_like(last)], axis=0).astype(bf16)


def target_rows(high, low):
    row, parts = squares(high, low)
    last = jnp.where(row < 3, parts, jnp.where(row < 6, 1.0, 0.0))
    rows = jnp.concatenate([high, high, low, low, last, jnp.zeros_like(last)], axis=0)
    return jnp.transpose(rows).astype(bf16)


def f32_halves(points):
    high, low = halves(points)
    return high.astype(f32), low.astype(f32)


def scaled_halves(points):
    return f32_halves(points.astype(f32) * POINT_SCALE)


def matern(square):
    square = jnp.maximum(square, 1e-30)
    t = square * lax.rsqrt(square)
    return (((t + POLY_A) * t + POLY_B) * jnp.exp2(POLY_LOG - t)).astype(bf16)


def index_body(order_ref, want_ref, src_ref, rank_ref, tick_ref):
    tick_ref[...] = jnp.zeros_like(tick_ref)
    group_count, _, pair = want_ref.shape
    lines = order_ref.shape[0]
    row_count = group_count * pair
    order = order_ref[...]
    owner = ((order.astype(f32) + 0.5) * (1.0 / row_count)).astype(jnp.int32)
    src = owner % group_count
    row = order - owner * row_count
    before = (
        lax.broadcasted_iota(jnp.int32, (128, 128), 0)
        < lax.broadcasted_iota(jnp.int32, (128, 128), 1)
    ).astype(f32).astype(bf16)
    above = (
        lax.broadcasted_iota(jnp.int32, (lines, lines), 1)
        < lax.broadcasted_iota(jnp.int32, (lines, lines), 0)
    ).astype(f32).astype(bf16)
    all_ones = jnp.ones((128, 128), bf16)
    rank = jnp.zeros(src.shape, f32)
    for g in range(group_count):
        here = src == g
        mask = here.astype(f32).astype(bf16)
        total = mm(mask, all_ones).astype(bf16)
        rank = jnp.where(here, mm(mask, before) + mm(above, total), rank)
    rank = rank.astype(jnp.int32)
    for i in range(lines // 2):
        for ref, x in ((src_ref, src), (rank_ref, rank)):
            ref[i] = jnp.concatenate([x[2 * i : 2 * i + 1], x[2 * i + 1 : 2 * i + 2]], axis=1)
    place = lax.broadcasted_iota(jnp.int32, (pair, 256), 0)
    owner = lax.broadcasted_iota(jnp.int32, (group_count, 256), 0)
    total = jnp.zeros((2 * group_count, pair), f32)
    for k in range(0, lines, 2):
        line = lambda x: jnp.concatenate([x[k : k + 1], x[k + 1 : k + 2]], axis=1)
        rank_line, src_line, row_line = line(rank), line(src), line(row)
        spots = (place == rank_line).astype(f32).astype(bf16)
        mine = owner == src_line
        high = jnp.where(mine, (row_line >> 7).astype(f32), 0.0)
        low = jnp.where(mine, (row_line & 127).astype(f32), 0.0)
        total += mm(jnp.concatenate([high, low], axis=0).astype(bf16), spots, NT)
    want = (total[:group_count] * 128.0 + total[group_count:]).astype(jnp.int32)
    for g in range(group_count):
        want_ref[g] = want[g : g + 1]


def index_lists(order, group_count, leaf_size):
    row_count = order.shape[0]
    assert leaf_size == 256
    return pl.pallas_call(
        index_body,
        out_shape=(
            jax.ShapeDtypeStruct((group_count, 1, row_count // group_count), jnp.int32),
            jax.ShapeDtypeStruct((row_count // leaf_size, 1, leaf_size), jnp.int32),
            jax.ShapeDtypeStruct((row_count // leaf_size, 1, leaf_size), jnp.int32),
            TICK,
        ),
        compiler_params=pltpu.CompilerParams(vmem_limit_bytes=8 * MIB),
        cost_estimate=pl.CostEstimate(flops=2 * 10**9, bytes_accessed=10**5, transcendentals=0),
        name="index_lists",
    )(order.reshape(-1, 128))


def table_body(points_ref, weights_ref, table_ref):
    height = weights_ref.shape[0] + 2 * points_ref.shape[0]
    for h in range(points_ref.shape[1] // 256):
        at = slice(h * 256, (h + 1) * 256)
        high, low = scaled_halves(points_ref[:, at])
        table_ref[h * height : (h + 1) * height, :] = jnp.concatenate(
            [weights_ref[:, at], high, low], axis=0
        ).astype(bf16)


def pick_table(points, weights):
    height = weights.shape[0] + 2 * points.shape[0]
    whole = pl.BlockSpec(memory_space=pltpu.VMEM)
    return pl.pallas_call(
        table_body,
        in_specs=[whole, whole],
        out_specs=whole,
        out_shape=jax.ShapeDtypeStruct((points.shape[1] // 256 * height, 256), bf16),
        compiler_params=pltpu.CompilerParams(vmem_limit_bytes=10 * MIB),
        cost_estimate=pl.CostEstimate(flops=3 * 10**9, bytes_accessed=3 * 10**6, transcendentals=0),
        name="pick_table",
    )(points, weights)


def pick_body(want_ref, table_ref, out_ref):
    group_count, height, pair = out_ref.shape
    high_count = table_ref.shape[0] // height
    batch = 8

    def devices(d, carry):
        want = jnp.concatenate([want_ref[2 * d], want_ref[2 * d + 1]], axis=1)
        low = want & 255
        high = want >> 8
        spots = (lax.broadcasted_iota(jnp.int32, (256, 2 * pair), 0) == low).astype(f32).astype(bf16)
        picked = jnp.zeros((height, 2 * pair), f32)
        for h in range(0, high_count, batch):
            found = mm(table_ref[h * height : (h + batch) * height, :], spots)
            for k in range(batch):
                picked = jnp.where(high == h + k, found[k * height : (k + 1) * height], picked)
        picked = picked.astype(bf16)
        out_ref[2 * d] = picked[:, :pair]
        out_ref[2 * d + 1] = picked[:, pair:]
        return carry

    lax.fori_loop(0, group_count // 2, devices, 0)


def pick(want, table, row_count):
    group_count, _, pair = want.shape
    height = table.shape[0] * 256 // row_count
    whole = pl.BlockSpec(memory_space=pltpu.VMEM)
    return pl.pallas_call(
        pick_body,
        in_specs=[whole, whole],
        out_specs=whole,
        out_shape=jax.ShapeDtypeStruct((group_count, height, pair), bf16),
        compiler_params=pltpu.CompilerParams(vmem_limit_bytes=16 * MIB),
        cost_estimate=pl.CostEstimate(flops=6 * 10**9, bytes_accessed=3 * 10**6, transcendentals=0),
        name="pick",
    )(want, table)


def place_body(src_ref, rank_ref, arrived_ref, leaf_ref, table):
    leaf_count, height, leaf_size = leaf_ref.shape
    pair = arrived_ref.shape[1]
    group_count = arrived_ref.shape[0] // height
    lines = table.shape[0] // height
    pieces = 2 * lines // group_count
    batch = 4
    step = 4
    for g in range(0, group_count, 2):
        two = jnp.concatenate(
            [arrived_ref[(g + k) * height : (g + k + 1) * height, :] for k in range(2)], axis=1
        )
        for k in range(pieces):
            at = (g // 2 * pieces + k) * height
            table[at : at + height, :] = two[:, k * 256 : (k + 1) * 256]

    def leaves(c, carry):
        for n in range(step):
            i = c * step + n
            slot = src_ref[i] * pair + rank_ref[i]
            low = slot & 255
            high = slot >> 8
            spots = (
                lax.broadcasted_iota(jnp.int32, (256, leaf_size), 0) == low
            ).astype(f32).astype(bf16)
            placed = jnp.zeros((height, leaf_size), f32)
            for h in range(0, lines, batch):
                found = mm(table[h * height : (h + batch) * height, :], spots)
                for k in range(batch):
                    placed = jnp.where(high == h + k, found[k * height : (k + 1) * height], placed)
            leaf_ref[i] = placed.astype(bf16)
        return carry

    lax.fori_loop(0, leaf_count // step, leaves, 0)


def place(src, rank, arrived):
    group_count, height, pair = arrived.shape
    leaf_count, _, leaf_size = src.shape
    whole = pl.BlockSpec(memory_space=pltpu.VMEM)
    return pl.pallas_call(
        place_body,
        in_specs=[whole] * 3,
        out_specs=whole,
        out_shape=jax.ShapeDtypeStruct((leaf_count, height, leaf_size), bf16),
        scratch_shapes=[pltpu.VMEM((group_count * pair // 256 * height, 256), bf16)],
        compiler_params=pltpu.CompilerParams(vmem_limit_bytes=14 * MIB),
        cost_estimate=pl.CostEstimate(flops=8 * 10**9, bytes_accessed=2 * 10**6, transcendentals=0),
        name="place",
    )(src, rank, arrived.reshape(group_count * height, pair))


def skeleton_body(leaf_ref, basis_ref, transfer_ref, skel_ref, upper_ref):
    leaf_count, cols, _ = skel_ref.shape

    def cluster(c, carry):
        total = jnp.zeros(upper_ref.shape[1:], f32)
        for n in range(KIDS):
            i = c * KIDS + n
            values = leaf_ref[i, :cols]
            basis_high, basis_low = halves(basis_ref[i])
            skel = mm(values, basis_high) + mm(values, basis_low)
            skel_ref[i] = skel.astype(bf16)
            total += mm3(skel, transfer_ref[i])
        upper_ref[c] = total.astype(bf16)
        return carry

    lax.fori_loop(0, leaf_count // KIDS, cluster, 0)


def skeleton(leaves, basis, transfer):
    leaf_count, _, rank_size = basis.shape
    cols = leaves.shape[1] - 16
    whole = pl.BlockSpec(memory_space=pltpu.VMEM)
    return pl.pallas_call(
        skeleton_body,
        in_specs=[whole] * 3,
        out_specs=(whole, whole),
        out_shape=(
            jax.ShapeDtypeStruct((leaf_count, cols, rank_size), bf16),
            jax.ShapeDtypeStruct((leaf_count // KIDS, cols, rank_size), bf16),
        ),
        compiler_params=pltpu.CompilerParams(vmem_limit_bytes=14 * MIB),
        cost_estimate=pl.CostEstimate(flops=10**9, bytes_accessed=7 * 10**6, transcendentals=0),
        name="skeleton",
    )(leaves, basis, transfer)


def near_body(list_ref, low_ref, own_ref, high_ref, after_ref, out_ref, tick_ref, rows, values):
    tick_ref[...] = jnp.zeros_like(tick_ref)
    leaf_count, height, leaf_size = own_ref.shape
    cols = height - 16
    for part, ref in enumerate((low_ref, own_ref, high_ref)):

        def fill(n, carry, part=part, ref=ref):
            values[part * leaf_count + n] = ref[n, :cols]
            tail = ref[n, cols:].astype(f32)
            rows[part * leaf_count + n] = source_rows(tail[:8], tail[8:])
            return carry

        lax.fori_loop(0, leaf_count, fill, 0)

    def leaf(i, carry):
        tail = own_ref[i, cols:].astype(f32)
        target = target_rows(tail[:8], tail[8:])
        total = jnp.zeros((leaf_size, cols), f32)
        for q in range(list_ref.shape[1]):
            j = list_ref[i, q]
            total += mm(matern(mm(target, rows[j])), values[j], NT)
        out_ref[i] = total
        return carry

    lax.fori_loop(0, leaf_count, leaf, 0)


def near_sums(lists, low, own, high, after):
    leaf_count, near = lists.shape
    height, leaf_size = own.shape[1:]
    cols = height - 16
    whole = pl.BlockSpec(memory_space=pltpu.VMEM)
    pairs = leaf_count * near * leaf_size * leaf_size
    return pl.pallas_call(
        near_body,
        in_specs=[pl.BlockSpec(memory_space=pltpu.SMEM), whole, whole, whole]
        + [pl.BlockSpec(memory_space=pl.ANY)],
        out_specs=(whole, whole),
        out_shape=(jax.ShapeDtypeStruct((leaf_count, leaf_size, cols), f32), TICK),
        scratch_shapes=[
            pltpu.VMEM((3 * leaf_count, AUG, leaf_size), bf16),
            pltpu.VMEM((3 * leaf_count, cols, leaf_size), bf16),
        ],
        compiler_params=pltpu.CompilerParams(vmem_limit_bytes=58 * MIB),
        cost_estimate=pl.CostEstimate(
            flops=pairs * 2500, bytes_accessed=6 * 10**6, transcendentals=2 * pairs
        ),
        name="near_sums",
    )(lists, low, own, high, after)


def fill_rows(points_ref, rows_ref):
    step = 8

    def fill(n, carry):
        for k in range(step):
            rows_ref[n * step + k] = source_rows(*f32_halves(points_ref[n * step + k]))
        return carry

    lax.fori_loop(0, rows_ref.shape[0] // step, fill, 0)


FAR_STEP = 4


def far_body(first, after_count, list_ref, target_ref, points_ref, *refs):
    out_ref, tick_ref, rows_ref = refs[after_count:]

    @pl.when(pl.program_id(0) == 0)
    def _():
        fill_rows(points_ref, rows_ref)

    rank_size = rows_ref.shape[2]
    far = list_ref.shape[1]
    batch = 4
    for n in range(FAR_STEP):
        i = first + pl.program_id(0) * FAR_STEP + n
        target = target_rows(*f32_halves(target_ref[i]))
        for q in range(0, far, batch):
            rows = jnp.concatenate([rows_ref[list_ref[i, q + k]] for k in range(batch)], axis=1)
            out_ref[n, :, q * rank_size : (q + batch) * rank_size] = matern(mm(target, rows))
    tick_ref[...] = jnp.zeros_like(tick_ref)


def far_kernels(first, count, lists, targets, points, *after):
    far = lists.shape[1]
    rank_size = points.shape[2]
    pairs = count * far * rank_size * rank_size
    anywhere = pl.BlockSpec(memory_space=pl.ANY)
    return pl.pallas_call(
        functools.partial(far_body, first, len(after)),
        grid_spec=pltpu.PrefetchScalarGridSpec(
            num_scalar_prefetch=1,
            grid=(count // FAR_STEP,),
            in_specs=[
                pl.BlockSpec(targets.shape, lambda i, s: (0, 0, 0)),
                pl.BlockSpec(points.shape, lambda i, s: (0, 0, 0)),
            ]
            + [anywhere] * len(after),
            out_specs=(
                pl.BlockSpec((FAR_STEP, rank_size, far * rank_size), lambda i, s: (i, 0, 0)),
                pl.BlockSpec(TICK.shape, lambda i, s: (0, 0)),
            ),
            scratch_shapes=[pltpu.VMEM((points.shape[0], AUG, rank_size), bf16)],
        ),
        out_shape=(jax.ShapeDtypeStruct((count, rank_size, far * rank_size), bf16), TICK),
        compiler_params=pltpu.CompilerParams(vmem_limit_bytes=52 * MIB),
        cost_estimate=pl.CostEstimate(
            flops=pairs * 20, bytes_accessed=10**6, transcendentals=0
        ),
        name="far_kernels",
    )(lists, targets, points, *after)


STREAM_STEP = 4


def far_sums_body(
    list_ref, target_ref, points_ref, gathered_ref, stored_ref, after_ref, out_ref, tick_ref, even, odd, stream, rows_ref, weights_ref, sems
):
    tick_ref[...] = jnp.zeros_like(tick_ref)
    early = stored_ref.shape[0]
    late = out_ref.shape[0] - early
    rank_size = weights_ref.shape[2]
    far = list_ref.shape[1]
    batch = 4
    blocks = early // STREAM_STEP
    copies = [
        pltpu.make_async_copy(
            stored_ref.at[pl.ds(k * STREAM_STEP, STREAM_STEP)], stream.at[k % 2], sems.at[k % 2]
        )
        for k in range(blocks)
    ]

    def listed(ref, i, q, n):
        return jnp.concatenate([ref[list_ref[i, q + k]] for k in range(n)], axis=1)

    def fill(i, kernel):
        target = target_rows(*f32_halves(target_ref[i]))
        for q in range(0, far, batch):
            kernel[:, q * rank_size : (q + batch) * rank_size] = matern(
                mm(target, listed(rows_ref, i, q, batch))
            )

    def apply(i, kernel):
        out_ref[i] = mm(kernel, listed(weights_ref, i, 0, far), NT)

    weights_copy = pltpu.make_async_copy(gathered_ref, weights_ref, sems.at[2])
    weights_copy.start()
    for copy in copies[:2]:
        copy.start()
    fill_rows(points_ref, rows_ref)
    fill(early, even)
    weights_copy.wait()

    def two(n, carry):
        i = early + 2 * n
        fill(i + 1, odd)
        apply(i, even[...])
        fill(jnp.minimum(i + 2, early + late - 1), even)
        apply(i + 1, odd[...])
        return carry

    lax.fori_loop(0, late // 2, two, 0)
    for k, copy in enumerate(copies):
        copy.wait()
        for n in range(STREAM_STEP):
            apply(k * STREAM_STEP + n, stream[k % 2, n])
        if k + 2 < blocks:
            copies[k + 2].start()


def far_sums(lists, targets, points, weights, stored, after):
    count, far = lists.shape
    cols, rank_size = weights.shape[1:]
    whole = pl.BlockSpec(memory_space=pltpu.VMEM)
    anywhere = pl.BlockSpec(memory_space=pl.ANY)
    pairs = count * far * rank_size * rank_size
    return pl.pallas_call(
        far_sums_body,
        in_specs=[pl.BlockSpec(memory_space=pltpu.SMEM), whole, whole, anywhere, anywhere, anywhere],
        out_specs=(whole, whole),
        out_shape=(jax.ShapeDtypeStruct((count, rank_size, cols), f32), TICK),
        scratch_shapes=[pltpu.VMEM((rank_size, far * rank_size), bf16)] * 2
        + [
            pltpu.VMEM((2, STREAM_STEP, rank_size, far * rank_size), bf16),
            pltpu.VMEM((points.shape[0], AUG, rank_size), bf16),
            pltpu.VMEM(weights.shape, bf16),
            pltpu.SemaphoreType.DMA((3,)),
        ],
        compiler_params=pltpu.CompilerParams(vmem_limit_bytes=58 * MIB),
        cost_estimate=pl.CostEstimate(
            flops=pairs * 2500, bytes_accessed=24 * 10**6, transcendentals=2 * pairs
        ),
        name="far_sums",
    )(lists, targets, points, weights, stored, after)


def upper_body(list_ref, own_ref, chip_ref, across_ref, after_ref, out_ref):
    dims, rank_size = own_ref.shape[1:]
    cols = out_ref.shape[2]
    batch = 4
    half = chip_ref.shape[0]

    def block_of(place):
        here = chip_ref[jnp.minimum(place, half - 1)]
        there = across_ref[jnp.maximum(place - half, 0)]
        return jnp.where(place < half, here, there)

    for c in range(own_ref.shape[0]):
        target = target_rows(*scaled_halves(own_ref[c]))
        total = jnp.zeros((rank_size, cols), f32)
        for q in range(0, list_ref.shape[1], batch):
            blocks = [block_of(list_ref[c, q + k]) for k in range(batch)]
            values = jnp.concatenate([x[:cols] for x in blocks], axis=1)
            points = jnp.concatenate([x[cols:].astype(f32)[:dims] for x in blocks], axis=1)
            kernel = matern(mm(target, source_rows(*scaled_halves(points))))
            total += mm(kernel, values, NT)
        out_ref[c] = total


def upper_sums(lists, own, chip, across, after):
    count, dims, rank_size = own.shape
    cols = chip.shape[1] - 2 * dims
    whole = pl.BlockSpec(memory_space=pltpu.VMEM)
    pairs = count * lists.shape[1] * rank_size * rank_size
    return pl.pallas_call(
        upper_body,
        in_specs=[pl.BlockSpec(memory_space=pltpu.SMEM), whole, whole, whole]
        + [pl.BlockSpec(memory_space=pl.ANY)],
        out_specs=whole,
        out_shape=jax.ShapeDtypeStruct((count, rank_size, cols), f32),
        compiler_params=pltpu.CompilerParams(vmem_limit_bytes=16 * MIB),
        cost_estimate=pl.CostEstimate(
            flops=pairs * 230, bytes_accessed=8 * 10**6, transcendentals=2 * pairs
        ),
        name="upper_sums",
    )(lists, own, chip, across, after)


def final_body(far_ref, upper_ref, transfer_ref, basis_ref, near_ref, out_ref):
    leaf_count, leaf_size, _ = basis_ref.shape
    step = 4

    def leaves(n, carry):
        upper = upper_ref[n * step // KIDS]
        for k in range(step):
            i = n * step + k
            skeleton = far_ref[i] + mm3(transfer_ref[i], upper)
            potential = mm3(basis_ref[i], skeleton) + near_ref[i]
            at = pl.ds(pl.multiple_of(i * leaf_size, leaf_size), leaf_size)
            out_ref[:, at] = jnp.transpose(potential)
        return carry

    lax.fori_loop(0, leaf_count // step, leaves, 0)


def final(far, upper, transfer, basis, near):
    leaf_count, leaf_size, rank_size = basis.shape
    cols = near.shape[2]
    whole = pl.BlockSpec(memory_space=pltpu.VMEM)
    return pl.pallas_call(
        final_body,
        in_specs=[whole] * 5,
        out_specs=whole,
        out_shape=jax.ShapeDtypeStruct((cols, leaf_count * leaf_size), f32),
        compiler_params=pltpu.CompilerParams(vmem_limit_bytes=20 * MIB),
        cost_estimate=pl.CostEstimate(flops=10**9, bytes_accessed=10**7, transcendentals=0),
        name="final",
    )(far, upper, transfer, basis, near)


def shifted(block, axis, move, count):
    return lax.ppermute(block, axis, [(i, move(i)) for i in range(count)])


def upper_places(clusters, count):
    owner = clusters // count
    group = owner % 16
    bulk = owner // 16
    mine = lax.axis_index("bulk")
    core = (bulk ^ mine) & 1
    hops = (bulk // 2 - mine // 2) & 3
    turn = hops
    return (((core * 4 + turn) * 16) + group) * count + clusters % count


def local(
    points,
    weights,
    leaf_order,
    basis,
    transfer,
    skel_leaf,
    skel_upper,
    near_list,
    leaf_interaction_list,
    far_upper,
):
    row_count = leaf_order.shape[0]
    group_count = lax.axis_size("group")
    bulk_count = lax.axis_size("bulk")
    device_count = group_count * bulk_count
    leaf_count = basis.shape[0]

    want, src, rank, tick = index_lists(leaf_order, group_count, basis.shape[1])
    scaled = skel_leaf.astype(f32) * POINT_SCALE + tick[0]
    subtree_points = lax.all_gather(scaled, "group", axis=0, tiled=True)
    wanted = lax.all_to_all(want, "group", split_axis=0, concat_axis=0, tiled=True)
    picked = pick(wanted, pick_table(points, weights), row_count)
    arrived = lax.all_to_all(picked, "group", split_axis=0, concat_axis=0, tiled=True)

    far_local = leaf_interaction_list - lax.axis_index("bulk") * (group_count * leaf_count)

    own = place(src, rank, arrived)
    skel_wb, upper_wb = skeleton(own, basis, transfer)
    sub_w = lax.all_gather(skel_wb, "group", axis=0, tiled=True)
    forward = [(i, i + 1) for i in range(device_count - 1)]
    backward = [(i + 1, i) for i in range(device_count - 1)]
    low = lax.ppermute(own, ("bulk", "group"), forward)
    high = lax.ppermute(own, ("bulk", "group"), backward)

    def joined(tick, *blocks):
        return jnp.concatenate(blocks, axis=0) + tick[0].astype(bf16)

    mine = jnp.concatenate([upper_wb, skel_upper, jnp.zeros(skel_upper.shape, bf16)], axis=1)
    copies = jnp.tile(mine, (group_count, 1, 1))
    block = lax.all_to_all(copies, "group", split_axis=0, concat_axis=0, tiled=True)
    part = leaf_count // 2
    kernels, tick = far_kernels(0, part, far_local, scaled, subtree_points, copies)
    block = joined(tick, block)
    ring = [shifted(block, "bulk", lambda i, hops=hops: (i - 2 * hops) % bulk_count, bulk_count) for hops in (1, 2, 3)]
    device = lax.axis_index(("bulk", "group"))
    near, tick = near_sums(near_list - (device - 1) * leaf_count, low, own, high, block)
    chip = joined(tick, block, *ring)
    other = shifted(chip, "bulk", lambda i: i ^ 1, bulk_count)
    far, tick = far_sums(far_local, scaled, subtree_points, sub_w, kernels, chip)
    upper = upper_sums(upper_places(far_upper, skel_upper.shape[0]), skel_upper, chip, other, tick)
    return final(far, upper, transfer, basis, near)


def solution(mesh):
    placed = (
        P(None, ("bulk", "group")),
        P(None, ("bulk", "group")),
        P(("bulk", "group")),
        P(("bulk", "group"), None, None),
        P(("bulk", "group"), None, None),
        P(("bulk", "group"), None, None),
        P(("bulk", "group"), None, None),
        P(("bulk", "group"), None),
        P(("bulk", "group"), None),
        P(("bulk", "group"), None),
    )
    return jax.shard_map(
        local, mesh=mesh, in_specs=placed, out_specs=P(None, ("bulk", "group")), check_vma=False
    )
```

```python
import functools
import math

import jax
import jax.numpy as jnp
from jax import lax
from jax.experimental import pallas as pl
from jax.experimental.pallas import tpu as pltpu
from jax.sharding import PartitionSpec as P

KIDS = 8

POINT_SCALE = math.sqrt(5.0) / 2.0 / math.log(2.0)
POLY_A = 3.0 / math.log(2.0)
POLY_B = 3.0 / math.log(2.0) ** 2
POLY_LOG = math.log2(math.log(2.0) ** 2 / 3.0)
AUG = 48
MIB = 1024 * 1024

f32 = jnp.float32
bf16 = jnp.bfloat16
TICK = jax.ShapeDtypeStruct((8, 128), f32)
NN = (((1,), (0,)), ((), ()))
NT = (((1,), (1,)), ((), ()))


def mm(a, b, dims=NN):
    return lax.dot_general(a, b, dims, preferred_element_type=f32)


def halves(x):
    high = x.astype(bf16)
    return high, (x - high.astype(f32)).astype(bf16)


def mm3(a, b):
    a_high, a_low = halves(a)
    b_high, b_low = halves(b)
    return mm(a_high, b_high) + (mm(a_high, b_low) + mm(a_low, b_high))


def squares(high, low):
    x = high + low
    norm = jnp.sum(x * x, axis=0, keepdims=True)
    first = norm.astype(bf16).astype(f32)
    second = (norm - first).astype(bf16).astype(f32)
    third = norm - first - second
    row = lax.broadcasted_iota(jnp.int32, high.shape, 0)
    parts = jnp.where(row % 3 == 0, first, jnp.where(row % 3 == 1, second, third))
    return row, parts


def source_rows(high, low):
    row, parts = squares(high, low)
    last = jnp.where(row < 3, 1.0, jnp.where(row < 6, parts, 0.0))
    high, low = -2.0 * high, -2.0 * low
    return jnp.concatenate([high, low, high, low, last, jnp.zeros_like(last)], axis=0).astype(bf16)


def target_rows(high, low):
    row, parts = squares(high, low)
    last = jnp.where(row < 3, parts, jnp.where(row < 6, 1.0, 0.0))
    rows = jnp.concatenate([high, high, low, low, last, jnp.zeros_like(last)], axis=0)
    return jnp.transpose(rows).astype(bf16)


def f32_halves(points):
    high, low = halves(points)
    return high.astype(f32), low.astype(f32)


def scaled_halves(points):
    return f32_halves(points.astype(f32) * POINT_SCALE)


def matern(square):
    square = jnp.maximum(square, 1e-30)
    t = square * lax.rsqrt(square)
    return (((t + POLY_A) * t + POLY_B) * jnp.exp2(POLY_LOG - t)).astype(bf16)


def index_body(order_ref, want_ref, src_ref, rank_ref, tick_ref):
    tick_ref[...] = jnp.zeros_like(tick_ref)
    group_count, _, pair = want_ref.shape
    lines = order_ref.shape[0]
    row_count = group_count * pair
    order = order_ref[...]
    owner = ((order.astype(f32) + 0.5) * (1.0 / row_count)).astype(jnp.int32)
    src = owner % group_count
    row = order - owner * row_count
    before = (
        lax.broadcasted_iota(jnp.int32, (128, 128), 0)
        < lax.broadcasted_iota(jnp.int32, (128, 128), 1)
    ).astype(f32).astype(bf16)
    above = (
        lax.broadcasted_iota(jnp.int32, (lines, lines), 1)
        < lax.broadcasted_iota(jnp.int32, (lines, lines), 0)
    ).astype(f32).astype(bf16)
    all_ones = jnp.ones((128, 128), bf16)
    rank = jnp.zeros(src.shape, f32)
    for g in range(group_count):
        here = src == g
        mask = here.astype(f32).astype(bf16)
        total = mm(mask, all_ones).astype(bf16)
        rank = jnp.where(here, mm(mask, before) + mm(above, total), rank)
    rank = rank.astype(jnp.int32)
    for i in range(lines // 2):
        for ref, x in ((src_ref, src), (rank_ref, rank)):
            ref[i] = jnp.concatenate([x[2 * i : 2 * i + 1], x[2 * i + 1 : 2 * i + 2]], axis=1)
    place = lax.broadcasted_iota(jnp.int32, (pair, 256), 0)
    owner = lax.broadcasted_iota(jnp.int32, (group_count, 256), 0)
    total = jnp.zeros((2 * group_count, pair), f32)
    for k in range(0, lines, 2):
        line = lambda x: jnp.concatenate([x[k : k + 1], x[k + 1 : k + 2]], axis=1)
        rank_line, src_line, row_line = line(rank), line(src), line(row)
        spots = (place == rank_line).astype(f32).astype(bf16)
        mine = owner == src_line
        high = jnp.where(mine, (row_line >> 7).astype(f32), 0.0)
        low = jnp.where(mine, (row_line & 127).astype(f32), 0.0)
        total += mm(jnp.concatenate([high, low], axis=0).astype(bf16), spots, NT)
    want = (total[:group_count] * 128.0 + total[group_count:]).astype(jnp.int32)
    for g in range(group_count):
        want_ref[g] = want[g : g + 1]


def index_lists(order, group_count, leaf_size):
    row_count = order.shape[0]
    assert leaf_size == 256
    return pl.pallas_call(
        index_body,
        out_shape=(
            jax.ShapeDtypeStruct((group_count, 1, row_count // group_count), jnp.int32),
            jax.ShapeDtypeStruct((row_count // leaf_size, 1, leaf_size), jnp.int32),
            jax.ShapeDtypeStruct((row_count // leaf_size, 1, leaf_size), jnp.int32),
            TICK,
        ),
        compiler_params=pltpu.CompilerParams(vmem_limit_bytes=8 * MIB),
        cost_estimate=pl.CostEstimate(flops=2 * 10**9, bytes_accessed=10**5, transcendentals=0),
        name="index_lists",
    )(order.reshape(-1, 128))


def table_body(points_ref, weights_ref, table_ref):
    height = weights_ref.shape[0] + 2 * points_ref.shape[0]
    for h in range(points_ref.shape[1] // 256):
        at = slice(h * 256, (h + 1) * 256)
        high, low = scaled_halves(points_ref[:, at])
        table_ref[h * height : (h + 1) * height, :] = jnp.concatenate(
            [weights_ref[:, at], high, low], axis=0
        ).astype(bf16)


def pick_table(points, weights):
    height = weights.shape[0] + 2 * points.shape[0]
    whole = pl.BlockSpec(memory_space=pltpu.VMEM)
    return pl.pallas_call(
        table_body,
        in_specs=[whole, whole],
        out_specs=whole,
        out_shape=jax.ShapeDtypeStruct((points.shape[1] // 256 * height, 256), bf16),
        compiler_params=pltpu.CompilerParams(vmem_limit_bytes=10 * MIB),
        cost_estimate=pl.CostEstimate(flops=3 * 10**9, bytes_accessed=3 * 10**6, transcendentals=0),
        name="pick_table",
    )(points, weights)


def pick_body(want_ref, table_ref, out_ref):
    group_count, height, pair = out_ref.shape
    high_count = table_ref.shape[0] // height
    batch = 8

    def devices(d, carry):
        want = jnp.concatenate([want_ref[2 * d], want_ref[2 * d + 1]], axis=1)
        low = want & 255
        high = want >> 8
        spots = (lax.broadcasted_iota(jnp.int32, (256, 2 * pair), 0) == low).astype(f32).astype(bf16)
        picked = jnp.zeros((height, 2 * pair), f32)
        for h in range(0, high_count, batch):
            found = mm(table_ref[h * height : (h + batch) * height, :], spots)
            for k in range(batch):
                picked = jnp.where(high == h + k, found[k * height : (k + 1) * height], picked)
        picked = picked.astype(bf16)
        out_ref[2 * d] = picked[:, :pair]
        out_ref[2 * d + 1] = picked[:, pair:]
        return carry

    lax.fori_loop(0, group_count // 2, devices, 0)


def pick(want, table, row_count):
    group_count, _, pair = want.shape
    height = table.shape[0] * 256 // row_count
    whole = pl.BlockSpec(memory_space=pltpu.VMEM)
    return pl.pallas_call(
        pick_body,
        in_specs=[whole, whole],
        out_specs=whole,
        out_shape=jax.ShapeDtypeStruct((group_count, height, pair), bf16),
        compiler_params=pltpu.CompilerParams(vmem_limit_bytes=16 * MIB),
        cost_estimate=pl.CostEstimate(flops=6 * 10**9, bytes_accessed=3 * 10**6, transcendentals=0),
        name="pick",
    )(want, table)


def place_body(src_ref, rank_ref, arrived_ref, leaf_ref, table):
    leaf_count, height, leaf_size = leaf_ref.shape
    pair = arrived_ref.shape[1]
    group_count = arrived_ref.shape[0] // height
    lines = table.shape[0] // height
    pieces = 2 * lines // group_count
    batch = 4
    step = 4
    for g in range(0, group_count, 2):
        two = jnp.concatenate(
            [arrived_ref[(g + k) * height : (g + k + 1) * height, :] for k in range(2)], axis=1
        )
        for k in range(pieces):
            at = (g // 2 * pieces + k) * height
            table[at : at + height, :] = two[:, k * 256 : (k + 1) * 256]

    def leaves(c, carry):
        for n in range(step):
            i = c * step + n
            slot = src_ref[i] * pair + rank_ref[i]
            low = slot & 255
            high = slot >> 8
            spots = (
                lax.broadcasted_iota(jnp.int32, (256, leaf_size), 0) == low
            ).astype(f32).astype(bf16)
            placed = jnp.zeros((height, leaf_size), f32)
            for h in range(0, lines, batch):
                found = mm(table[h * height : (h + batch) * height, :], spots)
                for k in range(batch):
                    placed = jnp.where(high == h + k, found[k * height : (k + 1) * height], placed)
            leaf_ref[i] = placed.astype(bf16)
        return carry

    lax.fori_loop(0, leaf_count // step, leaves, 0)


def place(src, rank, arrived):
    group_count, height, pair = arrived.shape
    leaf_count, _, leaf_size = src.shape
    whole = pl.BlockSpec(memory_space=pltpu.VMEM)
    return pl.pallas_call(
        place_body,
        in_specs=[whole] * 3,
        out_specs=whole,
        out_shape=jax.ShapeDtypeStruct((leaf_count, height, leaf_size), bf16),
        scratch_shapes=[pltpu.VMEM((group_count * pair // 256 * height, 256), bf16)],
        compiler_params=pltpu.CompilerParams(vmem_limit_bytes=14 * MIB),
        cost_estimate=pl.CostEstimate(flops=8 * 10**9, bytes_accessed=2 * 10**6, transcendentals=0),
        name="place",
    )(src, rank, arrived.reshape(group_count * height, pair))


def skeleton_body(leaf_ref, basis_ref, transfer_ref, skel_ref, upper_ref):
    leaf_count, cols, _ = skel_ref.shape

    def cluster(c, carry):
        total = jnp.zeros(upper_ref.shape[1:], f32)
        for n in range(KIDS):
            i = c * KIDS + n
            values = leaf_ref[i, :cols]
            basis_high, basis_low = halves(basis_ref[i])
            skel = mm(values, basis_high) + mm(values, basis_low)
            skel_ref[i] = skel.astype(bf16)
            total += mm3(skel, transfer_ref[i])
        upper_ref[c] = total.astype(bf16)
        return carry

    lax.fori_loop(0, leaf_count // KIDS, cluster, 0)


def skeleton(leaves, basis, transfer):
    leaf_count, _, rank_size = basis.shape
    cols = leaves.shape[1] - 16
    whole = pl.BlockSpec(memory_space=pltpu.VMEM)
    return pl.pallas_call(
        skeleton_body,
        in_specs=[whole] * 3,
        out_specs=(whole, whole),
        out_shape=(
            jax.ShapeDtypeStruct((leaf_count, cols, rank_size), bf16),
            jax.ShapeDtypeStruct((leaf_count // KIDS, cols, rank_size), bf16),
        ),
        compiler_params=pltpu.CompilerParams(vmem_limit_bytes=14 * MIB),
        cost_estimate=pl.CostEstimate(flops=10**9, bytes_accessed=7 * 10**6, transcendentals=0),
        name="skeleton",
    )(leaves, basis, transfer)


def near_body(list_ref, low_ref, own_ref, high_ref, after_ref, out_ref, tick_ref, rows, values):
    tick_ref[...] = jnp.zeros_like(tick_ref)
    leaf_count, height, leaf_size = own_ref.shape
    cols = height - 16
    for part, ref in enumerate((low_ref, own_ref, high_ref)):

        def fill(n, carry, part=part, ref=ref):
            values[part * leaf_count + n] = ref[n, :cols]
            tail = ref[n, cols:].astype(f32)
            rows[part * leaf_count + n] = source_rows(tail[:8], tail[8:])
            return carry

        lax.fori_loop(0, leaf_count, fill, 0)

    def leaf(i, carry):
        tail = own_ref[i, cols:].astype(f32)
        target = target_rows(tail[:8], tail[8:])
        total = jnp.zeros((leaf_size, cols), f32)
        for q in range(list_ref.shape[1]):
            j = list_ref[i, q]
            total += mm(matern(mm(target, rows[j])), values[j], NT)
        out_ref[i] = total
        return carry

    lax.fori_loop(0, leaf_count, leaf, 0)


def near_sums(lists, low, own, high, after):
    leaf_count, near = lists.shape
    height, leaf_size = own.shape[1:]
    cols = height - 16
    whole = pl.BlockSpec(memory_space=pltpu.VMEM)
    pairs = leaf_count * near * leaf_size * leaf_size
    return pl.pallas_call(
        near_body,
        in_specs=[pl.BlockSpec(memory_space=pltpu.SMEM), whole, whole, whole]
        + [pl.BlockSpec(memory_space=pl.ANY)],
        out_specs=(whole, whole),
        out_shape=(jax.ShapeDtypeStruct((leaf_count, leaf_size, cols), f32), TICK),
        scratch_shapes=[
            pltpu.VMEM((3 * leaf_count, AUG, leaf_size), bf16),
            pltpu.VMEM((3 * leaf_count, cols, leaf_size), bf16),
        ],
        compiler_params=pltpu.CompilerParams(vmem_limit_bytes=16 * MIB),
        cost_estimate=pl.CostEstimate(
            flops=pairs * 2500, bytes_accessed=6 * 10**6, transcendentals=2 * pairs
        ),
        name="near_sums",
    )(lists, low, own, high, after)


def fill_rows(points_ref, rows_ref):
    step = 8

    def fill(n, carry):
        for k in range(step):
            rows_ref[n * step + k] = source_rows(*f32_halves(points_ref[n * step + k]))
        return carry

    lax.fori_loop(0, rows_ref.shape[0] // step, fill, 0)


FAR_STEP = 4


def far_body(first, after_count, list_ref, target_ref, points_ref, *refs):
    out_ref, tick_ref, rows_ref = refs[after_count:]

    @pl.when(pl.program_id(0) == 0)
    def _():
        fill_rows(points_ref, rows_ref)

    rank_size = rows_ref.shape[2]
    far = list_ref.shape[1]
    batch = 4
    for n in range(FAR_STEP):
        i = first + pl.program_id(0) * FAR_STEP + n
        target = target_rows(*f32_halves(target_ref[i]))
        for q in range(0, far, batch):
            rows = jnp.concatenate([rows_ref[list_ref[i, q + k]] for k in range(batch)], axis=1)
            out_ref[n, :, q * rank_size : (q + batch) * rank_size] = matern(mm(target, rows))
    tick_ref[...] = jnp.zeros_like(tick_ref)


def far_kernels(first, count, lists, targets, points, *after):
    far = lists.shape[1]
    rank_size = points.shape[2]
    pairs = count * far * rank_size * rank_size
    anywhere = pl.BlockSpec(memory_space=pl.ANY)
    return pl.pallas_call(
        functools.partial(far_body, first, len(after)),
        grid_spec=pltpu.PrefetchScalarGridSpec(
            num_scalar_prefetch=1,
            grid=(count // FAR_STEP,),
            in_specs=[
                pl.BlockSpec(targets.shape, lambda i, s: (0, 0, 0)),
                pl.BlockSpec(points.shape, lambda i, s: (0, 0, 0)),
            ]
            + [anywhere] * len(after),
            out_specs=(
                pl.BlockSpec((FAR_STEP, rank_size, far * rank_size), lambda i, s: (i, 0, 0)),
                pl.BlockSpec(TICK.shape, lambda i, s: (0, 0)),
            ),
            scratch_shapes=[pltpu.VMEM((points.shape[0], AUG, rank_size), bf16)],
        ),
        out_shape=(jax.ShapeDtypeStruct((count, rank_size, far * rank_size), bf16), TICK),
        compiler_params=pltpu.CompilerParams(vmem_limit_bytes=52 * MIB),
        cost_estimate=pl.CostEstimate(
            flops=pairs * 20, bytes_accessed=10**6, transcendentals=0
        ),
        name="far_kernels",
    )(lists, targets, points, *after)


STREAM_STEP = 4


def far_sums_body(
    list_ref, target_ref, points_ref, gathered_ref, stored_ref, after_ref, out_ref, tick_ref, even, odd, stream, rows_ref, weights_ref, sems
):
    tick_ref[...] = jnp.zeros_like(tick_ref)
    early = stored_ref.shape[0]
    late = out_ref.shape[0] - early
    rank_size = weights_ref.shape[2]
    far = list_ref.shape[1]
    batch = 4
    blocks = early // STREAM_STEP
    copies = [
        pltpu.make_async_copy(
            stored_ref.at[pl.ds(k * STREAM_STEP, STREAM_STEP)], stream.at[k % 2], sems.at[k % 2]
        )
        for k in range(blocks)
    ]

    def listed(ref, i, q, n):
        return jnp.concatenate([ref[list_ref[i, q + k]] for k in range(n)], axis=1)

    def fill(i, kernel):
        target = target_rows(*f32_halves(target_ref[i]))
        for q in range(0, far, batch):
            kernel[:, q * rank_size : (q + batch) * rank_size] = matern(
                mm(target, listed(rows_ref, i, q, batch))
            )

    def apply(i, kernel):
        out_ref[i] = mm(kernel, listed(weights_ref, i, 0, far), NT)

    weights_copy = pltpu.make_async_copy(gathered_ref, weights_ref, sems.at[2])
    weights_copy.start()
    for copy in copies[:2]:
        copy.start()
    fill_rows(points_ref, rows_ref)
    fill(early, even)
    weights_copy.wait()

    def two(n, carry):
        i = early + 2 * n
        fill(i + 1, odd)
        apply(i, even[...])
        fill(jnp.minimum(i + 2, early + late - 1), even)
        apply(i + 1, odd[...])
        return carry

    lax.fori_loop(0, late // 2, two, 0)
    for k, copy in enumerate(copies):
        copy.wait()
        for n in range(STREAM_STEP):
            apply(k * STREAM_STEP + n, stream[k % 2, n])
        if k + 2 < blocks:
            copies[k + 2].start()


def far_sums(lists, targets, points, weights, stored, after):
    count, far = lists.shape
    cols, rank_size = weights.shape[1:]
    whole = pl.BlockSpec(memory_space=pltpu.VMEM)
    anywhere = pl.BlockSpec(memory_space=pl.ANY)
    pairs = count * far * rank_size * rank_size
    return pl.pallas_call(
        far_sums_body,
        in_specs=[pl.BlockSpec(memory_space=pltpu.SMEM), whole, whole, anywhere, anywhere, anywhere],
        out_specs=(whole, whole),
        out_shape=(jax.ShapeDtypeStruct((count, rank_size, cols), f32), TICK),
        scratch_shapes=[pltpu.VMEM((rank_size, far * rank_size), bf16)] * 2
        + [
            pltpu.VMEM((2, STREAM_STEP, rank_size, far * rank_size), bf16),
            pltpu.VMEM((points.shape[0], AUG, rank_size), bf16),
            pltpu.VMEM(weights.shape, bf16),
            pltpu.SemaphoreType.DMA((3,)),
        ],
        compiler_params=pltpu.CompilerParams(vmem_limit_bytes=58 * MIB),
        cost_estimate=pl.CostEstimate(
            flops=pairs * 2500, bytes_accessed=24 * 10**6, transcendentals=2 * pairs
        ),
        name="far_sums",
    )(lists, targets, points, weights, stored, after)


def upper_body(list_ref, own_ref, chip_ref, across_ref, after_ref, out_ref):
    dims, rank_size = own_ref.shape[1:]
    cols = out_ref.shape[2]
    batch = 4
    half = chip_ref.shape[0]

    def block_of(place):
        here = chip_ref[jnp.minimum(place, half - 1)]
        there = across_ref[jnp.maximum(place - half, 0)]
        return jnp.where(place < half, here, there)

    for c in range(own_ref.shape[0]):
        target = target_rows(*scaled_halves(own_ref[c]))
        total = jnp.zeros((rank_size, cols), f32)
        for q in range(0, list_ref.shape[1], batch):
            blocks = [block_of(list_ref[c, q + k]) for k in range(batch)]
            values = jnp.concatenate([x[:cols] for x in blocks], axis=1)
            points = jnp.concatenate([x[cols:].astype(f32)[:dims] for x in blocks], axis=1)
            kernel = matern(mm(target, source_rows(*scaled_halves(points))))
            total += mm(kernel, values, NT)
        out_ref[c] = total


def upper_sums(lists, own, chip, across, after):
    count, dims, rank_size = own.shape
    cols = chip.shape[1] - 2 * dims
    whole = pl.BlockSpec(memory_space=pltpu.VMEM)
    pairs = count * lists.shape[1] * rank_size * rank_size
    return pl.pallas_call(
        upper_body,
        in_specs=[pl.BlockSpec(memory_space=pltpu.SMEM), whole, whole, whole]
        + [pl.BlockSpec(memory_space=pl.ANY)],
        out_specs=whole,
        out_shape=jax.ShapeDtypeStruct((count, rank_size, cols), f32),
        compiler_params=pltpu.CompilerParams(vmem_limit_bytes=16 * MIB),
        cost_estimate=pl.CostEstimate(
            flops=pairs * 230, bytes_accessed=8 * 10**6, transcendentals=2 * pairs
        ),
        name="upper_sums",
    )(lists, own, chip, across, after)


def final_body(far_ref, upper_ref, transfer_ref, basis_ref, near_ref, out_ref):
    leaf_count, leaf_size, _ = basis_ref.shape
    step = 4

    def leaves(n, carry):
        upper = upper_ref[n * step // KIDS]
        for k in range(step):
            i = n * step + k
            skeleton = far_ref[i] + mm3(transfer_ref[i], upper)
            potential = mm3(basis_ref[i], skeleton) + near_ref[i]
            at = pl.ds(pl.multiple_of(i * leaf_size, leaf_size), leaf_size)
            out_ref[:, at] = jnp.transpose(potential)
        return carry

    lax.fori_loop(0, leaf_count // step, leaves, 0)


def final(far, upper, transfer, basis, near):
    leaf_count, leaf_size, rank_size = basis.shape
    cols = near.shape[2]
    whole = pl.BlockSpec(memory_space=pltpu.VMEM)
    return pl.pallas_call(
        final_body,
        in_specs=[whole] * 5,
        out_specs=whole,
        out_shape=jax.ShapeDtypeStruct((cols, leaf_count * leaf_size), f32),
        compiler_params=pltpu.CompilerParams(vmem_limit_bytes=20 * MIB),
        cost_estimate=pl.CostEstimate(flops=10**9, bytes_accessed=10**7, transcendentals=0),
        name="final",
    )(far, upper, transfer, basis, near)


def shifted(block, axis, move, count):
    return lax.ppermute(block, axis, [(i, move(i)) for i in range(count)])


def upper_places(clusters, count):
    owner = clusters // count
    group = owner % 16
    bulk = owner // 16
    mine = lax.axis_index("bulk")
    core = (bulk ^ mine) & 1
    hops = (bulk // 2 - mine // 2) & 3
    turn = hops
    return (((core * 4 + turn) * 16) + group) * count + clusters % count


def local(
    points,
    weights,
    leaf_order,
    basis,
    transfer,
    skel_leaf,
    skel_upper,
    near_list,
    leaf_interaction_list,
    far_upper,
):
    row_count = leaf_order.shape[0]
    group_count = lax.axis_size("group")
    bulk_count = lax.axis_size("bulk")
    device_count = group_count * bulk_count
    leaf_count = basis.shape[0]

    want, src, rank, tick = index_lists(leaf_order, group_count, basis.shape[1])
    scaled = skel_leaf.astype(f32) * POINT_SCALE + tick[0]
    subtree_points = lax.all_gather(scaled, "group", axis=0, tiled=True)
    wanted = lax.all_to_all(want, "group", split_axis=0, concat_axis=0, tiled=True)
    picked = pick(wanted, pick_table(points, weights), row_count)
    arrived = lax.all_to_all(picked, "group", split_axis=0, concat_axis=0, tiled=True)

    far_local = leaf_interaction_list - lax.axis_index("bulk") * (group_count * leaf_count)

    own = place(src, rank, arrived)
    skel_wb, upper_wb = skeleton(own, basis, transfer)
    sub_w = lax.all_gather(skel_wb, "group", axis=0, tiled=True)
    forward = [(i, i + 1) for i in range(device_count - 1)]
    backward = [(i + 1, i) for i in range(device_count - 1)]
    low = lax.ppermute(own, ("bulk", "group"), forward)
    high = lax.ppermute(own, ("bulk", "group"), backward)

    def joined(tick, *blocks):
        return jnp.concatenate(blocks, axis=0) + tick[0].astype(bf16)

    mine = jnp.concatenate([upper_wb, skel_upper, jnp.zeros(skel_upper.shape, bf16)], axis=1)
    copies = jnp.tile(mine, (group_count, 1, 1))
    block = lax.all_to_all(copies, "group", split_axis=0, concat_axis=0, tiled=True)
    part = leaf_count // 2
    kernels, tick = far_kernels(0, part, far_local, scaled, subtree_points, copies)
    block = joined(tick, block)
    ring = [shifted(block, "bulk", lambda i, hops=hops: (i - 2 * hops) % bulk_count, bulk_count) for hops in (1, 2, 3)]
    device = lax.axis_index(("bulk", "group"))
    near, tick = near_sums(near_list - (device - 1) * leaf_count, low, own, high, block)
    chip = joined(tick, block, *ring)
    other = shifted(chip, "bulk", lambda i: i ^ 1, bulk_count)
    far, tick = far_sums(far_local, scaled, subtree_points, sub_w, kernels, chip)
    upper = upper_sums(upper_places(far_upper, skel_upper.shape[0]), skel_upper, chip, other, tick)
    return final(far, upper, transfer, basis, near)


def solution(mesh):
    placed = (
        P(None, ("bulk", "group")),
        P(None, ("bulk", "group")),
        P(("bulk", "group")),
        P(("bulk", "group"), None, None),
        P(("bulk", "group"), None, None),
        P(("bulk", "group"), None, None),
        P(("bulk", "group"), None, None),
        P(("bulk", "group"), None),
        P(("bulk", "group"), None),
        P(("bulk", "group"), None),
    )
    return jax.shard_map(
        local, mesh=mesh, in_specs=placed, out_specs=P(None, ("bulk", "group")), check_vma=False
    )
```

```python
import functools
import math

import jax
import jax.numpy as jnp
from jax import lax
from jax.experimental import pallas as pl
from jax.experimental.pallas import tpu as pltpu
from jax.sharding import PartitionSpec as P

KIDS = 8

POINT_SCALE = math.sqrt(5.0) / 2.0 / math.log(2.0)
POLY_A = 3.0 / math.log(2.0)
POLY_B = 3.0 / math.log(2.0) ** 2
POLY_LOG = math.log2(math.log(2.0) ** 2 / 3.0)
AUG = 48
MIB = 1024 * 1024

f32 = jnp.float32
bf16 = jnp.bfloat16
TICK = jax.ShapeDtypeStruct((8, 128), f32)
NN = (((1,), (0,)), ((), ()))
NT = (((1,), (1,)), ((), ()))


def mm(a, b, dims=NN):
    return lax.dot_general(a, b, dims, preferred_element_type=f32)


def halves(x):
    high = x.astype(bf16)
    return high, (x - high.astype(f32)).astype(bf16)


def mm3(a, b):
    a_high, a_low = halves(a)
    b_high, b_low = halves(b)
    return mm(a_high, b_high) + (mm(a_high, b_low) + mm(a_low, b_high))


def squares(high, low):
    x = high + low
    norm = jnp.sum(x * x, axis=0, keepdims=True)
    first = norm.astype(bf16).astype(f32)
    second = (norm - first).astype(bf16).astype(f32)
    third = norm - first - second
    row = lax.broadcasted_iota(jnp.int32, high.shape, 0)
    parts = jnp.where(row % 3 == 0, first, jnp.where(row % 3 == 1, second, third))
    return row, parts


def source_rows(high, low):
    row, parts = squares(high, low)
    last = jnp.where(row < 3, 1.0, jnp.where(row < 6, parts, 0.0))
    high, low = -2.0 * high, -2.0 * low
    return jnp.concatenate([high, low, high, low, last, jnp.zeros_like(last)], axis=0).astype(bf16)


def target_rows(high, low):
    row, parts = squares(high, low)
    last = jnp.where(row < 3, parts, jnp.where(row < 6, 1.0, 0.0))
    rows = jnp.concatenate([high, high, low, low, last, jnp.zeros_like(last)], axis=0)
    return jnp.transpose(rows).astype(bf16)


def f32_halves(points):
    high, low = halves(points)
    return high.astype(f32), low.astype(f32)


def scaled_halves(points):
    return f32_halves(points.astype(f32) * POINT_SCALE)


def matern(square):
    square = jnp.maximum(square, 1e-30)
    t = square * lax.rsqrt(square)
    return (((t + POLY_A) * t + POLY_B) * jnp.exp2(POLY_LOG - t)).astype(bf16)


def index_body(order_ref, want_ref, src_ref, rank_ref, tick_ref):
    tick_ref[...] = jnp.zeros_like(tick_ref)
    group_count, _, pair = want_ref.shape
    lines = order_ref.shape[0]
    row_count = group_count * pair
    order = order_ref[...]
    owner = ((order.astype(f32) + 0.5) * (1.0 / row_count)).astype(jnp.int32)
    src = owner % group_count
    row = order - owner * row_count
    before = (
        lax.broadcasted_iota(jnp.int32, (128, 128), 0)
        < lax.broadcasted_iota(jnp.int32, (128, 128), 1)
    ).astype(f32).astype(bf16)
    above = (
        lax.broadcasted_iota(jnp.int32, (lines, lines), 1)
        < lax.broadcasted_iota(jnp.int32, (lines, lines), 0)
    ).astype(f32).astype(bf16)
    all_ones = jnp.ones((128, 128), bf16)
    rank = jnp.zeros(src.shape, f32)
    for g in range(group_count):
        here = src == g
        mask = here.astype(f32).astype(bf16)
        total = mm(mask, all_ones).astype(bf16)
        rank = jnp.where(here, mm(mask, before) + mm(above, total), rank)
    rank = rank.astype(jnp.int32)
    for i in range(lines // 2):
        for ref, x in ((src_ref, src), (rank_ref, rank)):
            ref[i] = jnp.concatenate([x[2 * i : 2 * i + 1], x[2 * i + 1 : 2 * i + 2]], axis=1)
    place = lax.broadcasted_iota(jnp.int32, (pair, 256), 0)
    owner = lax.broadcasted_iota(jnp.int32, (group_count, 256), 0)
    total = jnp.zeros((2 * group_count, pair), f32)
    for k in range(0, lines, 2):
        line = lambda x: jnp.concatenate([x[k : k + 1], x[k + 1 : k + 2]], axis=1)
        rank_line, src_line, row_line = line(rank), line(src), line(row)
        spots = (place == rank_line).astype(f32).astype(bf16)
        mine = owner == src_line
        high = jnp.where(mine, (row_line >> 7).astype(f32), 0.0)
        low = jnp.where(mine, (row_line & 127).astype(f32), 0.0)
        total += mm(jnp.concatenate([high, low], axis=0).astype(bf16), spots, NT)
    want = (total[:group_count] * 128.0 + total[group_count:]).astype(jnp.int32)
    for g in range(group_count):
        want_ref[g] = want[g : g + 1]


def index_lists(order, group_count, leaf_size):
    row_count = order.shape[0]
    assert leaf_size == 256
    return pl.pallas_call(
        index_body,
        out_shape=(
            jax.ShapeDtypeStruct((group_count, 1, row_count // group_count), jnp.int32),
            jax.ShapeDtypeStruct((row_count // leaf_size, 1, leaf_size), jnp.int32),
            jax.ShapeDtypeStruct((row_count // leaf_size, 1, leaf_size), jnp.int32),
            TICK,
        ),
        compiler_params=pltpu.CompilerParams(vmem_limit_bytes=8 * MIB),
        cost_estimate=pl.CostEstimate(flops=2 * 10**9, bytes_accessed=10**5, transcendentals=0),
        name="index_lists",
    )(order.reshape(-1, 128))


def table_body(points_ref, weights_ref, table_ref):
    height = weights_ref.shape[0] + 2 * points_ref.shape[0]
    for h in range(points_ref.shape[1] // 256):
        at = slice(h * 256, (h + 1) * 256)
        high, low = scaled_halves(points_ref[:, at])
        table_ref[h * height : (h + 1) * height, :] = jnp.concatenate(
            [weights_ref[:, at], high, low], axis=0
        ).astype(bf16)


def pick_table(points, weights):
    height = weights.shape[0] + 2 * points.shape[0]
    whole = pl.BlockSpec(memory_space=pltpu.VMEM)
    return pl.pallas_call(
        table_body,
        in_specs=[whole, whole],
        out_specs=whole,
        out_shape=jax.ShapeDtypeStruct((points.shape[1] // 256 * height, 256), bf16),
        compiler_params=pltpu.CompilerParams(vmem_limit_bytes=10 * MIB),
        cost_estimate=pl.CostEstimate(flops=3 * 10**9, bytes_accessed=3 * 10**6, transcendentals=0),
        name="pick_table",
    )(points, weights)


def pick_body(want_ref, table_ref, out_ref):
    group_count, height, pair = out_ref.shape
    high_count = table_ref.shape[0] // height
    batch = 8

    def devices(d, carry):
        want = jnp.concatenate([want_ref[2 * d], want_ref[2 * d + 1]], axis=1)
        low = want & 255
        high = want >> 8
        spots = (lax.broadcasted_iota(jnp.int32, (256, 2 * pair), 0) == low).astype(f32).astype(bf16)
        picked = jnp.zeros((height, 2 * pair), f32)
        for h in range(0, high_count, batch):
            found = mm(table_ref[h * height : (h + batch) * height, :], spots)
            for k in range(batch):
                picked = jnp.where(high == h + k, found[k * height : (k + 1) * height], picked)
        picked = picked.astype(bf16)
        out_ref[2 * d] = picked[:, :pair]
        out_ref[2 * d + 1] = picked[:, pair:]
        return carry

    lax.fori_loop(0, group_count // 2, devices, 0)


def pick(want, table, row_count):
    group_count, _, pair = want.shape
    height = table.shape[0] * 256 // row_count
    whole = pl.BlockSpec(memory_space=pltpu.VMEM)
    return pl.pallas_call(
        pick_body,
        in_specs=[whole, whole],
        out_specs=whole,
        out_shape=jax.ShapeDtypeStruct((group_count, height, pair), bf16),
        compiler_params=pltpu.CompilerParams(vmem_limit_bytes=16 * MIB),
        cost_estimate=pl.CostEstimate(flops=6 * 10**9, bytes_accessed=3 * 10**6, transcendentals=0),
        name="pick",
    )(want, table)


def place_body(src_ref, rank_ref, arrived_ref, leaf_ref, table):
    leaf_count, height, leaf_size = leaf_ref.shape
    pair = arrived_ref.shape[1]
    group_count = arrived_ref.shape[0] // height
    lines = table.shape[0] // height
    pieces = 2 * lines // group_count
    batch = 4
    step = 4
    for g in range(0, group_count, 2):
        two = jnp.concatenate(
            [arrived_ref[(g + k) * height : (g + k + 1) * height, :] for k in range(2)], axis=1
        )
        for k in range(pieces):
            at = (g // 2 * pieces + k) * height
            table[at : at + height, :] = two[:, k * 256 : (k + 1) * 256]

    def leaves(c, carry):
        for n in range(step):
            i = c * step + n
            slot = src_ref[i] * pair + rank_ref[i]
            low = slot & 255
            high = slot >> 8
            spots = (
                lax.broadcasted_iota(jnp.int32, (256, leaf_size), 0) == low
            ).astype(f32).astype(bf16)
            placed = jnp.zeros((height, leaf_size), f32)
            for h in range(0, lines, batch):
                found = mm(table[h * height : (h + batch) * height, :], spots)
                for k in range(batch):
                    placed = jnp.where(high == h + k, found[k * height : (k + 1) * height], placed)
            leaf_ref[i] = placed.astype(bf16)
        return carry

    lax.fori_loop(0, leaf_count // step, leaves, 0)


def place(src, rank, arrived):
    group_count, height, pair = arrived.shape
    leaf_count, _, leaf_size = src.shape
    whole = pl.BlockSpec(memory_space=pltpu.VMEM)
    return pl.pallas_call(
        place_body,
        in_specs=[whole] * 3,
        out_specs=whole,
        out_shape=jax.ShapeDtypeStruct((leaf_count, height, leaf_size), bf16),
        scratch_shapes=[pltpu.VMEM((group_count * pair // 256 * height, 256), bf16)],
        compiler_params=pltpu.CompilerParams(vmem_limit_bytes=14 * MIB),
        cost_estimate=pl.CostEstimate(flops=8 * 10**9, bytes_accessed=2 * 10**6, transcendentals=0),
        name="place",
    )(src, rank, arrived.reshape(group_count * height, pair))


def skeleton_body(leaf_ref, basis_ref, transfer_ref, skel_ref, upper_ref):
    leaf_count, cols, _ = skel_ref.shape

    def cluster(c, carry):
        total = jnp.zeros(upper_ref.shape[1:], f32)
        for n in range(KIDS):
            i = c * KIDS + n
            values = leaf_ref[i, :cols]
            basis_high, basis_low = halves(basis_ref[i])
            skel = mm(values, basis_high) + mm(values, basis_low)
            skel_ref[i] = skel.astype(bf16)
            total += mm3(skel, transfer_ref[i])
        upper_ref[c] = total.astype(bf16)
        return carry

    lax.fori_loop(0, leaf_count // KIDS, cluster, 0)


def skeleton(leaves, basis, transfer):
    leaf_count, _, rank_size = basis.shape
    cols = leaves.shape[1] - 16
    whole = pl.BlockSpec(memory_space=pltpu.VMEM)
    return pl.pallas_call(
        skeleton_body,
        in_specs=[whole] * 3,
        out_specs=(whole, whole),
        out_shape=(
            jax.ShapeDtypeStruct((leaf_count, cols, rank_size), bf16),
            jax.ShapeDtypeStruct((leaf_count // KIDS, cols, rank_size), bf16),
        ),
        compiler_params=pltpu.CompilerParams(vmem_limit_bytes=14 * MIB),
        cost_estimate=pl.CostEstimate(flops=10**9, bytes_accessed=7 * 10**6, transcendentals=0),
        name="skeleton",
    )(leaves, basis, transfer)


def near_body(list_ref, low_ref, own_ref, high_ref, after_ref, out_ref, tick_ref, rows, values):
    tick_ref[...] = jnp.zeros_like(tick_ref)
    leaf_count, height, leaf_size = own_ref.shape
    cols = height - 16
    for part, ref in enumerate((low_ref, own_ref, high_ref)):

        def fill(n, carry, part=part, ref=ref):
            values[part * leaf_count + n] = ref[n, :cols]
            tail = ref[n, cols:].astype(f32)
            rows[part * leaf_count + n] = source_rows(tail[:8], tail[8:])
            return carry

        lax.fori_loop(0, leaf_count, fill, 0)

    def leaf(i, carry):
        tail = own_ref[i, cols:].astype(f32)
        target = target_rows(tail[:8], tail[8:])
        total = jnp.zeros((leaf_size, cols), f32)
        for q in range(list_ref.shape[1]):
            j = list_ref[i, q]
            total += mm(matern(mm(target, rows[j])), values[j], NT)
        out_ref[i] = total
        return carry

    def leaves(n, carry):
        for k in range(4):
            leaf(4 * n + k, carry)
        return carry

    lax.fori_loop(0, leaf_count // 4, leaves, 0)


def near_sums(lists, low, own, high, after):
    leaf_count, near = lists.shape
    height, leaf_size = own.shape[1:]
    cols = height - 16
    whole = pl.BlockSpec(memory_space=pltpu.VMEM)
    pairs = leaf_count * near * leaf_size * leaf_size
    return pl.pallas_call(
        near_body,
        in_specs=[pl.BlockSpec(memory_space=pltpu.SMEM), whole, whole, whole]
        + [pl.BlockSpec(memory_space=pl.ANY)],
        out_specs=(whole, whole),
        out_shape=(jax.ShapeDtypeStruct((leaf_count, leaf_size, cols), f32), TICK),
        scratch_shapes=[
            pltpu.VMEM((3 * leaf_count, AUG, leaf_size), bf16),
            pltpu.VMEM((3 * leaf_count, cols, leaf_size), bf16),
        ],
        compiler_params=pltpu.CompilerParams(vmem_limit_bytes=16 * MIB),
        cost_estimate=pl.CostEstimate(
            flops=pairs * 2500, bytes_accessed=6 * 10**6, transcendentals=2 * pairs
        ),
        name="near_sums",
    )(lists, low, own, high, after)


def fill_rows(points_ref, rows_ref):
    step = 8

    def fill(n, carry):
        for k in range(step):
            rows_ref[n * step + k] = source_rows(*f32_halves(points_ref[n * step + k]))
        return carry

    lax.fori_loop(0, rows_ref.shape[0] // step, fill, 0)


FAR_STEP = 4


def far_body(first, after_count, list_ref, target_ref, points_ref, *refs):
    out_ref, tick_ref, rows_ref = refs[after_count:]

    @pl.when(pl.program_id(0) == 0)
    def _():
        fill_rows(points_ref, rows_ref)

    rank_size = rows_ref.shape[2]
    far = list_ref.shape[1]
    batch = 4
    for n in range(FAR_STEP):
        i = first + pl.program_id(0) * FAR_STEP + n
        target = target_rows(*f32_halves(target_ref[i]))
        for q in range(0, far, batch):
            rows = jnp.concatenate([rows_ref[list_ref[i, q + k]] for k in range(batch)], axis=1)
            out_ref[n, :, q * rank_size : (q + batch) * rank_size] = matern(mm(target, rows))
    tick_ref[...] = jnp.zeros_like(tick_ref)


def far_kernels(first, count, lists, targets, points, *after):
    far = lists.shape[1]
    rank_size = points.shape[2]
    pairs = count * far * rank_size * rank_size
    anywhere = pl.BlockSpec(memory_space=pl.ANY)
    return pl.pallas_call(
        functools.partial(far_body, first, len(after)),
        grid_spec=pltpu.PrefetchScalarGridSpec(
            num_scalar_prefetch=1,
            grid=(count // FAR_STEP,),
            in_specs=[
                pl.BlockSpec(targets.shape, lambda i, s: (0, 0, 0)),
                pl.BlockSpec(points.shape, lambda i, s: (0, 0, 0)),
            ]
            + [anywhere] * len(after),
            out_specs=(
                pl.BlockSpec((FAR_STEP, rank_size, far * rank_size), lambda i, s: (i, 0, 0)),
                pl.BlockSpec(TICK.shape, lambda i, s: (0, 0)),
            ),
            scratch_shapes=[pltpu.VMEM((points.shape[0], AUG, rank_size), bf16)],
        ),
        out_shape=(jax.ShapeDtypeStruct((count, rank_size, far * rank_size), bf16), TICK),
        compiler_params=pltpu.CompilerParams(vmem_limit_bytes=52 * MIB),
        cost_estimate=pl.CostEstimate(
            flops=pairs * 20, bytes_accessed=10**6, transcendentals=0
        ),
        name="far_kernels",
    )(lists, targets, points, *after)


STREAM_STEP = 4


def far_sums_body(
    list_ref, target_ref, points_ref, gathered_ref, stored_ref, after_ref, out_ref, tick_ref, even, odd, stream, rows_ref, weights_ref, sems
):
    tick_ref[...] = jnp.zeros_like(tick_ref)
    early = stored_ref.shape[0]
    late = out_ref.shape[0] - early
    rank_size = weights_ref.shape[2]
    far = list_ref.shape[1]
    batch = 4
    blocks = early // STREAM_STEP
    copies = [
        pltpu.make_async_copy(
            stored_ref.at[pl.ds(k * STREAM_STEP, STREAM_STEP)], stream.at[k % 2], sems.at[k % 2]
        )
        for k in range(blocks)
    ]

    def listed(ref, i, q, n):
        return jnp.concatenate([ref[list_ref[i, q + k]] for k in range(n)], axis=1)

    def fill(i, kernel):
        target = target_rows(*f32_halves(target_ref[i]))
        for q in range(0, far, batch):
            kernel[:, q * rank_size : (q + batch) * rank_size] = matern(
                mm(target, listed(rows_ref, i, q, batch))
            )

    def apply(i, kernel):
        out_ref[i] = mm(kernel, listed(weights_ref, i, 0, far), NT)

    weights_copy = pltpu.make_async_copy(gathered_ref, weights_ref, sems.at[2])
    weights_copy.start()
    for copy in copies[:2]:
        copy.start()
    fill_rows(points_ref, rows_ref)
    fill(early, even)
    weights_copy.wait()

    def two(n, carry):
        i = early + 2 * n
        fill(i + 1, odd)
        apply(i, even[...])
        fill(jnp.minimum(i + 2, early + late - 1), even)
        apply(i + 1, odd[...])
        return carry

    lax.fori_loop(0, late // 2, two, 0)
    for k, copy in enumerate(copies):
        copy.wait()
        for n in range(STREAM_STEP):
            apply(k * STREAM_STEP + n, stream[k % 2, n])
        if k + 2 < blocks:
            copies[k + 2].start()


def far_sums(lists, targets, points, weights, stored, after):
    count, far = lists.shape
    cols, rank_size = weights.shape[1:]
    whole = pl.BlockSpec(memory_space=pltpu.VMEM)
    anywhere = pl.BlockSpec(memory_space=pl.ANY)
    pairs = count * far * rank_size * rank_size
    return pl.pallas_call(
        far_sums_body,
        in_specs=[pl.BlockSpec(memory_space=pltpu.SMEM), whole, whole, anywhere, anywhere, anywhere],
        out_specs=(whole, whole),
        out_shape=(jax.ShapeDtypeStruct((count, rank_size, cols), f32), TICK),
        scratch_shapes=[pltpu.VMEM((rank_size, far * rank_size), bf16)] * 2
        + [
            pltpu.VMEM((2, STREAM_STEP, rank_size, far * rank_size), bf16),
            pltpu.VMEM((points.shape[0], AUG, rank_size), bf16),
            pltpu.VMEM(weights.shape, bf16),
            pltpu.SemaphoreType.DMA((3,)),
        ],
        compiler_params=pltpu.CompilerParams(vmem_limit_bytes=58 * MIB),
        cost_estimate=pl.CostEstimate(
            flops=pairs * 2500, bytes_accessed=24 * 10**6, transcendentals=2 * pairs
        ),
        name="far_sums",
    )(lists, targets, points, weights, stored, after)


def upper_body(list_ref, own_ref, chip_ref, across_ref, after_ref, out_ref):
    dims, rank_size = own_ref.shape[1:]
    cols = out_ref.shape[2]
    batch = 4
    half = chip_ref.shape[0]

    def block_of(place):
        here = chip_ref[jnp.minimum(place, half - 1)]
        there = across_ref[jnp.maximum(place - half, 0)]
        return jnp.where(place < half, here, there)

    for c in range(own_ref.shape[0]):
        target = target_rows(*scaled_halves(own_ref[c]))
        total = jnp.zeros((rank_size, cols), f32)
        for q in range(0, list_ref.shape[1], batch):
            blocks = [block_of(list_ref[c, q + k]) for k in range(batch)]
            values = jnp.concatenate([x[:cols] for x in blocks], axis=1)
            points = jnp.concatenate([x[cols:].astype(f32)[:dims] for x in blocks], axis=1)
            kernel = matern(mm(target, source_rows(*scaled_halves(points))))
            total += mm(kernel, values, NT)
        out_ref[c] = total


def upper_sums(lists, own, chip, across, after):
    count, dims, rank_size = own.shape
    cols = chip.shape[1] - 2 * dims
    whole = pl.BlockSpec(memory_space=pltpu.VMEM)
    pairs = count * lists.shape[1] * rank_size * rank_size
    return pl.pallas_call(
        upper_body,
        in_specs=[pl.BlockSpec(memory_space=pltpu.SMEM), whole, whole, whole]
        + [pl.BlockSpec(memory_space=pl.ANY)],
        out_specs=whole,
        out_shape=jax.ShapeDtypeStruct((count, rank_size, cols), f32),
        compiler_params=pltpu.CompilerParams(vmem_limit_bytes=16 * MIB),
        cost_estimate=pl.CostEstimate(
            flops=pairs * 230, bytes_accessed=8 * 10**6, transcendentals=2 * pairs
        ),
        name="upper_sums",
    )(lists, own, chip, across, after)


def final_body(far_ref, upper_ref, transfer_ref, basis_ref, near_ref, out_ref):
    leaf_count, leaf_size, _ = basis_ref.shape
    step = 4

    def leaves(n, carry):
        upper = upper_ref[n * step // KIDS]
        for k in range(step):
            i = n * step + k
            skeleton = far_ref[i] + mm3(transfer_ref[i], upper)
            potential = mm3(basis_ref[i], skeleton) + near_ref[i]
            at = pl.ds(pl.multiple_of(i * leaf_size, leaf_size), leaf_size)
            out_ref[:, at] = jnp.transpose(potential)
        return carry

    lax.fori_loop(0, leaf_count // step, leaves, 0)


def final(far, upper, transfer, basis, near):
    leaf_count, leaf_size, rank_size = basis.shape
    cols = near.shape[2]
    whole = pl.BlockSpec(memory_space=pltpu.VMEM)
    return pl.pallas_call(
        final_body,
        in_specs=[whole] * 5,
        out_specs=whole,
        out_shape=jax.ShapeDtypeStruct((cols, leaf_count * leaf_size), f32),
        compiler_params=pltpu.CompilerParams(vmem_limit_bytes=20 * MIB),
        cost_estimate=pl.CostEstimate(flops=10**9, bytes_accessed=10**7, transcendentals=0),
        name="final",
    )(far, upper, transfer, basis, near)


def shifted(block, axis, move, count):
    return lax.ppermute(block, axis, [(i, move(i)) for i in range(count)])


def upper_places(clusters, count):
    owner = clusters // count
    group = owner % 16
    bulk = owner // 16
    mine = lax.axis_index("bulk")
    core = (bulk ^ mine) & 1
    hops = (bulk // 2 - mine // 2) & 3
    turn = hops
    return (((core * 4 + turn) * 16) + group) * count + clusters % count


def local(
    points,
    weights,
    leaf_order,
    basis,
    transfer,
    skel_leaf,
    skel_upper,
    near_list,
    leaf_interaction_list,
    far_upper,
):
    row_count = leaf_order.shape[0]
    group_count = lax.axis_size("group")
    bulk_count = lax.axis_size("bulk")
    device_count = group_count * bulk_count
    leaf_count = basis.shape[0]

    want, src, rank, tick = index_lists(leaf_order, group_count, basis.shape[1])
    scaled = skel_leaf.astype(f32) * POINT_SCALE + tick[0]
    subtree_points = lax.all_gather(scaled, "group", axis=0, tiled=True)
    wanted = lax.all_to_all(want, "group", split_axis=0, concat_axis=0, tiled=True)
    picked = pick(wanted, pick_table(points, weights), row_count)
    arrived = lax.all_to_all(picked, "group", split_axis=0, concat_axis=0, tiled=True)

    far_local = leaf_interaction_list - lax.axis_index("bulk") * (group_count * leaf_count)

    own = place(src, rank, arrived)
    skel_wb, upper_wb = skeleton(own, basis, transfer)
    sub_w = lax.all_gather(skel_wb, "group", axis=0, tiled=True)
    forward = [(i, i + 1) for i in range(device_count - 1)]
    backward = [(i + 1, i) for i in range(device_count - 1)]
    low = lax.ppermute(own, ("bulk", "group"), forward)
    high = lax.ppermute(own, ("bulk", "group"), backward)

    def joined(tick, *blocks):
        return jnp.concatenate(blocks, axis=0) + tick[0].astype(bf16)

    mine = jnp.concatenate([upper_wb, skel_upper, jnp.zeros(skel_upper.shape, bf16)], axis=1)
    copies = jnp.tile(mine, (group_count, 1, 1))
    block = lax.all_to_all(copies, "group", split_axis=0, concat_axis=0, tiled=True)
    part = leaf_count // 2
    kernels, tick = far_kernels(0, part, far_local, scaled, subtree_points, copies)
    block = joined(tick, block)
    ring = [shifted(block, "bulk", lambda i, hops=hops: (i - 2 * hops) % bulk_count, bulk_count) for hops in (1, 2, 3)]
    device = lax.axis_index(("bulk", "group"))
    near, tick = near_sums(near_list - (device - 1) * leaf_count, low, own, high, block)
    chip = joined(tick, block, *ring)
    other = shifted(chip, "bulk", lambda i: i ^ 1, bulk_count)
    far, tick = far_sums(far_local, scaled, subtree_points, sub_w, kernels, chip)
    upper = upper_sums(upper_places(far_upper, skel_upper.shape[0]), skel_upper, chip, other, tick)
    return final(far, upper, transfer, basis, near)


def solution(mesh):
    placed = (
        P(None, ("bulk", "group")),
        P(None, ("bulk", "group")),
        P(("bulk", "group")),
        P(("bulk", "group"), None, None),
        P(("bulk", "group"), None, None),
        P(("bulk", "group"), None, None),
        P(("bulk", "group"), None, None),
        P(("bulk", "group"), None),
        P(("bulk", "group"), None),
        P(("bulk", "group"), None),
    )
    return jax.shard_map(
        local, mesh=mesh, in_specs=placed, out_specs=P(None, ("bulk", "group")), check_vma=False
    )
```
